32 devices in a mesh: dp: 4 (over z), ctx: 8 (over y, x, core).
Axes of the slice: x: 2, y: 2, z: 4, core: 2. Of those that a mesh axis runs over, the one named last changes fastest.
Arguments:
- q_proj: bfloat16 [4, 1024, 3072], P('dp', 'ctx'), may hold values from -6 to 6
- k_proj: bfloat16 [4, 1024, 512], P('dp', 'ctx'), may hold values from -6 to 6
- v_proj: bfloat16 [4, 1024, 512], P('dp', 'ctx'), may hold values from -6 to 6
- out_grad: bfloat16 [4, 1024, 3072], P('dp', 'ctx'), may hold values from -6 to 6
- q_gain: float32 [128], replicated, may hold values from 0.1 to 1.9
- k_gain: float32 [128], replicated, may hold values from 0.1 to 1.9
- pos_ids: int32 [4, 3, 1024], P('dp', None, 'ctx'), may hold values from 0 to 63
- stretch_lengths: int32 [4, 32], P('dp'), may hold values from 1 to 64, 1024 in all within a row
- stretch_windows: int32 [4, 32], P('dp'), may hold values from 0 to 1
- clip_ids: int32 [4, 32], P('dp'), may hold values from 0 to 7, never falling along the last dimension, each value on 1 to 8 neighbouring positions
- dispatch_plan: int32 [4, 8], P('dp'), may hold values from 0 to 7, as said below
Outputs:
- q_grad: bfloat16 [4, 1024, 3072], P('dp', 'ctx')
- k_grad: bfloat16 [4, 1024, 512], P('dp', 'ctx')
- v_grad: bfloat16 [4, 1024, 512], P('dp', 'ctx')
- q_gain_grad: float32 [128], replicated
- k_gain_grad: float32 [128], replicated
The draws below stay inside these ranges and needn't reach their ends.
Inputs may be any that keep to these rules, and one draw needn't show every extreme that they name: In each batch every block number appears once, and a slot holds a block of its own aligned pair of devices: dispatch_plan[s] // 2 == s // 2. `stretch_lengths`: in each batch the lengths sum to 1024, and the longest is exactly 64. `clip_ids`: never falls along a batch's stretches; each clip has 1 to 8 stretches, one exactly 8.
All inputs are finite; a program needn't handle non-finite values.
Results may differ from the reference program's by a relative error of at most 0.013.
Values may be sent and summed in bfloat16 or wider, within the bound.
A program may use at most 64 MiB of HBM per device.

```python
import math
import jax
import jax.numpy as jnp
import numpy as np
from jax import lax

HD = 128
HEADS = 24
KVG = 4
BLOCK = 128
BLK_DEV = 1
CLIP_MOST = 8
POS_RANGE = 64
TOK_DEV = 128
STRETCH_MOST = 64
SEQ = 1024
NCHUNK = 32
CLIPS = 8
N_DP = 4
N_CTX = 8


def draw_dispatch_plan(key, part):
    group_size = 2 * BLK_DEV
    pair_count = N_CTX // 2
    random_scores = jax.random.randint(key, (N_DP, pair_count, group_size), 0, 2 ** 20)
    distinct = random_scores * group_size + jnp.arange(group_size, dtype=jnp.int32)
    ranking = jnp.argsort(distinct, axis=-1, stable=True).astype(jnp.int32)
    pair_start = (jnp.arange(pair_count, dtype=jnp.int32) * group_size)[None, :, None]
    return (ranking + pair_start).reshape(N_DP, pair_count * group_size)


def plant(entries, key, smallest, top_value):
    place = [jax.random.randint(jax.random.fold_in(key, axis), (), 0, length) for axis, length in enumerate(entries.shape)]
    widest = entries.shape.index(max(entries.shape))
    beside = place[:widest] + [(place[widest] + 1) % entries.shape[widest]] + place[widest + 1:]
    return entries.at[tuple(place)].set(smallest).at[tuple(beside)].set(top_value)


def level_of(stream_key, shape, split, low, high):
    factor_of = 1.0
    for axis_at, blocks in split:
        heights = jax.random.uniform(jax.random.fold_in(jax.random.fold_in(stream_key, 6), axis_at), (blocks,), jnp.float32, low / len(split), high / len(split))
        factor_of = factor_of * jnp.repeat(jnp.exp(heights), shape[axis_at] // blocks).reshape((-1,) + (1,) * (len(shape) - 1 - axis_at))
    return factor_of


def split_up(number_of, total, reach, lean):
    portions = [(1 << 20) // math.isqrt(standing ** lean) + 1 for standing in range(2, number_of + 1)]
    rest, holding = total - reach - (number_of - 1), [1] * (number_of - 1)
    while rest > 0:
        movable = [i for i in range(number_of - 1) if holding[i] < reach]
        mass, remaining = sum([portions[i] for i in movable]), rest
        for i in movable:
            extra = min(reach - holding[i], max(1, remaining * portions[i] // mass), rest)
            holding[i] = holding[i] + extra
            rest = rest - extra
    return np.array([reach] + holding)


def ragged_sizes(own_key, number_of, total, limit, lean):
    if number_of == 2:
        one = jax.random.randint(own_key, (), max(1, total - limit), min(limit, total - 1) + 1)
        return jnp.stack([one, total - one])
    tallies = jnp.asarray(split_up(number_of, total, limit, lean), jnp.int32)
    couples = (number_of - 1) // 2
    donor, sink = tallies[1:1 + 2 * couples:2], tallies[2:2 + 2 * couples:2]
    room = jnp.minimum(donor - 1, limit - sink)
    passed = jax.random.randint(jax.random.fold_in(own_key, 1), (couples,), 0, 1 << 20) % (room + 1)
    tallies = tallies.at[1:1 + 2 * couples:2].set(donor - passed).at[2:2 + 2 * couples:2].set(sink + passed)
    return tallies[jax.random.permutation(jax.random.fold_in(own_key, 2), number_of)]


def scatter_about(stream_key, shape, width, most, shards=(), kind=jnp.bfloat16):
    drawn = width * jax.random.normal(stream_key, shape, jnp.float32)
    if shards:
        drawn = drawn * level_of(stream_key, shape, shards, -0.22, 0.18)
    return jnp.clip(drawn, -most, most).astype(kind)


def setup_inputs(seed: int = 0) -> dict:
    key_list = jax.random.split(jax.random.key(seed), 12)
    return {
        "q_proj": scatter_about(key_list[0], (N_DP, SEQ, HEADS * HD), 1.0, 6.0, ((0, 4), (1, 8))),
        "k_proj": scatter_about(key_list[1], (N_DP, SEQ, KVG * HD), 1.0, 6.0, ((0, 4), (1, 8))),
        "v_proj": scatter_about(key_list[2], (N_DP, SEQ, KVG * HD), 1.0, 6.0, ((0, 4), (1, 8))),
        "out_grad": scatter_about(key_list[3], (N_DP, SEQ, HEADS * HD), 1.0, 6.0, ((0, 4), (1, 8))),
        "q_gain": jnp.clip(1.0 + 0.18 * jax.random.normal(key_list[4], (HD,), jnp.float32), 0.1, 1.9),
        "k_gain": jnp.clip(1.0 + 0.18 * jax.random.normal(key_list[5], (HD,), jnp.float32), 0.1, 1.9),
        "pos_ids": plant(jax.random.randint(key_list[6], (N_DP, 3, SEQ), 0, POS_RANGE), jax.random.fold_in(key_list[6], 1), 0, POS_RANGE - 1).astype(jnp.int32),
        "stretch_lengths": jax.vmap(lambda own: ragged_sizes(own, NCHUNK, SEQ, STRETCH_MOST, 0))(jax.random.split(key_list[7], N_DP)).reshape((N_DP, NCHUNK)).astype(jnp.int32),
        "stretch_windows": plant(jax.random.randint(key_list[8], (N_DP, NCHUNK), 0, 2), jax.random.fold_in(key_list[8], 1), 0, 1).astype(jnp.int32),
        "clip_ids": jax.vmap(lambda own: jnp.searchsorted(jnp.cumsum(ragged_sizes(own, CLIPS, NCHUNK, CLIP_MOST, 0)), jnp.arange(NCHUNK), side="right"))(jax.random.split(key_list[9], N_DP)).reshape((N_DP, NCHUNK)).astype(jnp.int32),
        "dispatch_plan": draw_dispatch_plan(jax.random.fold_in(key_list[11], 71), 0),
    }


norm_eps = 1e-06
rope_base = 10000.0

def rope_tables(position_ids, head_dim):
    half_dim = head_dim // 2
    pair_index = jnp.arange(half_dim, dtype=jnp.int32)
    frequency = rope_base ** (-2.0 * pair_index.astype(jnp.float32) / head_dim)
    section = (pair_index >= head_dim // 8).astype(jnp.int32) + (pair_index >= head_dim // 8 + 3 * head_dim // 16).astype(jnp.int32)
    chosen = jnp.where(section[None, :] == 0, position_ids[0][:, None], jnp.where(section[None, :] == 1, position_ids[1][:, None], position_ids[2][:, None]))
    angles = chosen.astype(jnp.float32) * frequency[None, :]
    return (jnp.cos(angles), jnp.sin(angles))

def rotate(tensor, cosine_table, sine_table):
    half_dim = tensor.shape[-1] // 2
    front_half = tensor[..., :half_dim]
    back_half = tensor[..., half_dim:]
    cosine = cosine_table[:, None, :]
    sine = sine_table[:, None, :]
    return jnp.concatenate([front_half * cosine - back_half * sine, back_half * cosine + front_half * sine], axis=-1)

def unrotate(tensor, cosine_table, sine_table):
    half_dim = tensor.shape[-1] // 2
    front_half = tensor[..., :half_dim]
    back_half = tensor[..., half_dim:]
    cosine = cosine_table[:, None, :]
    sine = sine_table[:, None, :]
    return jnp.concatenate([front_half * cosine + back_half * sine, back_half * cosine - front_half * sine], axis=-1)

def normalize(rows_in, gain_row, cosine_table, sine_table):
    row_count = rows_in.shape[0]
    head_dim = gain_row.shape[0]
    widened = rows_in.astype(jnp.float32).reshape(row_count, -1, head_dim)
    inv_rms = lax.rsqrt(lax.optimization_barrier(jnp.mean(widened * widened, axis=-1, keepdims=True)) + norm_eps)
    unit_rows = widened * inv_rms
    rotated = rotate(unit_rows * gain_row, cosine_table, sine_table).astype(jnp.bfloat16)
    return (lax.optimization_barrier(rotated), unit_rows, inv_rms)

def normalize_back(rot_grad, unit_rows, inv_rms, gain_row, cosine_table, sine_table):
    grad_scaled = unrotate(rot_grad, cosine_table, sine_table)
    gain_term = lax.optimization_barrier(jnp.sum(grad_scaled * unit_rows, axis=(0, 1)))
    weighted = grad_scaled * gain_row
    grad_in = inv_rms * (weighted - unit_rows * lax.optimization_barrier(jnp.mean(weighted * unit_rows, axis=-1, keepdims=True)))
    return (grad_in.reshape(rot_grad.shape[0], -1).astype(jnp.bfloat16), gain_term)

def stretch_info(positions, lengths, windows, clip_table):
    stretch_ends = jnp.cumsum(lengths).astype(jnp.int32)
    stretch_of = lax.optimization_barrier(jnp.sum((stretch_ends[None, :] <= positions[:, None]).astype(jnp.int32), axis=1))
    matches = jnp.arange(lengths.shape[0], dtype=jnp.int32)[None, :] == stretch_of[:, None]
    clip_of = lax.optimization_barrier(jnp.sum(jnp.where(matches, clip_table[None, :], 0), axis=1))
    lowest = stretch_of - lax.optimization_barrier(jnp.sum(jnp.where(matches, windows[None, :], 0), axis=1))
    return (stretch_of, clip_of, lowest)

def low_round(tensor):
    return lax.optimization_barrier(tensor.astype(jnp.bfloat16)).astype(jnp.float32)

def one_batch(q_part, k_part, v_part, cot_part, ids_part, lengths, windows, clip_table, slot_plan, q_gain, k_gain):
    seq_len = q_part.shape[0]
    head_dim = q_gain.shape[0]
    head_count = q_part.shape[1] // head_dim
    groups = k_part.shape[1] // head_dim
    per_group = head_count // groups
    block_count = seq_len // BLOCK
    ranking = jnp.argsort(slot_plan).astype(jnp.int32)

    def to_natural(array):
        shaped = array.reshape((block_count, BLOCK) + array.shape[1:])
        return jnp.take(shaped, ranking, axis=0).reshape(array.shape)

    def to_slots(array):
        shaped = array.reshape((block_count, BLOCK) + array.shape[1:])
        return jnp.take(shaped, slot_plan, axis=0).reshape(array.shape)
    ids_nat = to_natural(ids_part.T).T
    cosine_table, sine_table = rope_tables(ids_nat, head_dim)
    q_rot, q_unit, q_inv = normalize(to_natural(q_part), q_gain, cosine_table, sine_table)
    k_rot, k_unit, k_inv = normalize(to_natural(k_part), k_gain, cosine_table, sine_table)
    v_nat = to_natural(v_part).astype(jnp.float32).reshape(seq_len, groups, head_dim)
    cot_nat = to_natural(cot_part).astype(jnp.float32).reshape(seq_len, groups, per_group, head_dim)
    positions = jnp.arange(seq_len, dtype=jnp.int32)
    stretch_of, clip_of, lowest = stretch_info(positions, lengths, windows, clip_table)
    lead = 2 * TOK_DEV
    tail = TOK_DEV
    span = 3 * TOK_DEV + BLOCK
    pad_rows = ((lead, tail), (0, 0), (0, 0))
    key_pad = jnp.pad(k_rot.astype(jnp.float32), pad_rows)
    value_pad = jnp.pad(v_nat, pad_rows)
    stretch_pad = jnp.pad(stretch_of, (lead, tail))
    clip_pad = jnp.pad(clip_of, (lead, tail))
    range_pad = jnp.pad(jnp.ones((seq_len,), jnp.int32), (lead, tail))
    query_all = q_rot.astype(jnp.float32).reshape(seq_len, groups, per_group, head_dim)
    inv_sqrt = head_dim ** (-0.5)

    def one_block(totals, block_index):
        key_acc, value_acc = totals
        row_start = (block_index * BLOCK).astype(jnp.int32)
        query_block = lax.dynamic_slice_in_dim(query_all, row_start, BLOCK, 0)
        cot_block = lax.dynamic_slice_in_dim(cot_nat, row_start, BLOCK, 0)
        key_block = lax.dynamic_slice_in_dim(key_pad, row_start, span, 0)
        value_block = lax.dynamic_slice_in_dim(value_pad, row_start, span, 0)
        stretch_q = lax.dynamic_slice_in_dim(stretch_of, row_start, BLOCK, 0)
        clip_q = lax.dynamic_slice_in_dim(clip_of, row_start, BLOCK, 0)
        lowest_q = lax.dynamic_slice_in_dim(lowest, row_start, BLOCK, 0)
        stretch_k = lax.dynamic_slice_in_dim(stretch_pad, row_start, span, 0)
        clip_k = lax.dynamic_slice_in_dim(clip_pad, row_start, span, 0)
        range_k = lax.dynamic_slice_in_dim(range_pad, row_start, span, 0)
        allowed = (range_k[None, :] > 0) & (clip_q[:, None] == clip_k[None, :]) & (stretch_k[None, :] >= lowest_q[:, None]) & (stretch_k[None, :] <= stretch_q[:, None])
        scores = jnp.einsum('qgjd,kgd->gjqk', query_block, key_block) * inv_sqrt
        raw_probs = jnp.where(allowed[None, None], jnp.exp(scores), 0.0)
        total = lax.optimization_barrier(jnp.sum(raw_probs, axis=-1))
        weighted = jnp.einsum('gjqk,kgd->gjqd', low_round(raw_probs), value_block)
        attended = low_round(weighted / total[..., None])
        log_total = jnp.log(total)
        row_delta = jnp.einsum('gjqd,qgjd->gjq', attended, cot_block)
        probs = jnp.where(allowed[None, None], jnp.exp(scores - log_total[..., None]), 0.0)
        prob_grad = jnp.einsum('qgjd,kgd->gjqk', cot_block, value_block)
        score_grad = low_round(probs * (prob_grad - row_delta[..., None]))
        query_grad = jnp.einsum('gjqk,kgd->qgjd', score_grad, key_block) * inv_sqrt
        key_grad = jnp.einsum('gjqk,qgjd->kgd', score_grad, query_block) * inv_sqrt
        value_grad = jnp.einsum('gjqk,qgjd->kgd', low_round(probs), cot_block)
        key_now = lax.dynamic_slice_in_dim(key_acc, row_start, span, 0)
        value_now = lax.dynamic_slice_in_dim(value_acc, row_start, span, 0)
        key_acc = lax.dynamic_update_slice_in_dim(key_acc, key_now + key_grad, row_start, 0)
        value_acc = lax.dynamic_update_slice_in_dim(value_acc, value_now + value_grad, row_start, 0)
        return ((key_acc, value_acc), query_grad)
    empty = jnp.zeros((seq_len + lead + tail, groups, head_dim), jnp.float32)
    (key_acc, value_acc), query_blocks = lax.scan(one_block, (empty, empty), jnp.arange(block_count, dtype=jnp.int32))
    qrot_grad = query_blocks.reshape(seq_len, head_count, head_dim)
    krot_grad = key_acc[lead:lead + seq_len]
    q_grad, q_term = normalize_back(qrot_grad, q_unit, q_inv, q_gain, cosine_table, sine_table)
    k_grad, k_term = normalize_back(krot_grad, k_unit, k_inv, k_gain, cosine_table, sine_table)
    v_grad = value_acc[lead:lead + seq_len].reshape(seq_len, groups * head_dim).astype(jnp.bfloat16)
    return (to_slots(q_grad), to_slots(k_grad), to_slots(v_grad), q_term, k_term)

def reference(q_proj, k_proj, v_proj, out_grad, q_gain, k_gain, pos_ids, stretch_lengths, stretch_windows, clip_ids, dispatch_plan):

    def per_batch(items):
        return one_batch(items[0], items[1], items[2], items[3], items[4], items[5], items[6], items[7], items[8], q_gain, k_gain)
    q_grad, k_grad, v_grad, q_terms, k_terms = lax.map(per_batch, (q_proj, k_proj, v_proj, out_grad, pos_ids, stretch_lengths, stretch_windows, clip_ids, dispatch_plan))
    head_count = q_proj.shape[2] // q_gain.shape[0]
    groups = k_proj.shape[2] // k_gain.shape[0]
    token_count = q_proj.shape[0] * q_proj.shape[1]
    q_gain_grad = lax.optimization_barrier(jnp.sum(q_terms, axis=0)) / math.sqrt(token_count * head_count)
    k_gain_grad = lax.optimization_barrier(jnp.sum(k_terms, axis=0)) / math.sqrt(token_count * groups)
    return (q_grad, k_grad, v_grad, q_gain_grad, k_gain_grad)
```

```python
import functools
import math

import jax
import jax.numpy as jnp
from jax import lax
from jax.experimental import pallas as pl
from jax.experimental.pallas import tpu as pltpu
from jax.sharding import PartitionSpec as P

MESH = pl.DeviceIdType.MESH
F32 = jnp.float32
BF16 = jnp.bfloat16
BLOCK = 128
HALF = BLOCK // 2
SPAN = 2 * BLOCK + HALF
norm_eps = 1e-06
VMEM_LIMIT = 40 * 1024 * 1024
rope_base = 10000.0

NT = (((1,), (1,)), ((), ()))
TN = (((0,), (0,)), ((), ()))


def sin_cos(angle):
    turns = jnp.floor(angle * (2.0 / math.pi) + 0.5)
    rest = angle - turns * 1.5703125
    rest = rest - turns * 4.837512969970703125e-4
    rest = rest - turns * 7.549789948768648e-8
    square = rest * rest
    sine = rest + rest * square * (
        -1.6666654611e-1 + square * (8.3321608736e-3 + square * -1.9515295891e-4)
    )
    cosine = (
        1.0
        - 0.5 * square
        + square
        * square
        * (4.166664568298827e-2 + square * (-1.388731625493765e-3 + square * 2.443315711809948e-5))
    )
    quarter = turns.astype(jnp.int32)
    odd = (quarter & 1) == 1
    sine_out = jnp.where(odd, cosine, sine)
    cosine_out = jnp.where(odd, sine, cosine)
    sine_out = jnp.where((quarter & 2) == 2, -sine_out, sine_out)
    cosine_out = jnp.where(((quarter + 1) & 2) == 2, -cosine_out, cosine_out)
    return sine_out, cosine_out


def roll_half(x):
    return pltpu.roll(x, HALF, 1)


def rope_tables(ids):
    rows = lax.broadcasted_iota(jnp.int32, (BLOCK, BLOCK), 0)
    lanes = lax.broadcasted_iota(jnp.int32, (BLOCK, BLOCK), 1)
    columns = [
        jnp.sum(jnp.where(rows == lanes, ids[t].astype(F32), 0.0), axis=1, keepdims=True)
        for t in range(3)
    ]
    pair = lanes % HALF
    chosen = jnp.where(pair < 16, columns[0], jnp.where(pair < 40, columns[1], columns[2]))
    pair_row = lax.broadcasted_iota(jnp.int32, (1, BLOCK), 1) % HALF
    frequency = jnp.exp(pair_row.astype(F32) * (-math.log(rope_base) / HALF))
    sine, cosine = sin_cos(chosen * frequency)
    return cosine, jnp.where(lanes < HALF, -sine, sine)


def key_ranges(lengths, windows, clips, start):
    count = lengths.shape[1]
    rows = lax.broadcasted_iota(jnp.int32, (count, count), 0)
    lanes = lax.broadcasted_iota(jnp.int32, (count, count), 1)

    def column(where_, values):
        return jnp.sum(jnp.where(where_, values.astype(F32), 0.0), axis=1, keepdims=True)

    ends = column(lanes <= rows, lengths)
    starts = column(lanes < rows, lengths)
    before = column(lanes == rows - 1, lengths)
    window = column(lanes == rows, windows)
    clip = column(lanes == rows, clips + 1)
    clip_before = column(lanes == rows - 1, clips + 1)
    low = starts - jnp.where(clip == clip_before, window * before, 0.0)
    spots = (start + lax.broadcasted_iota(jnp.int32, (count, BLOCK), 1)).astype(F32)
    inside = (starts <= spots) & (spots < ends)
    low_row = jnp.sum(jnp.where(inside, low, 0.0), axis=0, keepdims=True)
    high_row = jnp.sum(jnp.where(inside, ends, 0.0), axis=0, keepdims=True)
    return low_row, high_row


def kernel(
    n,
    n_dp,
    groups,
    per_group,
    plan_hbm,
    k_hbm,
    v_hbm,
    qg_hbm,
    kg_hbm,
    ids_hbm,
    len_hbm,
    win_hbm,
    clip_hbm,
    q_hbm,
    do_hbm,
    qgrad_ref,
    kgrad_ref,
    vgrad_ref,
    qgain_ref,
    kgain_ref,
    plan_ref,
    k_ref,
    v_ref,
    qg_ref,
    kg_ref,
    ids_ref,
    len_ref,
    win_ref,
    clip_ref,
    q_vm,
    do_vm,
    qrot,
    qinv,
    dq,
    own,
    other,
    to_prev,
    to_next,
    from_prev,
    from_next,
    parts,
    back_prev,
    back_next,
    back,
    met,
    home_prev,
    home_next,
    back_pair,
    home_pair,
    term_ctx,
    term_dp,
    load_sem,
    pair_s,
    pair_r,
    np_s,
    np_r,
    nn_s,
    nn_r,
    bp_s,
    bp_r,
    bn_s,
    bn_r,
    hp_s,
    hp_r,
    fp_s,
    fp_r,
    fn_s,
    fn_r,
    mt_s,
    mt_r,
    tc_s,
    tc_r,
    td_s,
    td_r,
):
    me = lax.axis_index("ctx")
    dp = lax.axis_index("dp")
    partner = me + 1 - 2 * lax.rem(me, 2)
    has_prev = me >= 2
    has_next = me < n - 2
    inv_sqrt = BLOCK ** (-0.5)

    sources = (
        ids_hbm, kg_hbm, k_hbm, v_hbm, plan_hbm, qg_hbm, len_hbm, win_hbm, clip_hbm, q_hbm, do_hbm
    )
    targets = (
        ids_ref, kg_ref, k_ref, v_ref, plan_ref, qg_ref, len_ref, win_ref, clip_ref, q_vm, do_vm
    )
    loads = [
        pltpu.make_async_copy(source, target, load_sem.at[i])
        for i, (source, target) in enumerate(zip(sources, targets))
    ]
    for load in loads:
        load.start()

    barrier = pltpu.get_barrier_semaphore()

    def greet_ctx(step, carry):
        peer = lax.rem(me + step, n)
        pl.semaphore_signal(barrier, inc=1, device_id=(dp, peer), device_id_type=MESH)
        return carry

    def greet_dp(step, carry):
        peer = lax.rem(dp + step, n_dp)
        pl.semaphore_signal(barrier, inc=1, device_id=(peer, me), device_id_type=MESH)
        return carry

    for g in range(groups):
        edge = lax.rem(me, 2) != g // (groups // 2)

        @pl.when(jnp.logical_or(edge, jnp.logical_not(has_prev)))
        def _():
            home_prev[g] = jnp.zeros_like(home_prev[g])

        @pl.when(jnp.logical_or(edge, jnp.logical_not(has_next)))
        def _():
            home_next[g] = jnp.zeros_like(home_next[g])

    @pl.when(jnp.logical_not(has_prev))
    def _():
        from_prev[...] = jnp.zeros_like(from_prev)

    @pl.when(jnp.logical_not(has_next))
    def _():
        from_next[...] = jnp.zeros_like(from_next)

    lax.fori_loop(1, n, greet_ctx, 0)
    lax.fori_loop(1, n_dp, greet_dp, 0)

    def remote(source, target, send, receive, peer):
        return pltpu.make_async_remote_copy(
            src_ref=source,
            dst_ref=target,
            send_sem=send,
            recv_sem=receive,
            device_id=peer,
            device_id_type=MESH,
        )

    for load in loads[:9]:
        load.wait()
    block = plan_ref[0, me]
    is_odd = lax.rem(block, 2) == 1

    cosine, sine = rope_tables(ids_ref)
    k_gain = kg_ref[...]
    q_gain = qg_ref[...]
    kc, ks = cosine * k_gain, sine * roll_half(k_gain)
    k_inv = []
    for g in range(groups):
        x = k_ref[0, :, g * BLOCK : (g + 1) * BLOCK].astype(F32)
        inv = lax.rsqrt(jnp.mean(x * x, axis=1, keepdims=True) + norm_eps)
        own[g, :, :BLOCK] = (inv * (x * kc + roll_half(x) * ks)).astype(BF16)
        own[g, :, BLOCK:] = v_ref[0, :, g * BLOCK : (g + 1) * BLOCK]

    pl.semaphore_wait(barrier, n - 1 + n_dp - 1)

    pair = [
        remote(own.at[g], other.at[g], pair_s.at[g], pair_r.at[g], (dp, partner))
        for g in range(groups)
    ]
    order = [g for i in range(groups // 2) for g in (i, i + groups // 2)]
    for g in order:
        pair[g].start()

    low_row, high_row = key_ranges(len_ref[...], win_ref[...], clip_ref[...], block * BLOCK)
    spots = ((block - 1) * BLOCK + lax.broadcasted_iota(jnp.int32, (SPAN, BLOCK), 0)).astype(F32)
    bias = jnp.where((spots >= low_row) & (spots < high_row), 0.0, -1e30)
    bias = jnp.concatenate([bias, bias], axis=1)

    qc, qs = cosine * q_gain, sine * roll_half(q_gain)
    loads[9].wait()

    def rotate_group(g):
        for j in range(per_group):
            h = g * per_group + j
            x = q_vm[0, :, h * BLOCK : (h + 1) * BLOCK].astype(F32)
            inv = lax.rsqrt(jnp.mean(x * x, axis=1, keepdims=True) + norm_eps)
            qinv[h] = inv
            qrot[g, j * BLOCK : (j + 1) * BLOCK, :] = (inv * (x * qc + roll_half(x) * qs)).astype(
                BF16
            )

    send_prev = [
        remote(to_prev.at[g], from_next.at[g], np_s.at[g], nn_r.at[g], (dp, me - 2))
        for g in range(groups)
    ]
    send_next = [
        remote(to_next.at[g], from_prev.at[g], nn_s.at[g], np_r.at[g], (dp, me + 2))
        for g in range(groups)
    ]
    pass_prev = [
        remote(from_prev.at[g], from_prev.at[g], fp_s.at[g], fp_r.at[g], (dp, partner))
        for g in range(groups)
    ]
    pass_next = [
        remote(from_next.at[g], from_next.at[g], fn_s.at[g], fn_r.at[g], (dp, partner))
        for g in range(groups)
    ]
    share = groups // 2
    core = lax.rem(me, 2)

    def mine(g):
        return core == g // share

    def both(one, two):
        return jnp.logical_and(one, two)

    for g in order:
        pair[g].wait_recv()

        @pl.when(mine(g))
        def _():
            own_g, other_g = own[g], other[g]
            to_next[g] = lax.select(is_odd, own_g, other_g)
            to_prev[g] = lax.select(is_odd, other_g[:HALF], own_g[:HALF])

        @pl.when(both(has_next, mine(g)))
        def _():
            send_next[g].start()

        @pl.when(both(has_prev, mine(g)))
        def _():
            send_prev[g].start()

    for g in range(groups):
        rotate_group(g)
    loads[10].wait()

    return_prev = [
        remote(back_prev.at[g], home_next.at[g], bp_s.at[g], bn_r.at[g], (dp, me - 2))
        for g in range(groups)
    ]
    return_next = [
        remote(back_next.at[g], home_prev.at[g], bn_s.at[g], bp_r.at[g], (dp, me + 2))
        for g in range(groups)
    ]
    scale = inv_sqrt * math.log2(math.e)
    def pass_on(g):
        @pl.when(both(has_prev, mine(g)))
        def _():
            send_next[g].wait_recv()
            pass_prev[g].start()

        @pl.when(both(has_next, mine(g)))
        def _():
            send_prev[g].wait_recv()
            pass_next[g].start()

    def send_back(g):
        @pl.when(mine(g))
        def _():
            meet[g].wait_recv()
            back_prev[g] = back[g, :BLOCK] + met[g, :BLOCK]
            back_next[g] = back[g, BLOCK:] + met[g, BLOCK:]

        @pl.when(both(has_prev, mine(g)))
        def _():
            return_prev[g].start()

        @pl.when(both(has_next, mine(g)))
        def _():
            return_next[g].start()

    meet = [
        remote(back.at[g], met.at[g], mt_s.at[g], mt_r.at[g], (dp, partner))
        for g in range(groups)
    ]
    for place, g in enumerate(order):
        if place % 2 == 0:
            pass_on(order[place])
            pass_on(order[place + 1])

        @pl.when(both(has_prev, jnp.logical_not(mine(g))))
        def _():
            pass_prev[g].wait_recv()

        @pl.when(both(has_next, jnp.logical_not(mine(g))))
        def _():
            pass_next[g].wait_recv()

        other_g = other[g]
        keys = jnp.concatenate(
            [
                lax.select(is_odd, other_g, from_prev[g]),
                own[g],
                lax.select(is_odd, from_next[g], other_g[:HALF]),
            ],
            axis=0,
        )
        key, value = keys[:, :BLOCK], keys[:, BLOCK:]
        prob_list, grad_list = [], []
        for j in range(per_group // 2):
            first = g * per_group + 2 * j
            query = qrot[g, 2 * j * BLOCK : (2 * j + 2) * BLOCK, :]
            cot = jnp.concatenate(
                [
                    do_vm[0, :, first * BLOCK : (first + 1) * BLOCK],
                    do_vm[0, :, (first + 1) * BLOCK : (first + 2) * BLOCK],
                ],
                axis=0,
            )
            scores = lax.dot_general(key, query, NT, preferred_element_type=F32)
            prob_grad = lax.dot_general(value, cot, NT, preferred_element_type=F32)
            weights = jnp.exp2(scores * scale + bias)
            inverse = 1.0 / jnp.sum(weights, axis=0, keepdims=True)
            delta = jnp.sum(weights * prob_grad, axis=0, keepdims=True) * inverse
            probs = weights * inverse
            prob_list.append(probs.astype(BF16))
            grad_list.append((probs * (prob_grad - delta)).astype(BF16))
        probs_low = jnp.concatenate(prob_list, axis=1)
        score_grad = jnp.concatenate(grad_list, axis=1)
        cots = jnp.concatenate(
            [
                do_vm[0, :, h * BLOCK : (h + 1) * BLOCK]
                for h in range(g * per_group, (g + 1) * per_group)
            ],
            axis=0,
        )
        parts[g, :, :BLOCK] = jnp.dot(score_grad, qrot[g], preferred_element_type=F32) * inv_sqrt
        parts[g, :, BLOCK:] = jnp.dot(probs_low, cots, preferred_element_type=F32)
        back[g, :BLOCK] = lax.select(
            is_odd, jnp.zeros((BLOCK, 2 * BLOCK), F32), parts[g, :BLOCK]
        ).astype(BF16)
        back[g, BLOCK:] = lax.select(
            is_odd, parts[g, 2 * BLOCK :], jnp.zeros((HALF, 2 * BLOCK), F32)
        ).astype(BF16)

        @pl.when(jnp.logical_not(mine(g)))
        def _():
            meet[g].start()

        if place % 2 == 0 and place >= 2:
            send_back(order[place - 2])
            send_back(order[place - 1])
        dq[g] = lax.dot_general(score_grad, key, TN, preferred_element_type=F32)

    send_back(order[-2])
    send_back(order[-1])
    cos_back, sin_back = cosine * inv_sqrt, sine * inv_sqrt
    q_term = jnp.zeros((BLOCK, BLOCK), F32)
    for g in range(groups):
        for j in range(per_group):
            h = g * per_group + j
            grad = dq[g, j * BLOCK : (j + 1) * BLOCK, :]
            inv = qinv[h]
            unit = q_vm[0, :, h * BLOCK : (h + 1) * BLOCK].astype(F32) * inv
            turned = grad * cos_back - roll_half(grad) * sin_back
            product = turned * unit
            q_term = q_term + product
            mean = jnp.mean(product * q_gain, axis=1, keepdims=True)
            qgrad_ref[0, :, h * BLOCK : (h + 1) * BLOCK] = (inv * (turned * q_gain - unit * mean)).astype(
                BF16
            )

    home = [
        remote(back_pair.at[g], home_pair.at[g], hp_s.at[g], hp_r.at[g], (dp, partner))
        for g in range(groups)
    ]
    for g in order:

        @pl.when(both(has_next, mine(g)))
        def _():
            return_prev[g].wait_recv()

        @pl.when(both(has_prev, mine(g)))
        def _():
            return_next[g].wait_recv()

        odd_in = home_next[g].astype(F32)
        even_in = home_prev[g].astype(F32)
        before, centre, after = parts[g, :BLOCK], parts[g, BLOCK : 2 * BLOCK], parts[g, 2 * BLOCK :]
        back_pair[g, :HALF] = lax.select(
            is_odd, before[:HALF] + even_in, after + odd_in[:HALF]
        ).astype(BF16)
        back_pair[g, HALF:] = lax.select(is_odd, before[HALF:], odd_in[HALF:]).astype(BF16)
        home[g].start()
        parts[g, BLOCK : BLOCK + HALF] = centre[:HALF] + lax.select(is_odd, odd_in[:HALF], even_in)
        parts[g, BLOCK + HALF : 2 * BLOCK] = centre[HALF:] + lax.select(
            is_odd, odd_in[HALF:], jnp.zeros((HALF, 2 * BLOCK), F32)
        )

    k_term = jnp.zeros((BLOCK, BLOCK), F32)
    for g in range(groups):
        home[g].wait_recv()
        total = parts[g, BLOCK : 2 * BLOCK] + home_pair[g].astype(F32)
        columns = slice(g * BLOCK, (g + 1) * BLOCK)
        vgrad_ref[0, :, columns] = total[:, BLOCK:].astype(BF16)
        grad = total[:, :BLOCK]
        x = k_ref[0, :, columns].astype(F32)
        inv = lax.rsqrt(jnp.mean(x * x, axis=1, keepdims=True) + norm_eps)
        unit = x * inv
        turned = grad * cosine - roll_half(grad) * sine
        product = turned * unit
        k_term = k_term + product
        mean = jnp.mean(product * k_gain, axis=1, keepdims=True)
        kgrad_ref[0, :, columns] = (inv * (turned * k_gain - unit * mean)).astype(BF16)

    term_ctx[me, 0:1] = jnp.sum(q_term, axis=0, keepdims=True)
    term_ctx[me, 1:2] = jnp.sum(k_term, axis=0, keepdims=True)

    def ctx_copy(step):
        peer = lax.rem(me + step, n)
        return remote(
            term_ctx.at[me], term_ctx.at[me], tc_s.at[step], tc_r.at[step], (dp, peer)
        )

    def dp_copy(step):
        peer = lax.rem(dp + step, n_dp)
        return remote(term_dp.at[dp], term_dp.at[dp], td_s.at[step], td_r.at[step], (peer, me))

    def run(copy_of, method):
        def body(step, carry):
            getattr(copy_of(step), method)()
            return carry

        return body

    lax.fori_loop(1, n, run(ctx_copy, "start"), 0)
    lax.fori_loop(1, n, run(ctx_copy, "wait_recv"), 0)
    term_dp[dp, 0:2] = jnp.sum(term_ctx[:, 0:2], axis=0)
    lax.fori_loop(1, n_dp, run(dp_copy, "start"), 0)

    for g in range(groups):
        pair[g].wait_send()
        home[g].wait_send()

        @pl.when(jnp.logical_not(mine(g)))
        def _():
            meet[g].wait_send()

        @pl.when(both(has_next, mine(g)))
        def _():
            send_next[g].wait_send()
            return_next[g].wait_send()
            pass_next[g].wait_send()

        @pl.when(both(has_prev, mine(g)))
        def _():
            send_prev[g].wait_send()
            return_prev[g].wait_send()
            pass_prev[g].wait_send()

    lax.fori_loop(1, n, run(ctx_copy, "wait_send"), 0)
    lax.fori_loop(1, n_dp, run(dp_copy, "wait_recv"), 0)
    sums = jnp.sum(term_dp[:, 0:2], axis=0)
    token_count = n_dp * n * BLOCK
    qgain_ref[...] = sums[0:1] * (1.0 / math.sqrt(token_count * groups * per_group))
    kgain_ref[...] = sums[1:2] * (1.0 / math.sqrt(token_count * groups))
    lax.fori_loop(1, n_dp, run(dp_copy, "wait_send"), 0)


def hand_over(*refs):
    count = (len(refs) - 1) // 2
    sems = refs[-1]
    copies = [pltpu.make_async_copy(s, d, sems.at[i]) for i, (s, d) in enumerate(zip(refs[:count], refs[count:2*count]))]
    for c in copies:
        c.start()
    for c in copies:
        c.wait()


def shards(
    q_proj,
    k_proj,
    v_proj,
    out_grad,
    q_gain,
    k_gain,
    pos_ids,
    stretch_lengths,
    stretch_windows,
    clip_ids,
    dispatch_plan,
):
    n = lax.axis_size("ctx")
    n_dp = lax.axis_size("dp")
    groups = k_proj.shape[2] // BLOCK
    heads = q_proj.shape[2] // BLOCK
    per_group = heads // groups
    hbm = pl.BlockSpec(memory_space=pl.ANY)
    dma = pltpu.SemaphoreType.DMA
    whole = pltpu.VMEM((groups, BLOCK, 2 * BLOCK), BF16)
    half = pltpu.VMEM((groups, HALF, 2 * BLOCK), BF16)
    count = stretch_lengths.shape[1]
    shapes = (
        jax.ShapeDtypeStruct(q_proj.shape, BF16),
        jax.ShapeDtypeStruct(k_proj.shape, BF16),
        jax.ShapeDtypeStruct(v_proj.shape, BF16),
        jax.ShapeDtypeStruct((1, BLOCK), F32),
        jax.ShapeDtypeStruct((1, BLOCK), F32),
    )
    both = pltpu.VMEM((groups, BLOCK + HALF, 2 * BLOCK), BF16)
    out = pl.pallas_call(
        functools.partial(kernel, n, n_dp, groups, per_group),
        out_shape=tuple(pltpu.VMEM(s.shape, s.dtype) for s in shapes),
        in_specs=[pl.BlockSpec(memory_space=pltpu.HBM)] * 11,
        out_specs=(pl.BlockSpec(memory_space=pltpu.VMEM),) * 5,
        scratch_shapes=[
            pltpu.SMEM(dispatch_plan.shape, jnp.int32),
            pltpu.VMEM(k_proj.shape, BF16),
            pltpu.VMEM(v_proj.shape, BF16),
            pltpu.VMEM((1, BLOCK), F32),
            pltpu.VMEM((1, BLOCK), F32),
            pltpu.VMEM((3, 1, BLOCK), jnp.int32),
            pltpu.VMEM((1, count), jnp.int32),
            pltpu.VMEM((1, count), jnp.int32),
            pltpu.VMEM((1, count), jnp.int32),
            pltpu.VMEM(q_proj.shape, BF16),
            pltpu.VMEM(q_proj.shape, BF16),
            pltpu.VMEM((groups, per_group * BLOCK, BLOCK), BF16),
            pltpu.VMEM((heads, BLOCK, 1), F32),
            pltpu.VMEM((groups, per_group * BLOCK, BLOCK), F32),
            whole,
            whole,
            half,
            whole,
            whole,
            half,
            pltpu.VMEM((groups, SPAN, 2 * BLOCK), F32),
            whole,
            half,
            both,
            both,
            half,
            whole,
            whole,
            whole,
            pltpu.VMEM((n, 8, BLOCK), F32),
            pltpu.VMEM((n_dp, 8, BLOCK), F32),
            dma((11,)),
        ]
        + [dma((groups,))] * 18
        + [dma((n,))] * 2
        + [dma((n_dp,))] * 2,
        compiler_params=pltpu.CompilerParams(
            collective_id=0, has_side_effects=True, vmem_limit_bytes=VMEM_LIMIT
        ),
        cost_estimate=pl.CostEstimate(
            flops=10 * heads * BLOCK * SPAN * BLOCK,
            bytes_accessed=6 * BLOCK * heads * BLOCK,
            transcendentals=heads * BLOCK * SPAN,
        ),
    )(*[pltpu.with_memory_space_constraint(a, pltpu.HBM) for a in (
        dispatch_plan,
        k_proj,
        v_proj,
        q_gain.reshape(1, BLOCK),
        k_gain.reshape(1, BLOCK),
        pos_ids.transpose(1, 0, 2),
        stretch_lengths,
        stretch_windows,
        clip_ids,
        q_proj,
        out_grad,
    )])
    out = pl.pallas_call(
        hand_over,
        out_shape=tuple(pltpu.HBM(s.shape, s.dtype) for s in shapes),
        in_specs=[hbm] * 5,
        out_specs=(pl.BlockSpec(memory_space=pltpu.HBM),) * 5,
        scratch_shapes=[dma((8,))],
    )(*[pltpu.with_memory_space_constraint(o, pltpu.VMEM) for o in out])
    return (out[0], out[1], out[2], out[3].reshape(BLOCK), out[4].reshape(BLOCK))


def solution(mesh):
    row = P("dp", "ctx", None)
    table = P("dp", None)
    return jax.shard_map(
        shards,
        mesh=mesh,
        in_specs=(row, row, row, row, P(), P(), P("dp", None, "ctx"), table, table, table, table),
        out_specs=(row, row, row, P(), P()),
        check_vma=False,
    )
```

```python
import functools
import math

import jax
import jax.numpy as jnp
from jax import lax
from jax.experimental import pallas as pl
from jax.experimental.pallas import tpu as pltpu
from jax.sharding import PartitionSpec as P

MESH = pl.DeviceIdType.MESH
F32 = jnp.float32
BF16 = jnp.bfloat16
BLOCK = 128
HALF = BLOCK // 2
SPAN = 2 * BLOCK + HALF
norm_eps = 1e-06
VMEM_LIMIT = 40 * 1024 * 1024
rope_base = 10000.0

NT = (((1,), (1,)), ((), ()))
TN = (((0,), (0,)), ((), ()))


def sin_cos(angle):
    turns = jnp.floor(angle * (2.0 / math.pi) + 0.5)
    rest = angle - turns * 1.5703125
    rest = rest - turns * 4.837512969970703125e-4
    rest = rest - turns * 7.549789948768648e-8
    square = rest * rest
    sine = rest + rest * square * (
        -1.6666654611e-1 + square * (8.3321608736e-3 + square * -1.9515295891e-4)
    )
    cosine = (
        1.0
        - 0.5 * square
        + square
        * square
        * (4.166664568298827e-2 + square * (-1.388731625493765e-3 + square * 2.443315711809948e-5))
    )
    quarter = turns.astype(jnp.int32)
    odd = (quarter & 1) == 1
    sine_out = jnp.where(odd, cosine, sine)
    cosine_out = jnp.where(odd, sine, cosine)
    sine_out = jnp.where((quarter & 2) == 2, -sine_out, sine_out)
    cosine_out = jnp.where(((quarter + 1) & 2) == 2, -cosine_out, cosine_out)
    return sine_out, cosine_out


def roll_half(x):
    return pltpu.roll(x, HALF, 1)


def rope_tables(ids):
    rows = lax.broadcasted_iota(jnp.int32, (BLOCK, BLOCK), 0)
    lanes = lax.broadcasted_iota(jnp.int32, (BLOCK, BLOCK), 1)
    columns = [
        jnp.sum(jnp.where(rows == lanes, ids[t].astype(F32), 0.0), axis=1, keepdims=True)
        for t in range(3)
    ]
    pair = lanes % HALF
    chosen = jnp.where(pair < 16, columns[0], jnp.where(pair < 40, columns[1], columns[2]))
    pair_row = lax.broadcasted_iota(jnp.int32, (1, BLOCK), 1) % HALF
    frequency = jnp.exp(pair_row.astype(F32) * (-math.log(rope_base) / HALF))
    sine, cosine = sin_cos(chosen * frequency)
    return cosine, jnp.where(lanes < HALF, -sine, sine)


def key_ranges(lengths, windows, clips, start):
    count = lengths.shape[1]
    rows = lax.broadcasted_iota(jnp.int32, (count, count), 0)
    lanes = lax.broadcasted_iota(jnp.int32, (count, count), 1)

    def column(where_, values):
        return jnp.sum(jnp.where(where_, values.astype(F32), 0.0), axis=1, keepdims=True)

    ends = column(lanes <= rows, lengths)
    starts = column(lanes < rows, lengths)
    before = column(lanes == rows - 1, lengths)
    window = column(lanes == rows, windows)
    clip = column(lanes == rows, clips + 1)
    clip_before = column(lanes == rows - 1, clips + 1)
    low = starts - jnp.where(clip == clip_before, window * before, 0.0)
    spots = (start + lax.broadcasted_iota(jnp.int32, (count, BLOCK), 1)).astype(F32)
    inside = (starts <= spots) & (spots < ends)
    low_row = jnp.sum(jnp.where(inside, low, 0.0), axis=0, keepdims=True)
    high_row = jnp.sum(jnp.where(inside, ends, 0.0), axis=0, keepdims=True)
    return low_row, high_row


def lane_sums(x, ones):
    high = x.astype(BF16)
    low = (x - high.astype(F32)).astype(BF16)
    return jnp.dot(jnp.concatenate([high, low], axis=1), ones, preferred_element_type=F32)


def fold_rows(x):
    return jnp.sum(x.reshape(x.shape[0] // 8, 8, x.shape[1]), axis=0)


def kernel(n, n_dp, groups, per_group, *refs):
    share = groups // 2
    wide = per_group * BLOCK
    refs = iter(refs)

    def take(count):
        return [next(refs) for _ in range(count)]

    (
        plan_hbm,
        k_hbm,
        v_hbm,
        qg_hbm,
        kg_hbm,
        ids_hbm,
        len_hbm,
        win_hbm,
        clip_hbm,
        q_hbm,
        do_hbm,
    ) = take(11)
    qgrad_ref, kgrad_ref, vgrad_ref, qgain_ref, kgain_ref = take(5)
    plan_ref, qg_ref, kg_ref, ids, near_ids, len_ref, win_ref, clip_ref = take(8)
    k_raw, v_raw, cosn, sinn, near_cos, near_sin, bias_ref, dk_all = take(8)
    k_out, v_out, term_pair, term_ctx, term_dp = take(5)
    q_in = take(share)
    do_in = take(share)
    kv = take(share)
    rolled = take(share)
    qrot = take(share)
    qinv = take(share)
    central = [take(2) for _ in range(share)]
    central_grad = [take(2) for _ in range(share)]
    probs_low = [take(2) for _ in range(share)]
    score_grad = [take(2) for _ in range(share)]
    dkv = take(share)
    dq = take(share)
    back_prev = take(share)
    back_next = take(share)
    arrived = take(share)
    q_out = take(share)
    load_sem, sent, got, near_s, near_r, tc_s, tc_r, td_s, td_r = take(9)

    me = lax.axis_index("ctx")
    dp = lax.axis_index("dp")
    core = lax.rem(me, 2)
    pair = me // 2
    partner = me + 1 - 2 * core
    has_prev = me >= 2
    has_next = me < n - 2
    inv_sqrt = BLOCK ** (-0.5)

    def columns(which, width, j=0):
        return pl.ds(pl.multiple_of(which * (share * width) + j * width, BLOCK), width)

    mine, theirs = core, 1 - core
    both_k = pl.ds(pl.multiple_of(mine * (share * BLOCK), BLOCK), share * BLOCK)
    their_k = pl.ds(pl.multiple_of(theirs * (share * BLOCK), BLOCK), share * BLOCK)
    moves = [
        (plan_hbm, plan_ref),
        (ids_hbm, ids.at[0]),
        (qg_hbm, qg_ref),
        (kg_hbm, kg_ref),
        (k_hbm.at[0, :, both_k], k_raw.at[0]),
        (v_hbm.at[0, :, both_k], v_raw.at[0]),
        (len_hbm, len_ref),
        (win_hbm, win_ref),
        (clip_hbm, clip_ref),
    ]
    for j in range(share):
        moves.append((q_hbm.at[0, :, columns(mine, wide, j)], q_in[j].at[0]))
        moves.append((do_hbm.at[0, :, columns(mine, wide, j)], do_in[j].at[0]))
    loads = [
        pltpu.make_async_copy(source, target, load_sem.at[i])
        for i, (source, target) in enumerate(moves)
    ]

    barrier = pltpu.get_barrier_semaphore()
    pl.semaphore_signal(barrier, inc=1, device_id=(dp, partner), device_id_type=MESH)

    def greet_ctx(step, carry):
        peer = lax.rem(partner + step, n)

        @pl.when(peer != me)
        def _():
            pl.semaphore_signal(barrier, inc=1, device_id=(dp, peer), device_id_type=MESH)

        return carry

    def greet_dp(step, carry):
        peer = lax.rem(dp + step, n_dp)
        pl.semaphore_signal(barrier, inc=1, device_id=(peer, me), device_id_type=MESH)
        return carry

    lax.fori_loop(1, n, greet_ctx, 0)
    lax.fori_loop(1, n_dp, greet_dp, 0)
    for load in loads:
        load.start()

    @pl.when(jnp.logical_not(has_prev))
    def _():
        near_ids[0] = jnp.zeros_like(near_ids[0])
        for j in range(share):
            kv[j][:BLOCK] = jnp.zeros((BLOCK, 2 * BLOCK), BF16)
            arrived[j][0, :HALF] = jnp.zeros((HALF, 2 * BLOCK), BF16)

    @pl.when(jnp.logical_not(has_next))
    def _():
        near_ids[1] = jnp.zeros_like(near_ids[1])
        for j in range(share):
            kv[j][3 * BLOCK :] = jnp.zeros((HALF, 2 * BLOCK), BF16)
            arrived[j][1] = jnp.zeros((BLOCK, 2 * BLOCK), BF16)

    for j in range(share):
        arrived[j][0, HALF:] = jnp.zeros((HALF, 2 * BLOCK), BF16)

    def remote(source, target, send, receive, peer):
        return pltpu.make_async_remote_copy(
            src_ref=source,
            dst_ref=target,
            send_sem=send,
            recv_sem=receive,
            device_id=peer,
            device_id_type=MESH,
        )

    count = [0]

    def numbered(source, target, peer):
        i = count[0]
        count[0] += 1
        return remote(source, target, sent.at[i], got.at[i], (dp, peer))

    k_swap = numbered(k_hbm.at[0, :, their_k], k_raw.at[1], partner)
    v_swap = numbered(v_hbm.at[0, :, their_k], v_raw.at[1], partner)
    ids_swap = numbered(ids_hbm, ids.at[1], partner)
    q_swap = [
        numbered(q_hbm.at[0, :, columns(theirs, wide, j)], q_in[j].at[1], partner)
        for j in range(share)
    ]
    do_swap = [
        numbered(do_hbm.at[0, :, columns(theirs, wide, j)], do_in[j].at[1], partner)
        for j in range(share)
    ]
    to_next = [
        numbered(kv[j].at[2 * BLOCK : 3 * BLOCK], kv[j].at[:BLOCK], me + 2) for j in range(share)
    ]
    to_prev = [
        numbered(kv[j].at[BLOCK : BLOCK + HALF], kv[j].at[3 * BLOCK :], me - 2)
        for j in range(share)
    ]
    home_prev = [numbered(back_prev[j], arrived[j].at[1], me - 2) for j in range(share)]
    home_next = [numbered(back_next[j], arrived[j].at[0, :HALF], me + 2) for j in range(share)]
    q_home = [
        numbered(q_out[j], qgrad_ref.at[mine, :, j * wide : (j + 1) * wide], partner)
        for j in range(share)
    ]
    k_home = numbered(k_out, kgrad_ref.at[mine], partner)
    v_home = numbered(v_out, vgrad_ref.at[mine], partner)
    term_swap = numbered(term_pair.at[0], term_pair.at[1], partner)

    def near_copy(side, other, sender):
        peer = 2 * pair + other + (2 if side == 0 else -2)
        return remote(
            ids_hbm,
            near_ids.at[side, sender],
            near_s.at[side, other],
            near_r.at[side, sender],
            (dp, peer),
        )

    pl.semaphore_wait(barrier, n - 1 + n_dp - 1)
    k_swap.start()
    v_swap.start()
    ids_swap.start()
    for j in range(share):
        q_swap[j].start()
        do_swap[j].start()

    @pl.when(has_next)
    def _():
        for other in range(2):
            near_copy(0, other, core).start()

    @pl.when(has_prev)
    def _():
        for other in range(2):
            near_copy(1, other, core).start()

    for load in loads[:9]:
        load.wait()
    odd = lax.rem(plan_ref[0, me], 2)
    slot_of = (odd, 1 - odd)
    q_gain, k_gain = qg_ref[...], kg_ref[...]
    ones = jnp.ones((2 * BLOCK, BLOCK), BF16)

    for t in range(2):
        start = (2 * pair + t) * BLOCK
        low_row, high_row = key_ranges(len_ref[...], win_ref[...], clip_ref[...], start)
        spots = (start - BLOCK + lax.broadcasted_iota(jnp.int32, (SPAN, BLOCK), 0)).astype(F32)
        bias_ref[t] = jnp.where((spots >= low_row) & (spots < high_row), 0.0, -1e30)

    ids_swap.wait_recv()
    for t in range(2):
        cosine, sine = rope_tables([ids[slot_of[t], i] for i in range(3)])
        cosn[t] = cosine
        sinn[t] = sine

    def table(t):
        return cosn[t], sinn[t]

    rolled_k_gain, rolled_q_gain = roll_half(k_gain), roll_half(q_gain)
    k_swap.wait_recv()
    v_swap.wait_recv()
    for j in range(share):
        lanes = slice(j * BLOCK, (j + 1) * BLOCK)
        for t in range(2):
            cosine, sine = table(t)
            x = k_raw[slot_of[t], :, lanes].astype(F32)
            inv = lax.rsqrt(lane_sums(x * x, ones) * (1.0 / BLOCK) + norm_eps)
            turned = inv * (x * (cosine * k_gain) + roll_half(x) * (sine * rolled_k_gain))
            spot = slice((1 + t) * BLOCK, (2 + t) * BLOCK)
            kv[j][spot, :BLOCK] = turned.astype(BF16)
            kv[j][spot, BLOCK:] = v_raw[slot_of[t], :, lanes]
            rolled[j][spot] = roll_half(turned).astype(BF16)

        @pl.when(has_next)
        def _():
            to_next[j].start()

        @pl.when(has_prev)
        def _():
            to_prev[j].start()

    def heads(value, m):
        return jnp.concatenate(
            [
                value[:, 2 * m * BLOCK : (2 * m + 1) * BLOCK],
                value[:, (2 * m + 1) * BLOCK : (2 * m + 2) * BLOCK],
            ],
            axis=0,
        )

    def stacked(value):
        return jnp.concatenate(
            [value[:, h * BLOCK : (h + 1) * BLOCK] for h in range(per_group)], axis=0
        )

    scale = inv_sqrt * math.log2(math.e)
    middle = (slice(BLOCK, SPAN), slice(0, 2 * BLOCK))
    edge = (slice(0, BLOCK), slice(2 * BLOCK, SPAN))
    offset = (0, BLOCK)

    def shifted(spot, t):
        return slice(spot.start + offset[t], spot.stop + offset[t])

    def scored(j, t, spot, m, cot):
        key = kv[j][shifted(spot, t), :BLOCK]
        value = kv[j][shifted(spot, t), BLOCK:]
        query = qrot[j][t, 2 * m * BLOCK : (2 * m + 2) * BLOCK, :]
        scores = lax.dot_general(key, query, NT, preferred_element_type=F32)
        grad = lax.dot_general(value, cot, NT, preferred_element_type=F32)
        bias = bias_ref[t, spot]
        weights = jnp.exp2(scores * scale + jnp.concatenate([bias, bias], axis=1))
        return weights, grad

    sums = {}
    for j in range(share):
        loads[9 + 2 * j].wait()
        loads[10 + 2 * j].wait()
        q_swap[j].wait_recv()
        do_swap[j].wait_recv()
        for t in range(2):
            cosine, sine = table(t)
            qc, qs = cosine * q_gain, sine * rolled_q_gain
            for h in range(per_group):
                lanes = slice(h * BLOCK, (h + 1) * BLOCK)
                x = q_in[j][slot_of[t], :, lanes].astype(F32)
                inv = lax.rsqrt(lane_sums(x * x, ones) * (1.0 / BLOCK) + norm_eps)
                qinv[j][t, :, lanes] = inv
                qrot[j][t, lanes, :] = (inv * (x * qc + roll_half(x) * qs)).astype(BF16)
            for m in range(per_group // 2):
                lanes = slice(2 * m * BLOCK, (2 * m + 2) * BLOCK)
                cot = heads(do_in[j][slot_of[t]], m)
                weights, grad = scored(j, t, middle[t], m, cot)
                central[j][t][:, lanes] = weights
                central_grad[j][t][:, lanes] = grad
                sums[j, t, m] = (
                    jnp.sum(weights, axis=0, keepdims=True),
                    jnp.sum(weights * grad, axis=0, keepdims=True),
                )

    @pl.when(has_prev)
    def _():
        for sender in range(2):
            near_copy(0, sender, sender).wait_recv()

    @pl.when(has_next)
    def _():
        for sender in range(2):
            near_copy(1, sender, sender).wait_recv()

    before = 1 - lax.rem(plan_ref[0, lax.max(2 * pair - 2, 0)], 2)
    after = lax.rem(plan_ref[0, lax.min(2 * pair + 2, n - 2)], 2)
    cosine, sine = rope_tables([near_ids[0, before, i] for i in range(3)])
    near_cos[:BLOCK] = cosine
    near_sin[:BLOCK] = sine
    cosine, sine = rope_tables([near_ids[1, after, i] for i in range(3)])
    near_cos[BLOCK:] = cosine[:HALF]
    near_sin[BLOCK:] = sine[:HALF]

    for j in range(share):

        @pl.when(has_prev)
        def _():
            to_next[j].wait_recv()

        @pl.when(has_next)
        def _():
            to_prev[j].wait_recv()

        for t in range(2):
            spot = edge[t]
            for m in range(per_group // 2):
                lanes = slice(2 * m * BLOCK, (2 * m + 2) * BLOCK)
                cot = heads(do_in[j][slot_of[t]], m)
                weights, grad = scored(j, t, spot, m, cot)
                total, delta = sums[j, t, m]
                inverse = 1.0 / (total + jnp.sum(weights, axis=0, keepdims=True))
                delta = (delta + jnp.sum(weights * grad, axis=0, keepdims=True)) * inverse
                sums[j, t, m] = (inverse, delta)
                probs = weights * inverse
                probs_low[j][t][spot, lanes] = probs.astype(BF16)
                score_grad[j][t][spot, lanes] = (probs * (grad - delta)).astype(BF16)
            key_grad = (
                jnp.dot(score_grad[j][t][spot], qrot[j][t], preferred_element_type=F32) * inv_sqrt
            )
            value_grad = jnp.dot(
                probs_low[j][t][spot],
                stacked(do_in[j][slot_of[t]]),
                preferred_element_type=F32,
            )
            dk_all[j, shifted(spot, t)] = key_grad
            back = (back_prev, back_next)[t][j]
            back[:, :BLOCK] = key_grad.astype(BF16)
            back[:, BLOCK:] = value_grad.astype(BF16)

            @pl.when((has_prev, has_next)[t])
            def _():
                (home_prev, home_next)[t][j].start()

    q_term = jnp.zeros((8, BLOCK), F32)
    k_term = jnp.zeros((8, BLOCK), F32)
    for j in range(share):
        own_key = kv[j][:, :BLOCK].astype(F32)
        rolled[j][:BLOCK] = roll_half(own_key[:BLOCK]).astype(BF16)
        rolled[j][3 * BLOCK :] = roll_half(own_key[3 * BLOCK :]).astype(BF16)
        parts = []
        for t in range(2):
            spot = middle[t]
            for m in range(per_group // 2):
                lanes = slice(2 * m * BLOCK, (2 * m + 2) * BLOCK)
                inverse, delta = sums[j, t, m]
                probs = central[j][t][:, lanes] * inverse
                probs_low[j][t][spot, lanes] = probs.astype(BF16)
                score_grad[j][t][spot, lanes] = (
                    probs * (central_grad[j][t][:, lanes] - delta)
                ).astype(BF16)
            key_grad = (
                jnp.dot(score_grad[j][t][spot], qrot[j][t], preferred_element_type=F32) * inv_sqrt
            )
            value_grad = jnp.dot(
                probs_low[j][t][spot],
                stacked(do_in[j][slot_of[t]]),
                preferred_element_type=F32,
            )
            parts.append((key_grad, value_grad))
            window = slice(offset[t], offset[t] + SPAN)
            keys = jnp.concatenate([kv[j][window, :BLOCK], rolled[j][window]], axis=1)
            dq[j][t] = lax.dot_general(score_grad[j][t][...], keys, TN, preferred_element_type=F32)
        for i in range(2):
            even, late = parts[0][i], parts[1][i]
            lanes = slice(i * BLOCK, (i + 1) * BLOCK)
            dkv[j][0, :, lanes] = even[:BLOCK] + late[:BLOCK]
            dkv[j][1, :HALF, lanes] = even[BLOCK:] + late[BLOCK : BLOCK + HALF]
            dkv[j][1, HALF:, lanes] = late[BLOCK + HALF :]
        for t in range(2):
            dk_all[j, (1 + t) * BLOCK : (2 + t) * BLOCK] = dkv[j][t, :, :BLOCK]
        key, grad = own_key, dk_all[j]
        cosine, sine = (
            jnp.concatenate([near[:BLOCK], own[0], own[1], near[BLOCK:]], axis=0)
            for near, own in ((near_cos, cosn), (near_sin, sinn))
        )
        product = (grad * cosine - roll_half(grad) * sine) * (
            key * cosine - rolled[j][...].astype(F32) * sine
        )
        k_term = k_term + fold_rows(product)

        for s in range(2):
            t = slot_of[s]
            cos_back, sin_back = cosn[t] * inv_sqrt, sinn[t] * inv_sqrt
            for h in range(per_group):
                lanes = slice(h * BLOCK, (h + 1) * BLOCK)
                grad = dq[j][t, lanes, :BLOCK]
                turned = grad * cos_back - dq[j][t, lanes, BLOCK:] * sin_back
                inv = qinv[j][t, :, lanes]
                unit = q_in[j][s, :, lanes].astype(F32) * inv
                product = turned * unit
                q_term = q_term + fold_rows(product)
                mean = lane_sums(product * q_gain, ones) * (1.0 / BLOCK)
                result = (inv * (turned * q_gain - unit * mean)).astype(BF16)
                if s == 0:
                    qgrad_ref[mine, :, j * wide + h * BLOCK : j * wide + (h + 1) * BLOCK] = result
                else:
                    q_out[j][:, lanes] = result
        q_home[j].start()

    term_pair[0, 0:1] = jnp.sum(q_term, axis=0, keepdims=True)
    term_pair[0, 1:2] = jnp.sum(k_term, axis=0, keepdims=True) / k_gain
    term_swap.start()

    def ctx_copy(step):
        peer = lax.rem(pair + step, n // 2)
        return remote(
            term_ctx.at[pair],
            term_ctx.at[pair],
            tc_s.at[step],
            tc_r.at[step],
            (dp, 2 * peer + core),
        )

    def dp_copy(step):
        peer = lax.rem(dp + step, n_dp)
        return remote(term_dp.at[dp], term_dp.at[dp], td_s.at[step], td_r.at[step], (peer, me))

    def run(copy_of, method):
        def body(step, carry):
            getattr(copy_of(step), method)()
            return carry

        return body

    term_swap.wait_recv()
    term_ctx[pair, 0:2] = term_pair[0, 0:2] + term_pair[1, 0:2]
    lax.fori_loop(1, n // 2, run(ctx_copy, "start"), 0)

    for j in range(share):

        @pl.when(has_next)
        def _():
            home_prev[j].wait_recv()

        @pl.when(has_prev)
        def _():
            home_next[j].wait_recv()

        lanes = slice(j * BLOCK, (j + 1) * BLOCK)
        for s in (1, 0):
            t = slot_of[s]
            cosine, sine = table(t)
            total = dkv[j][t] + arrived[j][t].astype(F32)
            grad = total[:, :BLOCK]
            x = k_raw[s, :, lanes].astype(F32)
            inv = lax.rsqrt(lane_sums(x * x, ones) * (1.0 / BLOCK) + norm_eps)
            unit = x * inv
            turned = grad * cosine - roll_half(grad) * sine
            mean = lane_sums(turned * unit * k_gain, ones) * (1.0 / BLOCK)
            result = (inv * (turned * k_gain - unit * mean)).astype(BF16)
            if s == 0:
                kgrad_ref[mine, :, lanes] = result
                vgrad_ref[mine, :, lanes] = total[:, BLOCK:].astype(BF16)
            else:
                k_out[:, lanes] = result
                v_out[:, lanes] = total[:, BLOCK:].astype(BF16)
    k_home.start()
    v_home.start()

    lax.fori_loop(1, n // 2, run(ctx_copy, "wait_recv"), 0)
    term_dp[dp, 0:2] = jnp.sum(term_ctx[:, 0:2], axis=0)
    lax.fori_loop(1, n_dp, run(dp_copy, "start"), 0)

    ids_swap.wait_send()
    k_swap.wait_send()
    v_swap.wait_send()
    for j in range(share):
        q_swap[j].wait_send()
        do_swap[j].wait_send()
        q_home[j].wait_recv()
        q_home[j].wait_send()

        @pl.when(has_next)
        def _():
            to_next[j].wait_send()
            home_next[j].wait_send()

        @pl.when(has_prev)
        def _():
            to_prev[j].wait_send()
            home_prev[j].wait_send()

    @pl.when(has_next)
    def _():
        for other in range(2):
            near_copy(0, other, core).wait_send()

    @pl.when(has_prev)
    def _():
        for other in range(2):
            near_copy(1, other, core).wait_send()

    term_swap.wait_send()
    lax.fori_loop(1, n // 2, run(ctx_copy, "wait_send"), 0)
    k_home.wait_recv()
    v_home.wait_recv()
    k_home.wait_send()
    v_home.wait_send()
    lax.fori_loop(1, n_dp, run(dp_copy, "wait_recv"), 0)
    totals = jnp.sum(term_dp[:, 0:2], axis=0)
    token_count = n_dp * n * BLOCK
    qgain_ref[...] = totals[0:1] * (1.0 / math.sqrt(token_count * groups * per_group))
    kgain_ref[...] = totals[1:2] * (1.0 / math.sqrt(token_count * groups))
    lax.fori_loop(1, n_dp, run(dp_copy, "wait_send"), 0)


def hand_over(*refs):
    sources, targets, sems = refs[:5], refs[5:10], refs[10]
    copies = []
    for source, target in zip(sources, targets):
        if len(source.shape) == 2:
            copies.append((source, target))
        else:
            width = source.shape[2]
            for half in range(2):
                lanes = slice(half * width, (half + 1) * width)
                copies.append((source.at[half], target.at[0, :, lanes]))
    copies = [
        pltpu.make_async_copy(source, target, sems.at[i])
        for i, (source, target) in enumerate(copies)
    ]
    for copy in copies:
        copy.start()
    for copy in copies:
        copy.wait()


def shards(
    q_proj,
    k_proj,
    v_proj,
    out_grad,
    q_gain,
    k_gain,
    pos_ids,
    stretch_lengths,
    stretch_windows,
    clip_ids,
    dispatch_plan,
):
    n = lax.axis_size("ctx")
    n_dp = lax.axis_size("dp")
    groups = k_proj.shape[2] // BLOCK
    heads = q_proj.shape[2] // BLOCK
    per_group = heads // groups
    share = groups // 2
    wide = per_group * BLOCK
    hbm = pl.BlockSpec(memory_space=pl.ANY)
    vmem = pl.BlockSpec(memory_space=pltpu.VMEM)
    dma = pltpu.SemaphoreType.DMA
    count = stretch_lengths.shape[1]
    nat = 3 * BLOCK + HALF
    central = (SPAN - BLOCK, 2 * BLOCK)
    out = pl.pallas_call(
        functools.partial(kernel, n, n_dp, groups, per_group),
        out_shape=(
            pltpu.VMEM((2, BLOCK, share * wide), BF16),
            pltpu.VMEM((2, BLOCK, share * BLOCK), BF16),
            pltpu.VMEM((2, BLOCK, share * BLOCK), BF16),
            pltpu.VMEM((1, BLOCK), F32),
            pltpu.VMEM((1, BLOCK), F32),
        ),
        in_specs=[hbm] * 11,
        out_specs=(vmem,) * 5,
        scratch_shapes=[
            pltpu.SMEM(dispatch_plan.shape, jnp.int32),
            pltpu.VMEM((1, BLOCK), F32),
            pltpu.VMEM((1, BLOCK), F32),
            pltpu.VMEM((2, 3, 1, BLOCK), jnp.int32),
            pltpu.VMEM((2, 2, 3, 1, BLOCK), jnp.int32),
            pltpu.VMEM((1, count), jnp.int32),
            pltpu.VMEM((1, count), jnp.int32),
            pltpu.VMEM((1, count), jnp.int32),
            pltpu.VMEM((2, BLOCK, share * BLOCK), BF16),
            pltpu.VMEM((2, BLOCK, share * BLOCK), BF16),
            pltpu.VMEM((2, BLOCK, BLOCK), F32),
            pltpu.VMEM((2, BLOCK, BLOCK), F32),
            pltpu.VMEM((BLOCK + HALF, BLOCK), F32),
            pltpu.VMEM((BLOCK + HALF, BLOCK), F32),
            pltpu.VMEM((2, SPAN, BLOCK), F32),
            pltpu.VMEM((share, nat, BLOCK), F32),
            pltpu.VMEM((BLOCK, share * BLOCK), BF16),
            pltpu.VMEM((BLOCK, share * BLOCK), BF16),
            pltpu.VMEM((2, 8, BLOCK), F32),
            pltpu.VMEM((n // 2, 8, BLOCK), F32),
            pltpu.VMEM((n_dp, 8, BLOCK), F32),
        ]
        + [pltpu.VMEM((2, BLOCK, wide), BF16)] * (2 * share)
        + [pltpu.VMEM((nat, 2 * BLOCK), BF16)] * share
        + [pltpu.VMEM((nat, BLOCK), BF16)] * share
        + [pltpu.VMEM((2, wide, BLOCK), BF16)] * share
        + [pltpu.VMEM((2, BLOCK, wide), F32)] * share
        + [pltpu.VMEM((rows, wide), F32) for rows in central] * (2 * share)
        + [pltpu.VMEM((SPAN, wide), BF16)] * (4 * share)
        + [pltpu.VMEM((2, BLOCK, 2 * BLOCK), F32)] * share
        + [pltpu.VMEM((2, wide, 2 * BLOCK), F32)] * share
        + [pltpu.VMEM((BLOCK, 2 * BLOCK), BF16)] * share
        + [pltpu.VMEM((HALF, 2 * BLOCK), BF16)] * share
        + [pltpu.VMEM((2, BLOCK, 2 * BLOCK), BF16)] * share
        + [pltpu.VMEM((BLOCK, wide), BF16)] * share
        + [
            dma((9 + 2 * share,)),
            dma((6 + 7 * share,)),
            dma((6 + 7 * share,)),
            dma((2, 2)),
            dma((2, 2)),
            dma((n // 2,)),
            dma((n // 2,)),
            dma((n_dp,)),
            dma((n_dp,)),
        ],
        compiler_params=pltpu.CompilerParams(
            collective_id=0, has_side_effects=True, vmem_limit_bytes=VMEM_LIMIT
        ),
        cost_estimate=pl.CostEstimate(
            flops=10 * heads * BLOCK * SPAN * BLOCK,
            bytes_accessed=6 * BLOCK * heads * BLOCK,
            transcendentals=heads * BLOCK * SPAN,
        ),
    )(
        *[
            pltpu.with_memory_space_constraint(array, pltpu.HBM)
            for array in (
                dispatch_plan,
                k_proj,
                v_proj,
                q_gain.reshape(1, BLOCK),
                k_gain.reshape(1, BLOCK),
                pos_ids.transpose(1, 0, 2),
                stretch_lengths,
                stretch_windows,
                clip_ids,
                q_proj,
                out_grad,
            )
        ]
    )
    out = pl.pallas_call(
        hand_over,
        out_shape=(
            pltpu.HBM(q_proj.shape, BF16),
            pltpu.HBM(k_proj.shape, BF16),
            pltpu.HBM(v_proj.shape, BF16),
            pltpu.HBM((1, BLOCK), F32),
            pltpu.HBM((1, BLOCK), F32),
        ),
        in_specs=[hbm] * 5,
        out_specs=(pl.BlockSpec(memory_space=pltpu.HBM),) * 5,
        scratch_shapes=[dma((8,))],
    )(*[pltpu.with_memory_space_constraint(array, pltpu.VMEM) for array in out])
    return (out[0], out[1], out[2], out[3].reshape(BLOCK), out[4].reshape(BLOCK))


def solution(mesh):
    row = P("dp", "ctx", None)
    table = P("dp", None)
    return jax.shard_map(
        shards,
        mesh=mesh,
        in_specs=(row, row, row, row, P(), P(), P("dp", None, "ctx"), table, table, table, table),
        out_specs=(row, row, row, P(), P()),
        check_vma=False,
    )
```

```python
import functools
import math

import jax
import jax.numpy as jnp
from jax import lax
from jax.experimental import pallas as pl
from jax.experimental.pallas import tpu as pltpu
from jax.sharding import PartitionSpec as P

MESH = pl.DeviceIdType.MESH
F32 = jnp.float32
BF16 = jnp.bfloat16
BLOCK = 128
HALF = BLOCK // 2
SPAN = 2 * BLOCK + HALF
norm_eps = 1e-06
VMEM_LIMIT = 40 * 1024 * 1024
rope_base = 10000.0

NT = (((1,), (1,)), ((), ()))
TN = (((0,), (0,)), ((), ()))


def sin_cos(angle):
    turns = jnp.floor(angle * (2.0 / math.pi) + 0.5)
    rest = angle - turns * 1.5703125
    rest = rest - turns * 4.837512969970703125e-4
    rest = rest - turns * 7.549789948768648e-8
    square = rest * rest
    sine = rest + rest * square * (
        -1.6666654611e-1 + square * (8.3321608736e-3 + square * -1.9515295891e-4)
    )
    cosine = (
        1.0
        - 0.5 * square
        + square
        * square
        * (4.166664568298827e-2 + square * (-1.388731625493765e-3 + square * 2.443315711809948e-5))
    )
    quarter = turns.astype(jnp.int32)
    odd = (quarter & 1) == 1
    sine_out = jnp.where(odd, cosine, sine)
    cosine_out = jnp.where(odd, sine, cosine)
    sine_out = jnp.where((quarter & 2) == 2, -sine_out, sine_out)
    cosine_out = jnp.where(((quarter + 1) & 2) == 2, -cosine_out, cosine_out)
    return sine_out, cosine_out


def roll_half(x):
    return pltpu.roll(x, HALF, 1)


def rope_tables(ids):
    rows = lax.broadcasted_iota(jnp.int32, (BLOCK, BLOCK), 0)
    lanes = lax.broadcasted_iota(jnp.int32, (BLOCK, BLOCK), 1)
    columns = [
        jnp.sum(jnp.where(rows == lanes, ids[t].astype(F32), 0.0), axis=1, keepdims=True)
        for t in range(3)
    ]
    pair = lanes % HALF
    chosen = jnp.where(pair < 16, columns[0], jnp.where(pair < 40, columns[1], columns[2]))
    pair_row = lax.broadcasted_iota(jnp.int32, (1, BLOCK), 1) % HALF
    frequency = jnp.exp(pair_row.astype(F32) * (-math.log(rope_base) / HALF))
    sine, cosine = sin_cos(chosen * frequency)
    return cosine, jnp.where(lanes < HALF, -sine, sine)


def key_ranges(lengths, windows, clips, start):
    count = lengths.shape[1]
    rows = lax.broadcasted_iota(jnp.int32, (count, count), 0)
    lanes = lax.broadcasted_iota(jnp.int32, (count, count), 1)

    def column(where_, values):
        return jnp.sum(jnp.where(where_, values.astype(F32), 0.0), axis=1, keepdims=True)

    ends = column(lanes <= rows, lengths)
    starts = column(lanes < rows, lengths)
    before = column(lanes == rows - 1, lengths)
    window = column(lanes == rows, windows)
    clip = column(lanes == rows, clips + 1)
    clip_before = column(lanes == rows - 1, clips + 1)
    low = starts - jnp.where(clip == clip_before, window * before, 0.0)
    spots = (start + lax.broadcasted_iota(jnp.int32, (count, BLOCK), 1)).astype(F32)
    inside = (starts <= spots) & (spots < ends)
    low_row = jnp.sum(jnp.where(inside, low, 0.0), axis=0, keepdims=True)
    high_row = jnp.sum(jnp.where(inside, ends, 0.0), axis=0, keepdims=True)
    return low_row, high_row


def lane_sums(x, ones):
    high = x.astype(BF16)
    low = (x - high.astype(F32)).astype(BF16)
    return jnp.dot(jnp.concatenate([high, low], axis=1), ones, preferred_element_type=F32)


def fold_rows(x):
    return jnp.sum(x.reshape(x.shape[0] // 8, 8, x.shape[1]), axis=0)


def kernel(n, n_dp, groups, per_group, *refs):
    share = groups // 2
    wide = per_group * BLOCK
    refs = iter(refs)

    def take(count):
        return [next(refs) for _ in range(count)]

    (
        plan_hbm,
        k_hbm,
        v_hbm,
        qg_hbm,
        kg_hbm,
        ids_hbm,
        len_hbm,
        win_hbm,
        clip_hbm,
        q_hbm,
        do_hbm,
    ) = take(11)
    qgrad_ref, kgrad_ref, vgrad_ref, qgain_ref, kgain_ref = take(5)
    plan_ref, qg_ref, kg_ref, ids, near_ids, len_ref, win_ref, clip_ref = take(8)
    k_raw, v_raw, cosn, sinn, near_cos, near_sin, bias_ref, dk_all = take(8)
    k_out, v_out, term_ctx, term_dp = take(4)
    q_in = take(share)
    do_in = take(share)
    kv = take(share)
    rolled = take(share)
    qrot = take(share)
    qinv = take(share)
    central = [take(2) for _ in range(share)]
    central_grad = [take(2) for _ in range(share)]
    probs_low = [take(2) for _ in range(share)]
    score_grad = [take(2) for _ in range(share)]
    dkv = take(share)
    dq = take(share)
    back_prev = take(share)
    back_next = take(share)
    arrived = take(share)
    q_out = take(share)
    q_turned = take(share)
    q_unit = take(share)
    load_sem, sent, got, near_s, near_r, tc_s, tc_r, td_s, td_r = take(9)

    me = lax.axis_index("ctx")
    dp = lax.axis_index("dp")
    core = lax.rem(me, 2)
    pair = me // 2
    partner = me + 1 - 2 * core
    has_prev = me >= 2
    has_next = me < n - 2
    inv_sqrt = BLOCK ** (-0.5)

    def columns(which, width, j=0):
        return pl.ds(pl.multiple_of(which * (share * width) + j * width, BLOCK), width)

    mine, theirs = core, 1 - core
    both_k = pl.ds(pl.multiple_of(mine * (share * BLOCK), BLOCK), share * BLOCK)
    their_k = pl.ds(pl.multiple_of(theirs * (share * BLOCK), BLOCK), share * BLOCK)
    moves = [
        (plan_hbm, plan_ref),
        (ids_hbm, ids.at[0]),
        (qg_hbm, qg_ref),
        (kg_hbm, kg_ref),
        (k_hbm.at[0, :, both_k], k_raw.at[0]),
        (v_hbm.at[0, :, both_k], v_raw.at[0]),
        (len_hbm, len_ref),
        (win_hbm, win_ref),
        (clip_hbm, clip_ref),
    ]
    for j in range(share):
        moves.append((q_hbm.at[0, :, columns(mine, wide, j)], q_in[j].at[0]))
        moves.append((do_hbm.at[0, :, columns(mine, wide, j)], do_in[j].at[0]))
    loads = [
        pltpu.make_async_copy(source, target, load_sem.at[i])
        for i, (source, target) in enumerate(moves)
    ]

    barrier = pltpu.get_barrier_semaphore()
    pl.semaphore_signal(barrier, inc=1, device_id=(dp, partner), device_id_type=MESH)

    def greet_ctx(step, carry):
        peer = lax.rem(partner + step, n)

        @pl.when(peer != me)
        def _():
            pl.semaphore_signal(barrier, inc=1, device_id=(dp, peer), device_id_type=MESH)

        return carry

    def greet_dp(step, carry):
        peer = lax.rem(dp + step, n_dp)
        pl.semaphore_signal(barrier, inc=1, device_id=(peer, me), device_id_type=MESH)
        return carry

    lax.fori_loop(1, n, greet_ctx, 0)
    lax.fori_loop(1, n_dp, greet_dp, 0)
    for load in loads:
        load.start()

    @pl.when(jnp.logical_not(has_prev))
    def _():
        near_ids[0] = jnp.zeros_like(near_ids[0])
        for j in range(share):
            kv[j][:BLOCK] = jnp.zeros((BLOCK, 2 * BLOCK), BF16)
            arrived[j][0, :HALF] = jnp.zeros((HALF, 2 * BLOCK), BF16)

    @pl.when(jnp.logical_not(has_next))
    def _():
        near_ids[1] = jnp.zeros_like(near_ids[1])
        for j in range(share):
            kv[j][3 * BLOCK :] = jnp.zeros((HALF, 2 * BLOCK), BF16)
            arrived[j][1] = jnp.zeros((BLOCK, 2 * BLOCK), BF16)

    for j in range(share):
        arrived[j][0, HALF:] = jnp.zeros((HALF, 2 * BLOCK), BF16)

    def remote(source, target, send, receive, peer):
        return pltpu.make_async_remote_copy(
            src_ref=source,
            dst_ref=target,
            send_sem=send,
            recv_sem=receive,
            device_id=peer,
            device_id_type=MESH,
        )

    count = [0]

    def numbered(source, target, peer):
        i = count[0]
        count[0] += 1
        return remote(source, target, sent.at[i], got.at[i], (dp, peer))

    k_swap = numbered(k_hbm.at[0, :, their_k], k_raw.at[1], partner)
    v_swap = numbered(v_hbm.at[0, :, their_k], v_raw.at[1], partner)
    ids_swap = numbered(ids_hbm, ids.at[1], partner)
    q_swap = [
        numbered(q_hbm.at[0, :, columns(theirs, wide, j)], q_in[j].at[1], partner)
        for j in range(share)
    ]
    do_swap = [
        numbered(do_hbm.at[0, :, columns(theirs, wide, j)], do_in[j].at[1], partner)
        for j in range(share)
    ]
    to_next = [
        numbered(kv[j].at[2 * BLOCK : 3 * BLOCK], kv[j].at[:BLOCK], me + 2) for j in range(share)
    ]
    to_prev = [
        numbered(kv[j].at[BLOCK : BLOCK + HALF], kv[j].at[3 * BLOCK :], me - 2)
        for j in range(share)
    ]
    home_prev = [numbered(back_prev[j], arrived[j].at[1], me - 2) for j in range(share)]
    home_next = [numbered(back_next[j], arrived[j].at[0, :HALF], me + 2) for j in range(share)]
    q_home = [
        numbered(q_out[j], qgrad_ref.at[mine, :, j * wide : (j + 1) * wide], partner)
        for j in range(share)
    ]
    k_home = numbered(k_out, kgrad_ref.at[mine], partner)
    v_home = numbered(v_out, vgrad_ref.at[mine], partner)

    def near_copy(side, other, sender):
        peer = 2 * pair + other + (2 if side == 0 else -2)
        return remote(
            ids_hbm,
            near_ids.at[side, sender],
            near_s.at[side, other],
            near_r.at[side, sender],
            (dp, peer),
        )

    pl.semaphore_wait(barrier, n - 1 + n_dp - 1)
    ids_swap.start()
    k_swap.start()
    v_swap.start()
    for j in range(share):
        q_swap[j].start()
        do_swap[j].start()

    @pl.when(has_next)
    def _():
        for other in range(2):
            near_copy(0, other, core).start()

    @pl.when(has_prev)
    def _():
        for other in range(2):
            near_copy(1, other, core).start()

    for load in loads[:9]:
        load.wait()
    odd = lax.rem(plan_ref[0, me], 2)
    slot_of = (odd, 1 - odd)
    q_gain, k_gain = qg_ref[...], kg_ref[...]
    ones = jnp.ones((2 * BLOCK, BLOCK), BF16)

    for s in range(2):
        if s == 1:
            ids_swap.wait_recv()
        cosine, sine = rope_tables([ids[s, i] for i in range(3)])
        cosn[s] = cosine
        sinn[s] = sine

    def table(t):
        return cosn[slot_of[t]], sinn[slot_of[t]]

    rolled_k_gain, rolled_q_gain = roll_half(k_gain), roll_half(q_gain)
    k_swap.wait_recv()
    v_swap.wait_recv()
    for j in range(share):
        lanes = slice(j * BLOCK, (j + 1) * BLOCK)
        for t in range(2):
            cosine, sine = table(t)
            x = k_raw[slot_of[t], :, lanes].astype(F32)
            inv = lax.rsqrt(lane_sums(x * x, ones) * (1.0 / BLOCK) + norm_eps)
            turned = inv * (x * (cosine * k_gain) + roll_half(x) * (sine * rolled_k_gain))
            spot = slice((1 + t) * BLOCK, (2 + t) * BLOCK)
            kv[j][spot, :BLOCK] = turned.astype(BF16)
            kv[j][spot, BLOCK:] = v_raw[slot_of[t], :, lanes]
            rolled[j][spot] = roll_half(turned).astype(BF16)

        @pl.when(has_prev)
        def _():
            to_prev[j].start()

        @pl.when(has_next)
        def _():
            to_next[j].start()

    for t in range(2):
        start = (2 * pair + t) * BLOCK
        low_row, high_row = key_ranges(len_ref[...], win_ref[...], clip_ref[...], start)
        spots = (start - BLOCK + lax.broadcasted_iota(jnp.int32, (SPAN, BLOCK), 0)).astype(F32)
        bias_ref[t] = jnp.where((spots >= low_row) & (spots < high_row), 0.0, -1e30)

    def heads(value, m):
        return jnp.concatenate(
            [
                value[:, 2 * m * BLOCK : (2 * m + 1) * BLOCK],
                value[:, (2 * m + 1) * BLOCK : (2 * m + 2) * BLOCK],
            ],
            axis=0,
        )

    def stacked(value):
        return jnp.concatenate(
            [value[:, h * BLOCK : (h + 1) * BLOCK] for h in range(per_group)], axis=0
        )

    scale = inv_sqrt * math.log2(math.e)
    middle = (slice(BLOCK, SPAN), slice(0, 2 * BLOCK))
    edge = (slice(0, BLOCK), slice(2 * BLOCK, SPAN))
    offset = (0, BLOCK)

    def shifted(spot, t):
        return slice(spot.start + offset[t], spot.stop + offset[t])

    def scored(j, t, spot, m, cot):
        key = kv[j][shifted(spot, t), :BLOCK]
        value = kv[j][shifted(spot, t), BLOCK:]
        query = qrot[j][t, 2 * m * BLOCK : (2 * m + 2) * BLOCK, :]
        scores = lax.dot_general(key, query, NT, preferred_element_type=F32)
        grad = lax.dot_general(value, cot, NT, preferred_element_type=F32)
        bias = bias_ref[t, spot]
        weights = jnp.exp2(scores * scale + jnp.concatenate([bias, bias], axis=1))
        return weights, grad

    sums = {}
    for j in range(share):
        loads[9 + 2 * j].wait()
        loads[10 + 2 * j].wait()
        q_swap[j].wait_recv()
        do_swap[j].wait_recv()
        for t in range(2):
            cosine, sine = table(t)
            qc, qs = cosine * q_gain, sine * rolled_q_gain
            for h in range(per_group):
                lanes = slice(h * BLOCK, (h + 1) * BLOCK)
                x = q_in[j][slot_of[t], :, lanes].astype(F32)
                inv = lax.rsqrt(lane_sums(x * x, ones) * (1.0 / BLOCK) + norm_eps)
                qinv[j][t, :, lanes] = inv
                qrot[j][t, lanes, :] = (inv * (x * qc + roll_half(x) * qs)).astype(BF16)
            for m in range(per_group // 2):
                lanes = slice(2 * m * BLOCK, (2 * m + 2) * BLOCK)
                cot = heads(do_in[j][slot_of[t]], m)
                weights, grad = scored(j, t, middle[t], m, cot)
                central[j][t][:, lanes] = weights
                central_grad[j][t][:, lanes] = grad
                sums[j, t, m] = (
                    jnp.sum(weights, axis=0, keepdims=True),
                    jnp.sum(weights * grad, axis=0, keepdims=True),
                )

    @pl.when(has_prev)
    def _():
        for sender in range(2):
            near_copy(0, sender, sender).wait_recv()

    @pl.when(has_next)
    def _():
        for sender in range(2):
            near_copy(1, sender, sender).wait_recv()

    before = 1 - lax.rem(plan_ref[0, lax.max(2 * pair - 2, 0)], 2)
    after = lax.rem(plan_ref[0, lax.min(2 * pair + 2, n - 2)], 2)
    cosine, sine = rope_tables([near_ids[0, before, i] for i in range(3)])
    near_cos[:BLOCK] = cosine
    near_sin[:BLOCK] = sine
    cosine, sine = rope_tables([near_ids[1, after, i] for i in range(3)])
    near_cos[BLOCK:] = cosine[:HALF]
    near_sin[BLOCK:] = sine[:HALF]

    def join(j, i, parts):
        even, late = parts
        lanes = slice(i * BLOCK, (i + 1) * BLOCK)
        dkv[j][0, :, lanes] = even[:BLOCK] + late[:BLOCK]
        dkv[j][1, :HALF, lanes] = even[BLOCK:] + late[BLOCK : BLOCK + HALF]
        dkv[j][1, HALF:, lanes] = late[BLOCK + HALF :]

    q_term = jnp.zeros((8, BLOCK), F32)
    k_term = jnp.zeros((8, BLOCK), F32)
    for j in range(share):

        @pl.when(has_prev)
        def _():
            to_next[j].wait_recv()

        @pl.when(has_next)
        def _():
            to_prev[j].wait_recv()

        for t in range(2):
            spot = edge[t]
            for m in range(per_group // 2):
                lanes = slice(2 * m * BLOCK, (2 * m + 2) * BLOCK)
                cot = heads(do_in[j][slot_of[t]], m)
                weights, grad = scored(j, t, spot, m, cot)
                total, delta = sums[j, t, m]
                inverse = 1.0 / (total + jnp.sum(weights, axis=0, keepdims=True))
                delta = (delta + jnp.sum(weights * grad, axis=0, keepdims=True)) * inverse
                sums[j, t, m] = (inverse, delta)
                probs = weights * inverse
                probs_low[j][t][spot, lanes] = probs.astype(BF16)
                score_grad[j][t][spot, lanes] = (probs * (grad - delta)).astype(BF16)
            key_grad = (
                jnp.dot(score_grad[j][t][spot], qrot[j][t], preferred_element_type=F32) * inv_sqrt
            )
            value_grad = jnp.dot(
                probs_low[j][t][spot],
                stacked(do_in[j][slot_of[t]]),
                preferred_element_type=F32,
            )
            dk_all[j, shifted(spot, t)] = key_grad
            back = (back_prev, back_next)[t][j]
            back[:, :BLOCK] = key_grad.astype(BF16)
            back[:, BLOCK:] = value_grad.astype(BF16)

            @pl.when((has_prev, has_next)[t])
            def _():
                (home_prev, home_next)[t][j].start()

        own_key = kv[j][:, :BLOCK].astype(F32)
        rolled[j][:BLOCK] = roll_half(own_key[:BLOCK]).astype(BF16)
        rolled[j][3 * BLOCK :] = roll_half(own_key[3 * BLOCK :]).astype(BF16)
        parts = []
        for t in range(2):
            spot = middle[t]
            for m in range(per_group // 2):
                lanes = slice(2 * m * BLOCK, (2 * m + 2) * BLOCK)
                inverse, delta = sums[j, t, m]
                probs = central[j][t][:, lanes] * inverse
                probs_low[j][t][spot, lanes] = probs.astype(BF16)
                score_grad[j][t][spot, lanes] = (
                    probs * (central_grad[j][t][:, lanes] - delta)
                ).astype(BF16)
            parts.append(
                jnp.dot(score_grad[j][t][spot], qrot[j][t], preferred_element_type=F32) * inv_sqrt
            )
            window = slice(offset[t], offset[t] + SPAN)
            keys = jnp.concatenate([kv[j][window, :BLOCK], rolled[j][window]], axis=1)
            dq[j][t] = lax.dot_general(score_grad[j][t][...], keys, TN, preferred_element_type=F32)
        join(j, 0, parts)
        for t in range(2):
            dk_all[j, (1 + t) * BLOCK : (2 + t) * BLOCK] = dkv[j][t, :, :BLOCK]
        key, grad = own_key, dk_all[j]
        cosine, sine = (
            jnp.concatenate([near[:BLOCK], own[odd], own[1 - odd], near[BLOCK:]], axis=0)
            for near, own in ((near_cos, cosn), (near_sin, sinn))
        )
        product = (grad * cosine - roll_half(grad) * sine) * (
            key * cosine - rolled[j][...].astype(F32) * sine
        )
        k_term = k_term + fold_rows(product)

    for j in range(share):
        for s in range(2):
            t = slot_of[s]
            cos_back, sin_back = cosn[s] * inv_sqrt, sinn[s] * inv_sqrt
            for h in range(per_group):
                lanes = slice(h * BLOCK, (h + 1) * BLOCK)
                grad = dq[j][t, lanes, :BLOCK]
                turned = grad * cos_back - dq[j][t, lanes, BLOCK:] * sin_back
                unit = q_in[j][s, :, lanes].astype(F32) * qinv[j][t, :, lanes]
                product = turned * unit
                q_term = q_term + fold_rows(product)
                q_turned[j][s, :, lanes] = turned
                q_unit[j][s, :, lanes] = unit

    term_dp[dp, 0:1] = jnp.sum(q_term, axis=0, keepdims=True)
    term_dp[dp, 1:2] = jnp.sum(k_term, axis=0, keepdims=True) / k_gain

    def ctx_copy(step):
        peer = lax.rem(me + step, n)
        return remote(term_ctx.at[me], term_ctx.at[me], tc_s.at[step], tc_r.at[step], (dp, peer))

    def dp_copy(step):
        peer = lax.rem(dp + step, n_dp)
        return remote(term_dp.at[dp], term_dp.at[dp], td_s.at[step], td_r.at[step], (peer, me))

    ctx_copies = [ctx_copy(step) for step in range(1, n)]
    dp_copies = [dp_copy(step) for step in range(1, n_dp)]
    for copy in dp_copies:
        copy.start()

    for j in range(share):
        for s in (1, 0):
            for h in range(per_group):
                lanes = slice(h * BLOCK, (h + 1) * BLOCK)
                turned, unit = q_turned[j][s, :, lanes], q_unit[j][s, :, lanes]
                weighted = turned * q_gain
                mean = lane_sums(weighted * unit, ones) * (1.0 / BLOCK)
                result = (qinv[j][slot_of[s], :, lanes] * (weighted - unit * mean)).astype(BF16)
                if s == 0:
                    qgrad_ref[mine, :, j * wide + h * BLOCK : j * wide + (h + 1) * BLOCK] = result
                else:
                    q_out[j][:, lanes] = result
            if s == 1:
                q_home[j].start()
    for j in range(share):
        parts = [
            jnp.dot(
                probs_low[j][t][middle[t]],
                stacked(do_in[j][slot_of[t]]),
                preferred_element_type=F32,
            )
            for t in range(2)
        ]
        join(j, 1, parts)

    for copy in dp_copies:
        copy.wait_recv()
    term_ctx[me, 0:2] = jnp.sum(term_dp[:, 0:2], axis=0)
    for copy in ctx_copies:
        copy.start()

    for j in range(share):

        @pl.when(has_next)
        def _():
            home_prev[j].wait_recv()

        @pl.when(has_prev)
        def _():
            home_next[j].wait_recv()

        lanes = slice(j * BLOCK, (j + 1) * BLOCK)
        for s in (1, 0):
            t = slot_of[s]
            cosine, sine = cosn[s], sinn[s]
            total = dkv[j][t] + arrived[j][t].astype(F32)
            grad = total[:, :BLOCK]
            x = k_raw[s, :, lanes].astype(F32)
            inv = lax.rsqrt(lane_sums(x * x, ones) * (1.0 / BLOCK) + norm_eps)
            unit = x * inv
            turned = grad * cosine - roll_half(grad) * sine
            mean = lane_sums(turned * unit * k_gain, ones) * (1.0 / BLOCK)
            result = (inv * (turned * k_gain - unit * mean)).astype(BF16)
            if s == 0:
                kgrad_ref[mine, :, lanes] = result
                vgrad_ref[mine, :, lanes] = total[:, BLOCK:].astype(BF16)
            else:
                k_out[:, lanes] = result
                v_out[:, lanes] = total[:, BLOCK:].astype(BF16)
    k_home.start()
    v_home.start()

    ids_swap.wait_send()
    k_swap.wait_send()
    v_swap.wait_send()
    for j in range(share):
        q_swap[j].wait_send()
        do_swap[j].wait_send()
        q_home[j].wait_recv()
        q_home[j].wait_send()

        @pl.when(has_next)
        def _():
            to_next[j].wait_send()
            home_next[j].wait_send()

        @pl.when(has_prev)
        def _():
            to_prev[j].wait_send()
            home_prev[j].wait_send()

    @pl.when(has_next)
    def _():
        for other in range(2):
            near_copy(0, other, core).wait_send()

    @pl.when(has_prev)
    def _():
        for other in range(2):
            near_copy(1, other, core).wait_send()

    for copy in dp_copies:
        copy.wait_send()
    k_home.wait_recv()
    v_home.wait_recv()
    k_home.wait_send()
    v_home.wait_send()
    for copy in ctx_copies:
        copy.wait_recv()
    totals = jnp.sum(term_ctx[:, 0:2], axis=0)
    token_count = n_dp * n * BLOCK
    qgain_ref[...] = totals[0:1] * (1.0 / math.sqrt(token_count * groups * per_group))
    kgain_ref[...] = totals[1:2] * (1.0 / math.sqrt(token_count * groups))
    for copy in ctx_copies:
        copy.wait_send()


def hand_over(*refs):
    sources, targets, sems = refs[:5], refs[5:10], refs[10]
    copies = []
    for source, target in zip(sources, targets):
        if len(source.shape) == 2:
            copies.append((source, target))
        else:
            width = source.shape[2]
            for half in range(2):
                lanes = slice(half * width, (half + 1) * width)
                copies.append((source.at[half], target.at[0, :, lanes]))
    copies = [
        pltpu.make_async_copy(source, target, sems.at[i])
        for i, (source, target) in enumerate(copies)
    ]
    for copy in copies:
        copy.start()
    for copy in copies:
        copy.wait()


def shards(
    q_proj,
    k_proj,
    v_proj,
    out_grad,
    q_gain,
    k_gain,
    pos_ids,
    stretch_lengths,
    stretch_windows,
    clip_ids,
    dispatch_plan,
):
    n = lax.axis_size("ctx")
    n_dp = lax.axis_size("dp")
    groups = k_proj.shape[2] // BLOCK
    heads = q_proj.shape[2] // BLOCK
    per_group = heads // groups
    share = groups // 2
    wide = per_group * BLOCK
    hbm = pl.BlockSpec(memory_space=pl.ANY)
    vmem = pl.BlockSpec(memory_space=pltpu.VMEM)
    dma = pltpu.SemaphoreType.DMA
    count = stretch_lengths.shape[1]
    nat = 3 * BLOCK + HALF
    central = (SPAN - BLOCK, 2 * BLOCK)
    out = pl.pallas_call(
        functools.partial(kernel, n, n_dp, groups, per_group),
        out_shape=(
            pltpu.VMEM((2, BLOCK, share * wide), BF16),
            pltpu.VMEM((2, BLOCK, share * BLOCK), BF16),
            pltpu.VMEM((2, BLOCK, share * BLOCK), BF16),
            pltpu.VMEM((1, BLOCK), F32),
            pltpu.VMEM((1, BLOCK), F32),
        ),
        in_specs=[hbm] * 11,
        out_specs=(vmem,) * 5,
        scratch_shapes=[
            pltpu.SMEM(dispatch_plan.shape, jnp.int32),
            pltpu.VMEM((1, BLOCK), F32),
            pltpu.VMEM((1, BLOCK), F32),
            pltpu.VMEM((2, 3, 1, BLOCK), jnp.int32),
            pltpu.VMEM((2, 2, 3, 1, BLOCK), jnp.int32),
            pltpu.VMEM((1, count), jnp.int32),
            pltpu.VMEM((1, count), jnp.int32),
            pltpu.VMEM((1, count), jnp.int32),
            pltpu.VMEM((2, BLOCK, share * BLOCK), BF16),
            pltpu.VMEM((2, BLOCK, share * BLOCK), BF16),
            pltpu.VMEM((2, BLOCK, BLOCK), F32),
            pltpu.VMEM((2, BLOCK, BLOCK), F32),
            pltpu.VMEM((BLOCK + HALF, BLOCK), F32),
            pltpu.VMEM((BLOCK + HALF, BLOCK), F32),
            pltpu.VMEM((2, SPAN, BLOCK), F32),
            pltpu.VMEM((share, nat, BLOCK), F32),
            pltpu.VMEM((BLOCK, share * BLOCK), BF16),
            pltpu.VMEM((BLOCK, share * BLOCK), BF16),
            pltpu.VMEM((n, 8, BLOCK), F32),
            pltpu.VMEM((n_dp, 8, BLOCK), F32),
        ]
        + [pltpu.VMEM((2, BLOCK, wide), BF16)] * (2 * share)
        + [pltpu.VMEM((nat, 2 * BLOCK), BF16)] * share
        + [pltpu.VMEM((nat, BLOCK), BF16)] * share
        + [pltpu.VMEM((2, wide, BLOCK), BF16)] * share
        + [pltpu.VMEM((2, BLOCK, wide), F32)] * share
        + [pltpu.VMEM((rows, wide), F32) for rows in central] * (2 * share)
        + [pltpu.VMEM((SPAN, wide), BF16)] * (4 * share)
        + [pltpu.VMEM((2, BLOCK, 2 * BLOCK), F32)] * share
        + [pltpu.VMEM((2, wide, 2 * BLOCK), F32)] * share
        + [pltpu.VMEM((BLOCK, 2 * BLOCK), BF16)] * share
        + [pltpu.VMEM((HALF, 2 * BLOCK), BF16)] * share
        + [pltpu.VMEM((2, BLOCK, 2 * BLOCK), BF16)] * share
        + [pltpu.VMEM((BLOCK, wide), BF16)] * share
        + [pltpu.VMEM((2, BLOCK, wide), F32)] * (2 * share)
        + [
            dma((9 + 2 * share,)),
            dma((5 + 7 * share,)),
            dma((5 + 7 * share,)),
            dma((2, 2)),
            dma((2, 2)),
            dma((n,)),
            dma((n,)),
            dma((n_dp,)),
            dma((n_dp,)),
        ],
        compiler_params=pltpu.CompilerParams(
            collective_id=0, has_side_effects=True, vmem_limit_bytes=VMEM_LIMIT
        ),
        cost_estimate=pl.CostEstimate(
            flops=10 * heads * BLOCK * SPAN * BLOCK,
            bytes_accessed=6 * BLOCK * heads * BLOCK,
            transcendentals=heads * BLOCK * SPAN,
        ),
    )(
        *[
            pltpu.with_memory_space_constraint(array, pltpu.HBM)
            for array in (
                dispatch_plan,
                k_proj,
                v_proj,
                q_gain.reshape(1, BLOCK),
                k_gain.reshape(1, BLOCK),
                pos_ids.transpose(1, 0, 2),
                stretch_lengths,
                stretch_windows,
                clip_ids,
                q_proj,
                out_grad,
            )
        ]
    )
    out = pl.pallas_call(
        hand_over,
        out_shape=(
            pltpu.HBM(q_proj.shape, BF16),
            pltpu.HBM(k_proj.shape, BF16),
            pltpu.HBM(v_proj.shape, BF16),
            pltpu.HBM((1, BLOCK), F32),
            pltpu.HBM((1, BLOCK), F32),
        ),
        in_specs=[hbm] * 5,
        out_specs=(pl.BlockSpec(memory_space=pltpu.HBM),) * 5,
        scratch_shapes=[dma((8,))],
    )(*[pltpu.with_memory_space_constraint(array, pltpu.VMEM) for array in out])
    return (out[0], out[1], out[2], out[3].reshape(BLOCK), out[4].reshape(BLOCK))


def solution(mesh):
    row = P("dp", "ctx", None)
    table = P("dp", None)
    return jax.shard_map(
        shards,
        mesh=mesh,
        in_specs=(row, row, row, row, P(), P(), P("dp", None, "ctx"), table, table, table, table),
        out_specs=(row, row, row, P(), P()),
        check_vma=False,
    )
```

```python
import functools
import math

import jax
import jax.numpy as jnp
from jax import lax
from jax.experimental import pallas as pl
from jax.experimental.pallas import tpu as pltpu
from jax.sharding import PartitionSpec as P

MESH = pl.DeviceIdType.MESH
F32 = jnp.float32
BF16 = jnp.bfloat16
BLOCK = 128
HALF = BLOCK // 2
SPAN = 2 * BLOCK + HALF
norm_eps = 1e-06
VMEM_LIMIT = 40 * 1024 * 1024
rope_base = 10000.0

NT = (((1,), (1,)), ((), ()))
TN = (((0,), (0,)), ((), ()))


def sin_cos(angle):
    turns = jnp.floor(angle * (2.0 / math.pi) + 0.5)
    rest = angle - turns * 1.5703125
    rest = rest - turns * 4.837512969970703125e-4
    rest = rest - turns * 7.549789948768648e-8
    square = rest * rest
    sine = rest + rest * square * (
        -1.6666654611e-1 + square * (8.3321608736e-3 + square * -1.9515295891e-4)
    )
    cosine = (
        1.0
        - 0.5 * square
        + square
        * square
        * (4.166664568298827e-2 + square * (-1.388731625493765e-3 + square * 2.443315711809948e-5))
    )
    quarter = turns.astype(jnp.int32)
    odd = (quarter & 1) == 1
    sine_out = jnp.where(odd, cosine, sine)
    cosine_out = jnp.where(odd, sine, cosine)
    sine_out = jnp.where((quarter & 2) == 2, -sine_out, sine_out)
    cosine_out = jnp.where(((quarter + 1) & 2) == 2, -cosine_out, cosine_out)
    return sine_out, cosine_out


def roll_half(x):
    return pltpu.roll(x, HALF, 1)


def rope_tables(ids):
    rows = lax.broadcasted_iota(jnp.int32, (BLOCK, BLOCK), 0)
    lanes = lax.broadcasted_iota(jnp.int32, (BLOCK, BLOCK), 1)
    columns = [
        jnp.sum(jnp.where(rows == lanes, ids[t].astype(F32), 0.0), axis=1, keepdims=True)
        for t in range(3)
    ]
    pair = lanes % HALF
    chosen = jnp.where(pair < 16, columns[0], jnp.where(pair < 40, columns[1], columns[2]))
    pair_row = lax.broadcasted_iota(jnp.int32, (1, BLOCK), 1) % HALF
    frequency = jnp.exp(pair_row.astype(F32) * (-math.log(rope_base) / HALF))
    sine, cosine = sin_cos(chosen * frequency)
    return cosine, jnp.where(lanes < HALF, -sine, sine)


def key_ranges(lengths, windows, clips, start):
    count = lengths.shape[1]
    rows = lax.broadcasted_iota(jnp.int32, (count, count), 0)
    lanes = lax.broadcasted_iota(jnp.int32, (count, count), 1)

    def column(where_, values):
        return jnp.sum(jnp.where(where_, values.astype(F32), 0.0), axis=1, keepdims=True)

    ends = column(lanes <= rows, lengths)
    starts = column(lanes < rows, lengths)
    before = column(lanes == rows - 1, lengths)
    window = column(lanes == rows, windows)
    clip = column(lanes == rows, clips + 1)
    clip_before = column(lanes == rows - 1, clips + 1)
    low = starts - jnp.where(clip == clip_before, window * before, 0.0)
    spots = (start + lax.broadcasted_iota(jnp.int32, (count, BLOCK), 1)).astype(F32)
    inside = (starts <= spots) & (spots < ends)
    low_row = jnp.sum(jnp.where(inside, low, 0.0), axis=0, keepdims=True)
    high_row = jnp.sum(jnp.where(inside, ends, 0.0), axis=0, keepdims=True)
    return low_row, high_row


def lane_sums(x, ones):
    high = x.astype(BF16)
    low = (x - high.astype(F32)).astype(BF16)
    return jnp.dot(jnp.concatenate([high, low], axis=1), ones, preferred_element_type=F32)


def fold_rows(x):
    return jnp.sum(x.reshape(x.shape[0] // 8, 8, x.shape[1]), axis=0)


def kernel(n, n_dp, groups, per_group, *refs):
    share = groups // 2
    wide = per_group * BLOCK
    refs = iter(refs)

    def take(count):
        return [next(refs) for _ in range(count)]

    (
        plan_hbm,
        k_hbm,
        v_hbm,
        qg_hbm,
        kg_hbm,
        ids_hbm,
        len_hbm,
        win_hbm,
        clip_hbm,
        q_hbm,
        do_hbm,
    ) = take(11)
    qgrad_ref, kgrad_ref, vgrad_ref, qgain_ref, kgain_ref = take(5)
    plan_ref, qg_ref, kg_ref, ids, near_ids, len_ref, win_ref, clip_ref = take(8)
    k_raw, v_raw, cosn, sinn, near_cos, near_sin, bias_ref, dk_all = take(8)
    k_out, v_out, term_ctx, term_dp = take(4)
    q_in = take(share)
    do_in = take(share)
    kv = take(share)
    rolled = take(share)
    qrot = take(share)
    qinv = take(share)
    central = [take(2) for _ in range(share)]
    central_grad = [take(2) for _ in range(share)]
    probs_low = [take(2) for _ in range(share)]
    score_grad = [take(2) for _ in range(share)]
    dkv = take(share)
    dq = take(share)
    back_prev = take(share)
    back_next = take(share)
    arrived = take(share)
    q_out = take(share)
    q_turned = take(share)
    q_unit = take(share)
    load_sem, sent, got, near_s, near_r, tc_s, tc_r, td_s, td_r = take(9)

    me = lax.axis_index("ctx")
    dp = lax.axis_index("dp")
    core = lax.rem(me, 2)
    pair = me // 2
    partner = me + 1 - 2 * core
    has_prev = me >= 2
    has_next = me < n - 2
    inv_sqrt = BLOCK ** (-0.5)

    def columns(which, width, j=0):
        return pl.ds(pl.multiple_of(which * (share * width) + j * width, BLOCK), width)

    mine, theirs = core, 1 - core
    both_k = pl.ds(pl.multiple_of(mine * (share * BLOCK), BLOCK), share * BLOCK)
    their_k = pl.ds(pl.multiple_of(theirs * (share * BLOCK), BLOCK), share * BLOCK)
    moves = [
        (plan_hbm, plan_ref),
        (ids_hbm, ids.at[0]),
        (qg_hbm, qg_ref),
        (kg_hbm, kg_ref),
        (k_hbm.at[0, :, both_k], k_raw.at[0]),
        (v_hbm.at[0, :, both_k], v_raw.at[0]),
        (len_hbm, len_ref),
        (win_hbm, win_ref),
        (clip_hbm, clip_ref),
    ]
    for j in range(share):
        moves.append((q_hbm.at[0, :, columns(mine, wide, j)], q_in[j].at[0]))
        moves.append((do_hbm.at[0, :, columns(mine, wide, j)], do_in[j].at[0]))
    loads = [
        pltpu.make_async_copy(source, target, load_sem.at[i])
        for i, (source, target) in enumerate(moves)
    ]

    barrier = pltpu.get_barrier_semaphore()
    pl.semaphore_signal(barrier, inc=1, device_id=(dp, partner), device_id_type=MESH)

    def greet_ctx(step, carry):
        peer = lax.rem(partner + step, n)

        @pl.when(peer != me)
        def _():
            pl.semaphore_signal(barrier, inc=1, device_id=(dp, peer), device_id_type=MESH)

        return carry

    def greet_dp(step, carry):
        peer = lax.rem(dp + step, n_dp)
        pl.semaphore_signal(barrier, inc=1, device_id=(peer, me), device_id_type=MESH)
        pl.semaphore_signal(barrier, inc=1, device_id=(peer, partner), device_id_type=MESH)
        return carry

    lax.fori_loop(1, n, greet_ctx, 0)
    lax.fori_loop(1, n_dp, greet_dp, 0)
    for load in loads:
        load.start()

    @pl.when(jnp.logical_not(has_prev))
    def _():
        near_ids[0] = jnp.zeros_like(near_ids[0])
        for j in range(share):
            kv[j][:BLOCK] = jnp.zeros((BLOCK, 2 * BLOCK), BF16)
            arrived[j][0, :HALF] = jnp.zeros((HALF, 2 * BLOCK), BF16)

    @pl.when(jnp.logical_not(has_next))
    def _():
        near_ids[1] = jnp.zeros_like(near_ids[1])
        for j in range(share):
            kv[j][3 * BLOCK :] = jnp.zeros((HALF, 2 * BLOCK), BF16)
            arrived[j][1] = jnp.zeros((BLOCK, 2 * BLOCK), BF16)

    for j in range(share):
        arrived[j][0, HALF:] = jnp.zeros((HALF, 2 * BLOCK), BF16)

    def remote(source, target, send, receive, peer):
        return pltpu.make_async_remote_copy(
            src_ref=source,
            dst_ref=target,
            send_sem=send,
            recv_sem=receive,
            device_id=peer,
            device_id_type=MESH,
        )

    count = [0]

    def numbered(source, target, peer):
        i = count[0]
        count[0] += 1
        return remote(source, target, sent.at[i], got.at[i], (dp, peer))

    k_swap = numbered(k_hbm.at[0, :, their_k], k_raw.at[1], partner)
    v_swap = numbered(v_hbm.at[0, :, their_k], v_raw.at[1], partner)
    ids_swap = numbered(ids_hbm, ids.at[1], partner)
    q_swap = [
        numbered(q_hbm.at[0, :, columns(theirs, wide, j)], q_in[j].at[1], partner)
        for j in range(share)
    ]
    do_swap = [
        numbered(do_hbm.at[0, :, columns(theirs, wide, j)], do_in[j].at[1], partner)
        for j in range(share)
    ]
    to_next = [
        numbered(kv[j].at[2 * BLOCK : 3 * BLOCK], kv[j].at[:BLOCK], me + 2) for j in range(share)
    ]
    to_prev = [
        numbered(kv[j].at[BLOCK : BLOCK + HALF], kv[j].at[3 * BLOCK :], me - 2)
        for j in range(share)
    ]
    home_prev = [numbered(back_prev[j], arrived[j].at[1], me - 2) for j in range(share)]
    home_next = [numbered(back_next[j], arrived[j].at[0, :HALF], me + 2) for j in range(share)]
    q_home = [
        numbered(q_out[j], qgrad_ref.at[mine, :, j * wide : (j + 1) * wide], partner)
        for j in range(share)
    ]
    k_home = numbered(k_out, kgrad_ref.at[mine], partner)
    v_home = numbered(v_out, vgrad_ref.at[mine], partner)

    def near_copy(side, other, sender):
        peer = 2 * pair + other + (2 if side == 0 else -2)
        return remote(
            ids_hbm,
            near_ids.at[side, sender],
            near_s.at[side, other],
            near_r.at[side, sender],
            (dp, peer),
        )

    pl.semaphore_wait(barrier, n - 1 + 2 * (n_dp - 1))
    ids_swap.start()
    k_swap.start()
    v_swap.start()
    for j in range(share):
        q_swap[j].start()
        do_swap[j].start()

    @pl.when(has_next)
    def _():
        for other in range(2):
            near_copy(0, other, core).start()

    @pl.when(has_prev)
    def _():
        for other in range(2):
            near_copy(1, other, core).start()

    for load in loads[:9]:
        load.wait()
    odd = lax.rem(plan_ref[0, me], 2)
    slot_of = (odd, 1 - odd)
    q_gain, k_gain = qg_ref[...], kg_ref[...]
    ones = jnp.ones((2 * BLOCK, BLOCK), BF16)

    for s in range(2):
        if s == 1:
            ids_swap.wait_recv()
        cosine, sine = rope_tables([ids[s, i] for i in range(3)])
        cosn[s] = cosine
        sinn[s] = sine

    def table(t):
        return cosn[slot_of[t]], sinn[slot_of[t]]

    rolled_k_gain, rolled_q_gain = roll_half(k_gain), roll_half(q_gain)
    k_swap.wait_recv()
    v_swap.wait_recv()
    for j in range(share):
        lanes = slice(j * BLOCK, (j + 1) * BLOCK)
        for t in range(2):
            cosine, sine = table(t)
            x = k_raw[slot_of[t], :, lanes].astype(F32)
            inv = lax.rsqrt(lane_sums(x * x, ones) * (1.0 / BLOCK) + norm_eps)
            turned = inv * (x * (cosine * k_gain) + roll_half(x) * (sine * rolled_k_gain))
            spot = slice((1 + t) * BLOCK, (2 + t) * BLOCK)
            kv[j][spot, :BLOCK] = turned.astype(BF16)
            kv[j][spot, BLOCK:] = v_raw[slot_of[t], :, lanes]
            rolled[j][spot] = roll_half(turned).astype(BF16)

        @pl.when(has_prev)
        def _():
            to_prev[j].start()

        @pl.when(has_next)
        def _():
            to_next[j].start()

    for t in range(2):
        start = (2 * pair + t) * BLOCK
        low_row, high_row = key_ranges(len_ref[...], win_ref[...], clip_ref[...], start)
        spots = (start - BLOCK + lax.broadcasted_iota(jnp.int32, (SPAN, BLOCK), 0)).astype(F32)
        bias_ref[t] = jnp.where((spots >= low_row) & (spots < high_row), 0.0, -1e30)

    def heads(value, m):
        return jnp.concatenate(
            [
                value[:, 2 * m * BLOCK : (2 * m + 1) * BLOCK],
                value[:, (2 * m + 1) * BLOCK : (2 * m + 2) * BLOCK],
            ],
            axis=0,
        )

    def stacked(value):
        return jnp.concatenate(
            [value[:, h * BLOCK : (h + 1) * BLOCK] for h in range(per_group)], axis=0
        )

    scale = inv_sqrt * math.log2(math.e)
    middle = (slice(BLOCK, SPAN), slice(0, 2 * BLOCK))
    edge = (slice(0, BLOCK), slice(2 * BLOCK, SPAN))
    offset = (0, BLOCK)

    def shifted(spot, t):
        return slice(spot.start + offset[t], spot.stop + offset[t])

    def scored(j, t, spot, m, cot):
        key = kv[j][shifted(spot, t), :BLOCK]
        value = kv[j][shifted(spot, t), BLOCK:]
        query = qrot[j][t, 2 * m * BLOCK : (2 * m + 2) * BLOCK, :]
        scores = lax.dot_general(key, query, NT, preferred_element_type=F32)
        grad = lax.dot_general(value, cot, NT, preferred_element_type=F32)
        bias = bias_ref[t, spot]
        weights = jnp.exp2(scores * scale + jnp.concatenate([bias, bias], axis=1))
        return weights, grad

    sums = {}
    for j in range(share):
        loads[9 + 2 * j].wait()
        loads[10 + 2 * j].wait()
        q_swap[j].wait_recv()
        do_swap[j].wait_recv()
        for t in range(2):
            cosine, sine = table(t)
            qc, qs = cosine * q_gain, sine * rolled_q_gain
            for h in range(per_group):
                lanes = slice(h * BLOCK, (h + 1) * BLOCK)
                x = q_in[j][slot_of[t], :, lanes].astype(F32)
                inv = lax.rsqrt(lane_sums(x * x, ones) * (1.0 / BLOCK) + norm_eps)
                qinv[j][t, :, lanes] = inv
                qrot[j][t, lanes, :] = (inv * (x * qc + roll_half(x) * qs)).astype(BF16)
            for m in range(per_group // 2):
                lanes = slice(2 * m * BLOCK, (2 * m + 2) * BLOCK)
                cot = heads(do_in[j][slot_of[t]], m)
                weights, grad = scored(j, t, middle[t], m, cot)
                central[j][t][:, lanes] = weights
                central_grad[j][t][:, lanes] = grad
                sums[j, t, m] = (
                    jnp.sum(weights, axis=0, keepdims=True),
                    jnp.sum(weights * grad, axis=0, keepdims=True),
                )

    @pl.when(has_prev)
    def _():
        for sender in range(2):
            near_copy(0, sender, sender).wait_recv()

    @pl.when(has_next)
    def _():
        for sender in range(2):
            near_copy(1, sender, sender).wait_recv()

    before = 1 - lax.rem(plan_ref[0, lax.max(2 * pair - 2, 0)], 2)
    after = lax.rem(plan_ref[0, lax.min(2 * pair + 2, n - 2)], 2)
    cosine, sine = rope_tables([near_ids[0, before, i] for i in range(3)])
    near_cos[:BLOCK] = cosine
    near_sin[:BLOCK] = sine
    cosine, sine = rope_tables([near_ids[1, after, i] for i in range(3)])
    near_cos[BLOCK:] = cosine[:HALF]
    near_sin[BLOCK:] = sine[:HALF]

    def join(j, i, parts):
        even, late = parts
        lanes = slice(i * BLOCK, (i + 1) * BLOCK)
        dkv[j][0, :, lanes] = even[:BLOCK] + late[:BLOCK]
        dkv[j][1, :HALF, lanes] = even[BLOCK:] + late[BLOCK : BLOCK + HALF]
        dkv[j][1, HALF:, lanes] = late[BLOCK + HALF :]

    q_term = jnp.zeros((8, BLOCK), F32)
    k_term = jnp.zeros((8, BLOCK), F32)
    for j in range(share):

        @pl.when(has_prev)
        def _():
            to_next[j].wait_recv()

        @pl.when(has_next)
        def _():
            to_prev[j].wait_recv()

        if j > 0:

            @pl.when(has_prev)
            def _():
                home_prev[j - 1].start()

            @pl.when(has_next)
            def _():
                home_next[j - 1].start()

        for t in range(2):
            spot = edge[t]
            for m in range(per_group // 2):
                lanes = slice(2 * m * BLOCK, (2 * m + 2) * BLOCK)
                cot = heads(do_in[j][slot_of[t]], m)
                weights, grad = scored(j, t, spot, m, cot)
                total, delta = sums[j, t, m]
                inverse = 1.0 / (total + jnp.sum(weights, axis=0, keepdims=True))
                delta = (delta + jnp.sum(weights * grad, axis=0, keepdims=True)) * inverse
                sums[j, t, m] = (inverse, delta)
                probs = weights * inverse
                probs_low[j][t][spot, lanes] = probs.astype(BF16)
                score_grad[j][t][spot, lanes] = (probs * (grad - delta)).astype(BF16)
            key_grad = (
                jnp.dot(score_grad[j][t][spot], qrot[j][t], preferred_element_type=F32) * inv_sqrt
            )
            value_grad = jnp.dot(
                probs_low[j][t][spot],
                stacked(do_in[j][slot_of[t]]),
                preferred_element_type=F32,
            )
            dk_all[j, shifted(spot, t)] = key_grad
            back = (back_prev, back_next)[t][j]
            back[:, :BLOCK] = key_grad.astype(BF16)
            back[:, BLOCK:] = value_grad.astype(BF16)


        own_key = kv[j][:, :BLOCK].astype(F32)
        rolled[j][:BLOCK] = roll_half(own_key[:BLOCK]).astype(BF16)
        rolled[j][3 * BLOCK :] = roll_half(own_key[3 * BLOCK :]).astype(BF16)
        parts = []
        for t in range(2):
            spot = middle[t]
            for m in range(per_group // 2):
                lanes = slice(2 * m * BLOCK, (2 * m + 2) * BLOCK)
                inverse, delta = sums[j, t, m]
                probs = central[j][t][:, lanes] * inverse
                probs_low[j][t][spot, lanes] = probs.astype(BF16)
                score_grad[j][t][spot, lanes] = (
                    probs * (central_grad[j][t][:, lanes] - delta)
                ).astype(BF16)
            parts.append(
                jnp.dot(score_grad[j][t][spot], qrot[j][t], preferred_element_type=F32) * inv_sqrt
            )
            window = slice(offset[t], offset[t] + SPAN)
            keys = jnp.concatenate([kv[j][window, :BLOCK], rolled[j][window]], axis=1)
            dq[j][t] = lax.dot_general(score_grad[j][t][...], keys, TN, preferred_element_type=F32)
        join(j, 0, parts)
        for t in range(2):
            dk_all[j, (1 + t) * BLOCK : (2 + t) * BLOCK] = dkv[j][t, :, :BLOCK]
        key, grad = own_key, dk_all[j]
        cosine, sine = (
            jnp.concatenate([near[:BLOCK], own[odd], own[1 - odd], near[BLOCK:]], axis=0)
            for near, own in ((near_cos, cosn), (near_sin, sinn))
        )
        product = (grad * cosine - roll_half(grad) * sine) * (
            key * cosine - rolled[j][...].astype(F32) * sine
        )
        k_term = k_term + fold_rows(product)

    for j in range(share):
        for s in range(2):
            t = slot_of[s]
            cos_back, sin_back = cosn[s] * inv_sqrt, sinn[s] * inv_sqrt
            for h in range(per_group):
                lanes = slice(h * BLOCK, (h + 1) * BLOCK)
                grad = dq[j][t, lanes, :BLOCK]
                turned = grad * cos_back - dq[j][t, lanes, BLOCK:] * sin_back
                unit = q_in[j][s, :, lanes].astype(F32) * qinv[j][t, :, lanes]
                product = turned * unit
                q_term = q_term + fold_rows(product)
                q_turned[j][s, :, lanes] = turned
                q_unit[j][s, :, lanes] = unit

    term_dp[core, dp, 0:1] = jnp.sum(q_term, axis=0, keepdims=True)
    term_dp[core, dp, 1:2] = jnp.sum(k_term, axis=0, keepdims=True) / k_gain

    gathers = core == 1
    outer = 2 * pair + 1

    def dp_copy(step, sender):
        peer = lax.rem(dp + step, n_dp)
        mine_spot = (core, dp)
        return remote(
            term_dp.at[mine_spot],
            term_dp.at[mine_spot],
            td_s.at[step],
            td_r.at[sender, step],
            (peer, outer),
        )

    def ctx_copy(step, side):
        peer = 2 * lax.rem(pair + step, n // 2) + side
        return remote(
            term_ctx.at[pair], term_ctx.at[pair], tc_s.at[step, side], tc_r.at[step], (dp, peer)
        )

    for step in range(1, n_dp):
        dp_copy(step, core).start()

    @pl.when(jnp.logical_not(gathers))
    def _():
        dp_copy(0, 0).start()

    @pl.when(has_prev)
    def _():
        home_prev[share - 1].start()

    @pl.when(has_next)
    def _():
        home_next[share - 1].start()

    for j in range(share):
        for s in (1, 0):
            for h in range(per_group):
                lanes = slice(h * BLOCK, (h + 1) * BLOCK)
                turned, unit = q_turned[j][s, :, lanes], q_unit[j][s, :, lanes]
                weighted = turned * q_gain
                mean = lane_sums(weighted * unit, ones) * (1.0 / BLOCK)
                result = (qinv[j][slot_of[s], :, lanes] * (weighted - unit * mean)).astype(BF16)
                if s == 0:
                    qgrad_ref[mine, :, j * wide + h * BLOCK : j * wide + (h + 1) * BLOCK] = result
                else:
                    q_out[j][:, lanes] = result
            if s == 1:
                q_home[j].start()
    for j in range(share):
        parts = [
            jnp.dot(
                probs_low[j][t][middle[t]],
                stacked(do_in[j][slot_of[t]]),
                preferred_element_type=F32,
            )
            for t in range(2)
        ]
        join(j, 1, parts)

    @pl.when(gathers)
    def _():
        for step in range(n_dp):
            dp_copy(step, 0).wait_recv()
        for step in range(1, n_dp):
            dp_copy(step, 1).wait_recv()
        term_ctx[pair, 0:2] = jnp.sum(jnp.sum(term_dp[:, :, 0:2], axis=0), axis=0)
        for step in range(1, n // 2):
            ctx_copy(step, 0).start()
            ctx_copy(step, 1).start()
        ctx_copy(0, 0).start()

    for j in range(share):

        @pl.when(has_next)
        def _():
            home_prev[j].wait_recv()

        @pl.when(has_prev)
        def _():
            home_next[j].wait_recv()

        lanes = slice(j * BLOCK, (j + 1) * BLOCK)
        for s in (1, 0):
            t = slot_of[s]
            cosine, sine = cosn[s], sinn[s]
            total = dkv[j][t] + arrived[j][t].astype(F32)
            grad = total[:, :BLOCK]
            x = k_raw[s, :, lanes].astype(F32)
            inv = lax.rsqrt(lane_sums(x * x, ones) * (1.0 / BLOCK) + norm_eps)
            unit = x * inv
            turned = grad * cosine - roll_half(grad) * sine
            mean = lane_sums(turned * unit * k_gain, ones) * (1.0 / BLOCK)
            result = (inv * (turned * k_gain - unit * mean)).astype(BF16)
            if s == 0:
                kgrad_ref[mine, :, lanes] = result
                vgrad_ref[mine, :, lanes] = total[:, BLOCK:].astype(BF16)
            else:
                k_out[:, lanes] = result
                v_out[:, lanes] = total[:, BLOCK:].astype(BF16)
    k_home.start()
    v_home.start()

    ids_swap.wait_send()
    k_swap.wait_send()
    v_swap.wait_send()
    for j in range(share):
        q_swap[j].wait_send()
        do_swap[j].wait_send()
        q_home[j].wait_recv()
        q_home[j].wait_send()

        @pl.when(has_next)
        def _():
            to_next[j].wait_send()
            home_next[j].wait_send()

        @pl.when(has_prev)
        def _():
            to_prev[j].wait_send()
            home_prev[j].wait_send()

    @pl.when(has_next)
    def _():
        for other in range(2):
            near_copy(0, other, core).wait_send()

    @pl.when(has_prev)
    def _():
        for other in range(2):
            near_copy(1, other, core).wait_send()

    for step in range(1, n_dp):
        dp_copy(step, core).wait_send()

    @pl.when(jnp.logical_not(gathers))
    def _():
        dp_copy(0, 0).wait_send()

    k_home.wait_recv()
    v_home.wait_recv()
    k_home.wait_send()
    v_home.wait_send()
    for step in range(1, n // 2):
        ctx_copy(step, core).wait_recv()

    @pl.when(jnp.logical_not(gathers))
    def _():
        ctx_copy(0, 0).wait_recv()

    totals = jnp.sum(term_ctx[:, 0:2], axis=0)
    token_count = n_dp * n * BLOCK
    qgain_ref[...] = totals[0:1] * (1.0 / math.sqrt(token_count * groups * per_group))
    kgain_ref[...] = totals[1:2] * (1.0 / math.sqrt(token_count * groups))

    @pl.when(gathers)
    def _():
        for step in range(1, n // 2):
            ctx_copy(step, 0).wait_send()
            ctx_copy(step, 1).wait_send()
        ctx_copy(0, 0).wait_send()


def hand_over(*refs):
    sources, targets, sems = refs[:5], refs[5:10], refs[10]
    copies = []
    for source, target in zip(sources, targets):
        if len(source.shape) == 2:
            copies.append((source, target))
        else:
            width = source.shape[2]
            for half in range(2):
                lanes = slice(half * width, (half + 1) * width)
                copies.append((source.at[half], target.at[0, :, lanes]))
    copies = [
        pltpu.make_async_copy(source, target, sems.at[i])
        for i, (source, target) in enumerate(copies)
    ]
    for copy in copies:
        copy.start()
    for copy in copies:
        copy.wait()


def shards(
    q_proj,
    k_proj,
    v_proj,
    out_grad,
    q_gain,
    k_gain,
    pos_ids,
    stretch_lengths,
    stretch_windows,
    clip_ids,
    dispatch_plan,
):
    n = lax.axis_size("ctx")
    n_dp = lax.axis_size("dp")
    groups = k_proj.shape[2] // BLOCK
    heads = q_proj.shape[2] // BLOCK
    per_group = heads // groups
    share = groups // 2
    wide = per_group * BLOCK
    hbm = pl.BlockSpec(memory_space=pl.ANY)
    vmem = pl.BlockSpec(memory_space=pltpu.VMEM)
    dma = pltpu.SemaphoreType.DMA
    count = stretch_lengths.shape[1]
    nat = 3 * BLOCK + HALF
    central = (SPAN - BLOCK, 2 * BLOCK)
    out = pl.pallas_call(
        functools.partial(kernel, n, n_dp, groups, per_group),
        out_shape=(
            pltpu.VMEM((2, BLOCK, share * wide), BF16),
            pltpu.VMEM((2, BLOCK, share * BLOCK), BF16),
            pltpu.VMEM((2, BLOCK, share * BLOCK), BF16),
            pltpu.VMEM((1, BLOCK), F32),
            pltpu.VMEM((1, BLOCK), F32),
        ),
        in_specs=[hbm] * 11,
        out_specs=(vmem,) * 5,
        scratch_shapes=[
            pltpu.SMEM(dispatch_plan.shape, jnp.int32),
            pltpu.VMEM((1, BLOCK), F32),
            pltpu.VMEM((1, BLOCK), F32),
            pltpu.VMEM((2, 3, 1, BLOCK), jnp.int32),
            pltpu.VMEM((2, 2, 3, 1, BLOCK), jnp.int32),
            pltpu.VMEM((1, count), jnp.int32),
            pltpu.VMEM((1, count), jnp.int32),
            pltpu.VMEM((1, count), jnp.int32),
            pltpu.VMEM((2, BLOCK, share * BLOCK), BF16),
            pltpu.VMEM((2, BLOCK, share * BLOCK), BF16),
            pltpu.VMEM((2, BLOCK, BLOCK), F32),
            pltpu.VMEM((2, BLOCK, BLOCK), F32),
            pltpu.VMEM((BLOCK + HALF, BLOCK), F32),
            pltpu.VMEM((BLOCK + HALF, BLOCK), F32),
            pltpu.VMEM((2, SPAN, BLOCK), F32),
            pltpu.VMEM((share, nat, BLOCK), F32),
            pltpu.VMEM((BLOCK, share * BLOCK), BF16),
            pltpu.VMEM((BLOCK, share * BLOCK), BF16),
            pltpu.VMEM((n // 2, 8, BLOCK), F32),
            pltpu.VMEM((2, n_dp, 8, BLOCK), F32),
        ]
        + [pltpu.VMEM((2, BLOCK, wide), BF16)] * (2 * share)
        + [pltpu.VMEM((nat, 2 * BLOCK), BF16)] * share
        + [pltpu.VMEM((nat, BLOCK), BF16)] * share
        + [pltpu.VMEM((2, wide, BLOCK), BF16)] * share
        + [pltpu.VMEM((2, BLOCK, wide), F32)] * share
        + [pltpu.VMEM((rows, wide), F32) for rows in central] * (2 * share)
        + [pltpu.VMEM((SPAN, wide), BF16)] * (4 * share)
        + [pltpu.VMEM((2, BLOCK, 2 * BLOCK), F32)] * share
        + [pltpu.VMEM((2, wide, 2 * BLOCK), F32)] * share
        + [pltpu.VMEM((BLOCK, 2 * BLOCK), BF16)] * share
        + [pltpu.VMEM((HALF, 2 * BLOCK), BF16)] * share
        + [pltpu.VMEM((2, BLOCK, 2 * BLOCK), BF16)] * share
        + [pltpu.VMEM((BLOCK, wide), BF16)] * share
        + [pltpu.VMEM((2, BLOCK, wide), F32)] * (2 * share)
        + [
            dma((9 + 2 * share,)),
            dma((5 + 7 * share,)),
            dma((5 + 7 * share,)),
            dma((2, 2)),
            dma((2, 2)),
            dma((n // 2, 2)),
            dma((n // 2,)),
            dma((n_dp,)),
            dma((2, n_dp)),
        ],
        compiler_params=pltpu.CompilerParams(
            collective_id=0, has_side_effects=True, vmem_limit_bytes=VMEM_LIMIT
        ),
        cost_estimate=pl.CostEstimate(
            flops=10 * heads * BLOCK * SPAN * BLOCK,
            bytes_accessed=6 * BLOCK * heads * BLOCK,
            transcendentals=heads * BLOCK * SPAN,
        ),
    )(
        *[
            pltpu.with_memory_space_constraint(array, pltpu.HBM)
            for array in (
                dispatch_plan,
                k_proj,
                v_proj,
                q_gain.reshape(1, BLOCK),
                k_gain.reshape(1, BLOCK),
                pos_ids.transpose(1, 0, 2),
                stretch_lengths,
                stretch_windows,
                clip_ids,
                q_proj,
                out_grad,
            )
        ]
    )
    out = pl.pallas_call(
        hand_over,
        out_shape=(
            pltpu.HBM(q_proj.shape, BF16),
            pltpu.HBM(k_proj.shape, BF16),
            pltpu.HBM(v_proj.shape, BF16),
            pltpu.HBM((1, BLOCK), F32),
            pltpu.HBM((1, BLOCK), F32),
        ),
        in_specs=[hbm] * 5,
        out_specs=(pl.BlockSpec(memory_space=pltpu.HBM),) * 5,
        scratch_shapes=[dma((8,))],
    )(*[pltpu.with_memory_space_constraint(array, pltpu.VMEM) for array in out])
    return (out[0], out[1], out[2], out[3].reshape(BLOCK), out[4].reshape(BLOCK))


def solution(mesh):
    row = P("dp", "ctx", None)
    table = P("dp", None)
    return jax.shard_map(
        shards,
        mesh=mesh,
        in_specs=(row, row, row, row, P(), P(), P("dp", None, "ctx"), table, table, table, table),
        out_specs=(row, row, row, P(), P()),
        check_vma=False,
    )
```

```python
import functools
import math

import jax
import jax.numpy as jnp
from jax import lax
from jax.experimental import pallas as pl
from jax.experimental.pallas import tpu as pltpu
from jax.sharding import PartitionSpec as P

MESH = pl.DeviceIdType.MESH
F32 = jnp.float32
BF16 = jnp.bfloat16
BLOCK = 128
HALF = BLOCK // 2
SPAN = 2 * BLOCK + HALF
norm_eps = 1e-06
VMEM_LIMIT = 40 * 1024 * 1024
rope_base = 10000.0

NT = (((1,), (1,)), ((), ()))
TN = (((0,), (0,)), ((), ()))


def sin_cos(angle):
    turns = jnp.floor(angle * (2.0 / math.pi) + 0.5)
    rest = angle - turns * 1.5703125
    rest = rest - turns * 4.837512969970703125e-4
    rest = rest - turns * 7.549789948768648e-8
    square = rest * rest
    sine = rest + rest * square * (
        -1.6666654611e-1 + square * (8.3321608736e-3 + square * -1.9515295891e-4)
    )
    cosine = (
        1.0
        - 0.5 * square
        + square
        * square
        * (4.166664568298827e-2 + square * (-1.388731625493765e-3 + square * 2.443315711809948e-5))
    )
    quarter = turns.astype(jnp.int32)
    odd = (quarter & 1) == 1
    sine_out = jnp.where(odd, cosine, sine)
    cosine_out = jnp.where(odd, sine, cosine)
    sine_out = jnp.where((quarter & 2) == 2, -sine_out, sine_out)
    cosine_out = jnp.where(((quarter + 1) & 2) == 2, -cosine_out, cosine_out)
    return sine_out, cosine_out


def roll_half(x):
    return pltpu.roll(x, HALF, 1)


def rope_tables(ids):
    rows = lax.broadcasted_iota(jnp.int32, (BLOCK, BLOCK), 0)
    lanes = lax.broadcasted_iota(jnp.int32, (BLOCK, BLOCK), 1)
    columns = [
        jnp.sum(jnp.where(rows == lanes, ids[t].astype(F32), 0.0), axis=1, keepdims=True)
        for t in range(3)
    ]
    pair = lanes % HALF
    chosen = jnp.where(pair < 16, columns[0], jnp.where(pair < 40, columns[1], columns[2]))
    pair_row = lax.broadcasted_iota(jnp.int32, (1, BLOCK), 1) % HALF
    frequency = jnp.exp(pair_row.astype(F32) * (-math.log(rope_base) / HALF))
    sine, cosine = sin_cos(chosen * frequency)
    return cosine, jnp.where(lanes < HALF, -sine, sine)


def key_ranges(lengths, windows, clips, start):
    count = lengths.shape[1]
    rows = lax.broadcasted_iota(jnp.int32, (count, count), 0)
    lanes = lax.broadcasted_iota(jnp.int32, (count, count), 1)

    def column(where_, values):
        return jnp.sum(jnp.where(where_, values.astype(F32), 0.0), axis=1, keepdims=True)

    ends = column(lanes <= rows, lengths)
    starts = column(lanes < rows, lengths)
    before = column(lanes == rows - 1, lengths)
    window = column(lanes == rows, windows)
    clip = column(lanes == rows, clips + 1)
    clip_before = column(lanes == rows - 1, clips + 1)
    low = starts - jnp.where(clip == clip_before, window * before, 0.0)
    spots = (start + lax.broadcasted_iota(jnp.int32, (count, BLOCK), 1)).astype(F32)
    inside = (starts <= spots) & (spots < ends)
    low_row = jnp.sum(jnp.where(inside, low, 0.0), axis=0, keepdims=True)
    high_row = jnp.sum(jnp.where(inside, ends, 0.0), axis=0, keepdims=True)
    return low_row, high_row


def lane_sums(x, ones):
    high = x.astype(BF16)
    low = (x - high.astype(F32)).astype(BF16)
    return jnp.dot(jnp.concatenate([high, low], axis=1), ones, preferred_element_type=F32)


def fold_rows(x):
    return jnp.sum(x.reshape(x.shape[0] // 8, 8, x.shape[1]), axis=0)


def kernel(n, n_dp, groups, per_group, *refs):
    share = groups // 2
    wide = per_group * BLOCK
    refs = iter(refs)

    def take(count):
        return [next(refs) for _ in range(count)]

    (
        plan_hbm,
        k_hbm,
        v_hbm,
        qg_hbm,
        kg_hbm,
        ids_hbm,
        len_hbm,
        win_hbm,
        clip_hbm,
        q_hbm,
        do_hbm,
    ) = take(11)
    qgrad_ref, kgrad_ref, vgrad_ref, qgain_ref, kgain_ref = take(5)
    plan_ref, qg_ref, kg_ref, ids, near_ids, len_ref, win_ref, clip_ref = take(8)
    k_raw, v_raw, cosn, sinn, near_cos, near_sin, bias_ref, dk_all = take(8)
    k_out, v_out, term_ctx, term_dp = take(4)
    q_in = take(share)
    do_in = take(share)
    kv = take(share)
    rolled = take(share)
    qrot = take(share)
    qinv = take(share)
    central = [take(2) for _ in range(share)]
    central_grad = [take(2) for _ in range(share)]
    probs_low = [take(2) for _ in range(share)]
    score_grad = [take(2) for _ in range(share)]
    dkv = take(share)
    dq = take(share)
    back_prev = take(share)
    back_next = take(share)
    arrived = take(share)
    q_out = take(share)
    q_turned = take(share)
    q_unit = take(share)
    load_sem, sent, got, near_s, near_r, tc_s, tc_r, td_s, td_r = take(9)

    me = lax.axis_index("ctx")
    dp = lax.axis_index("dp")
    core = lax.rem(me, 2)
    pair = me // 2
    partner = me + 1 - 2 * core
    has_prev = me >= 2
    has_next = me < n - 2
    inv_sqrt = BLOCK ** (-0.5)

    def columns(which, width, j=0):
        return pl.ds(pl.multiple_of(which * (share * width) + j * width, BLOCK), width)

    mine, theirs = core, 1 - core
    both_k = pl.ds(pl.multiple_of(mine * (share * BLOCK), BLOCK), share * BLOCK)
    their_k = pl.ds(pl.multiple_of(theirs * (share * BLOCK), BLOCK), share * BLOCK)
    moves = [
        (plan_hbm, plan_ref),
        (ids_hbm, ids.at[0]),
        (qg_hbm, qg_ref),
        (kg_hbm, kg_ref),
        (k_hbm.at[0, :, both_k], k_raw.at[0]),
        (v_hbm.at[0, :, both_k], v_raw.at[0]),
        (len_hbm, len_ref),
        (win_hbm, win_ref),
        (clip_hbm, clip_ref),
    ]
    for j in range(share):
        moves.append((q_hbm.at[0, :, columns(mine, wide, j)], q_in[j].at[0]))
        moves.append((do_hbm.at[0, :, columns(mine, wide, j)], do_in[j].at[0]))
    loads = [
        pltpu.make_async_copy(source, target, load_sem.at[i])
        for i, (source, target) in enumerate(moves)
    ]

    barrier = pltpu.get_barrier_semaphore()
    pl.semaphore_signal(barrier, inc=1, device_id=(dp, partner), device_id_type=MESH)

    for step in range(1, n // 2):
        for side in range(2):
            peer = (dp, 2 * lax.rem(pair + step, n // 2) + side)
            pl.semaphore_signal(barrier, inc=1, device_id=peer, device_id_type=MESH)
    for step in range(1, n_dp):
        for side in range(2):
            peer = (lax.rem(dp + step, n_dp), 2 * pair + side)
            pl.semaphore_signal(barrier, inc=1, device_id=peer, device_id_type=MESH)

    @pl.when(jnp.logical_not(has_prev))
    def _():
        near_ids[0] = jnp.zeros_like(near_ids[0])
        for j in range(share):
            kv[j][:BLOCK] = jnp.zeros((BLOCK, 2 * BLOCK), BF16)
            arrived[j][0, :HALF] = jnp.zeros((HALF, 2 * BLOCK), BF16)

    @pl.when(jnp.logical_not(has_next))
    def _():
        near_ids[1] = jnp.zeros_like(near_ids[1])
        for j in range(share):
            kv[j][3 * BLOCK :] = jnp.zeros((HALF, 2 * BLOCK), BF16)
            arrived[j][1] = jnp.zeros((BLOCK, 2 * BLOCK), BF16)

    for j in range(share):
        arrived[j][0, HALF:] = jnp.zeros((HALF, 2 * BLOCK), BF16)

    def remote(source, target, send, receive, peer):
        return pltpu.make_async_remote_copy(
            src_ref=source,
            dst_ref=target,
            send_sem=send,
            recv_sem=receive,
            device_id=peer,
            device_id_type=MESH,
        )

    count = [0]

    def numbered(source, target, peer):
        i = count[0]
        count[0] += 1
        return remote(source, target, sent.at[i], got.at[i], (dp, peer))

    k_swap = numbered(k_hbm.at[0, :, their_k], k_raw.at[1], partner)
    v_swap = numbered(v_hbm.at[0, :, their_k], v_raw.at[1], partner)
    ids_swap = numbered(ids_hbm, ids.at[1], partner)
    q_swap = [
        numbered(q_hbm.at[0, :, columns(theirs, wide, j)], q_in[j].at[1], partner)
        for j in range(share)
    ]
    do_swap = [
        numbered(do_hbm.at[0, :, columns(theirs, wide, j)], do_in[j].at[1], partner)
        for j in range(share)
    ]
    last_block, last_half = slice(2 * BLOCK, 3 * BLOCK), slice(3 * BLOCK, SPAN + BLOCK)
    first_block, first_half = slice(0, BLOCK), slice(BLOCK, BLOCK + HALF)
    pieces = [slice(0, BLOCK) if j == 0 else slice(0, 2 * BLOCK) for j in range(share)]
    values = slice(BLOCK, 2 * BLOCK)
    to_next = [
        numbered(kv[j].at[last_block, pieces[j]], kv[j].at[first_block, pieces[j]], me + 2)
        for j in range(share)
    ]
    to_prev = [
        numbered(kv[j].at[first_half, pieces[j]], kv[j].at[last_half, pieces[j]], me - 2)
        for j in range(share)
    ]
    ahead_next = numbered(kv[0].at[last_block, values], kv[0].at[first_block, values], me + 2)
    ahead_prev = numbered(kv[0].at[first_half, values], kv[0].at[last_half, values], me - 2)
    home_prev = [numbered(back_prev[j], arrived[j].at[1], me - 2) for j in range(share)]
    home_next = [numbered(back_next[j], arrived[j].at[0, :HALF], me + 2) for j in range(share)]
    q_home = [
        numbered(q_out[j], qgrad_ref.at[mine, :, j * wide : (j + 1) * wide], partner)
        for j in range(share)
    ]
    k_home = numbered(k_out, kgrad_ref.at[mine], partner)
    v_home = numbered(v_out, vgrad_ref.at[mine], partner)

    def near_copy(side, other, sender):
        peer = 2 * pair + other + (2 if side == 0 else -2)
        return remote(
            ids_hbm,
            near_ids.at[side, sender],
            near_s.at[side, other],
            near_r.at[side, sender],
            (dp, peer),
        )

    pl.semaphore_wait(barrier, n - 1 + 2 * (n_dp - 1))
    v_swap.start()
    ids_swap.start()
    k_swap.start()
    for load in loads:
        load.start()
    for j in range(share):
        q_swap[j].start()
        do_swap[j].start()

    @pl.when(has_next)
    def _():
        for other in range(2):
            near_copy(0, other, core).start()

    @pl.when(has_prev)
    def _():
        for other in range(2):
            near_copy(1, other, core).start()

    for load in loads[:9]:
        load.wait()
    odd = lax.rem(plan_ref[0, me], 2)
    slot_of = (odd, 1 - odd)
    q_gain, k_gain = qg_ref[...], kg_ref[...]
    ones = jnp.ones((2 * BLOCK, BLOCK), BF16)

    for s in range(2):
        if s == 1:
            v_swap.wait_recv()
            for j in range(share):
                for t in range(2):
                    spot = slice((1 + t) * BLOCK, (2 + t) * BLOCK)
                    kv[j][spot, BLOCK:] = v_raw[slot_of[t], :, j * BLOCK : (j + 1) * BLOCK]
                if j == 0:

                    @pl.when(has_prev)
                    def _():
                        ahead_prev.start()

                    @pl.when(has_next)
                    def _():
                        ahead_next.start()

            ids_swap.wait_recv()
        cosine, sine = rope_tables([ids[s, i] for i in range(3)])
        cosn[s] = cosine
        sinn[s] = sine

    def table(t):
        return cosn[slot_of[t]], sinn[slot_of[t]]

    rolled_k_gain, rolled_q_gain = roll_half(k_gain), roll_half(q_gain)
    k_swap.wait_recv()
    for j in range(share):
        lanes = slice(j * BLOCK, (j + 1) * BLOCK)
        for t in range(2):
            cosine, sine = table(t)
            x = k_raw[slot_of[t], :, lanes].astype(F32)
            inv = lax.rsqrt(lane_sums(x * x, ones) * (1.0 / BLOCK) + norm_eps)
            turned = inv * (x * (cosine * k_gain) + roll_half(x) * (sine * rolled_k_gain))
            spot = slice((1 + t) * BLOCK, (2 + t) * BLOCK)
            kv[j][spot, :BLOCK] = turned.astype(BF16)
            rolled[j][spot] = roll_half(turned).astype(BF16)

        @pl.when(has_prev)
        def _():
            to_prev[j].start()

        @pl.when(has_next)
        def _():
            to_next[j].start()

    for t in range(2):
        start = (2 * pair + t) * BLOCK
        low_row, high_row = key_ranges(len_ref[...], win_ref[...], clip_ref[...], start)
        spots = (start - BLOCK + lax.broadcasted_iota(jnp.int32, (SPAN, BLOCK), 0)).astype(F32)
        bias_ref[t] = jnp.where((spots >= low_row) & (spots < high_row), 0.0, -1e30)

    def heads(value, m):
        return jnp.concatenate(
            [
                value[:, 2 * m * BLOCK : (2 * m + 1) * BLOCK],
                value[:, (2 * m + 1) * BLOCK : (2 * m + 2) * BLOCK],
            ],
            axis=0,
        )

    def stacked(value):
        return jnp.concatenate(
            [value[:, h * BLOCK : (h + 1) * BLOCK] for h in range(per_group)], axis=0
        )

    scale = inv_sqrt * math.log2(math.e)
    middle = (slice(BLOCK, SPAN), slice(0, 2 * BLOCK))
    edge = (slice(0, BLOCK), slice(2 * BLOCK, SPAN))
    offset = (0, BLOCK)

    def shifted(spot, t):
        return slice(spot.start + offset[t], spot.stop + offset[t])

    def scored(j, t, spot, m, cot):
        key = kv[j][shifted(spot, t), :BLOCK]
        value = kv[j][shifted(spot, t), BLOCK:]
        query = qrot[j][t, 2 * m * BLOCK : (2 * m + 2) * BLOCK, :]
        scores = lax.dot_general(key, query, NT, preferred_element_type=F32)
        grad = lax.dot_general(value, cot, NT, preferred_element_type=F32)
        bias = bias_ref[t, spot]
        weights = jnp.exp2(scores * scale + jnp.concatenate([bias, bias], axis=1))
        return weights, grad

    sums = {}
    for j in range(share):
        loads[9 + 2 * j].wait()
        loads[10 + 2 * j].wait()
        q_swap[j].wait_recv()
        do_swap[j].wait_recv()
        for t in range(2):
            cosine, sine = table(t)
            qc, qs = cosine * q_gain, sine * rolled_q_gain
            for h in range(per_group):
                lanes = slice(h * BLOCK, (h + 1) * BLOCK)
                x = q_in[j][slot_of[t], :, lanes].astype(F32)
                inv = lax.rsqrt(lane_sums(x * x, ones) * (1.0 / BLOCK) + norm_eps)
                qinv[j][t, :, lanes] = inv
                qrot[j][t, lanes, :] = (inv * (x * qc + roll_half(x) * qs)).astype(BF16)
            for m in range(per_group // 2):
                lanes = slice(2 * m * BLOCK, (2 * m + 2) * BLOCK)
                cot = heads(do_in[j][slot_of[t]], m)
                weights, grad = scored(j, t, middle[t], m, cot)
                central[j][t][:, lanes] = weights
                central_grad[j][t][:, lanes] = grad
                sums[j, t, m] = (
                    jnp.sum(weights, axis=0, keepdims=True),
                    jnp.sum(weights * grad, axis=0, keepdims=True),
                )

    @pl.when(has_prev)
    def _():
        for sender in range(2):
            near_copy(0, sender, sender).wait_recv()

    @pl.when(has_next)
    def _():
        for sender in range(2):
            near_copy(1, sender, sender).wait_recv()

    before = 1 - lax.rem(plan_ref[0, lax.max(2 * pair - 2, 0)], 2)
    after = lax.rem(plan_ref[0, lax.min(2 * pair + 2, n - 2)], 2)
    cosine, sine = rope_tables([near_ids[0, before, i] for i in range(3)])
    near_cos[:BLOCK] = cosine
    near_sin[:BLOCK] = sine
    cosine, sine = rope_tables([near_ids[1, after, i] for i in range(3)])
    near_cos[BLOCK:] = cosine[:HALF]
    near_sin[BLOCK:] = sine[:HALF]

    def join(j, i, parts):
        even, late = parts
        lanes = slice(i * BLOCK, (i + 1) * BLOCK)
        dkv[j][0, :, lanes] = even[:BLOCK] + late[:BLOCK]
        dkv[j][1, :HALF, lanes] = even[BLOCK:] + late[BLOCK : BLOCK + HALF]
        dkv[j][1, HALF:, lanes] = late[BLOCK + HALF :]

    q_term = jnp.zeros((8, BLOCK), F32)
    k_term = jnp.zeros((8, BLOCK), F32)
    @pl.when(has_prev)
    def _():
        ahead_next.wait_recv()

    @pl.when(has_next)
    def _():
        ahead_prev.wait_recv()

    for j in range(share):

        @pl.when(has_prev)
        def _():
            to_next[j].wait_recv()

        @pl.when(has_next)
        def _():
            to_prev[j].wait_recv()

        if j > 0:

            @pl.when(has_prev)
            def _():
                home_prev[j - 1].start()

            @pl.when(has_next)
            def _():
                home_next[j - 1].start()

        for t in range(2):
            spot = edge[t]
            for m in range(per_group // 2):
                lanes = slice(2 * m * BLOCK, (2 * m + 2) * BLOCK)
                cot = heads(do_in[j][slot_of[t]], m)
                weights, grad = scored(j, t, spot, m, cot)
                total, delta = sums[j, t, m]
                inverse = 1.0 / (total + jnp.sum(weights, axis=0, keepdims=True))
                delta = (delta + jnp.sum(weights * grad, axis=0, keepdims=True)) * inverse
                sums[j, t, m] = (inverse, delta)
                probs = weights * inverse
                probs_low[j][t][spot, lanes] = probs.astype(BF16)
                score_grad[j][t][spot, lanes] = (probs * (grad - delta)).astype(BF16)
            key_grad = (
                jnp.dot(score_grad[j][t][spot], qrot[j][t], preferred_element_type=F32) * inv_sqrt
            )
            value_grad = jnp.dot(
                probs_low[j][t][spot],
                stacked(do_in[j][slot_of[t]]),
                preferred_element_type=F32,
            )
            dk_all[j, shifted(spot, t)] = key_grad
            back = (back_prev, back_next)[t][j]
            back[:, :BLOCK] = key_grad.astype(BF16)
            back[:, BLOCK:] = value_grad.astype(BF16)


        own_key = kv[j][:, :BLOCK].astype(F32)
        rolled[j][:BLOCK] = roll_half(own_key[:BLOCK]).astype(BF16)
        rolled[j][3 * BLOCK :] = roll_half(own_key[3 * BLOCK :]).astype(BF16)
        parts = []
        for t in range(2):
            spot = middle[t]
            for m in range(per_group // 2):
                lanes = slice(2 * m * BLOCK, (2 * m + 2) * BLOCK)
                inverse, delta = sums[j, t, m]
                probs = central[j][t][:, lanes] * inverse
                probs_low[j][t][spot, lanes] = probs.astype(BF16)
                score_grad[j][t][spot, lanes] = (
                    probs * (central_grad[j][t][:, lanes] - delta)
                ).astype(BF16)
            parts.append(
                jnp.dot(score_grad[j][t][spot], qrot[j][t], preferred_element_type=F32) * inv_sqrt
            )
            window = slice(offset[t], offset[t] + SPAN)
            keys = jnp.concatenate([kv[j][window, :BLOCK], rolled[j][window]], axis=1)
            dq[j][t] = lax.dot_general(score_grad[j][t][...], keys, TN, preferred_element_type=F32)
        join(j, 0, parts)
        for t in range(2):
            dk_all[j, (1 + t) * BLOCK : (2 + t) * BLOCK] = dkv[j][t, :, :BLOCK]
        key, grad = own_key, dk_all[j]
        cosine, sine = (
            jnp.concatenate([near[:BLOCK], own[odd], own[1 - odd], near[BLOCK:]], axis=0)
            for near, own in ((near_cos, cosn), (near_sin, sinn))
        )
        product = (grad * cosine - roll_half(grad) * sine) * (
            key * cosine - rolled[j][...].astype(F32) * sine
        )
        k_term = k_term + fold_rows(product)

    for j in range(share):
        for s in range(2):
            t = slot_of[s]
            cos_back, sin_back = cosn[s] * inv_sqrt, sinn[s] * inv_sqrt
            for h in range(per_group):
                lanes = slice(h * BLOCK, (h + 1) * BLOCK)
                grad = dq[j][t, lanes, :BLOCK]
                turned = grad * cos_back - dq[j][t, lanes, BLOCK:] * sin_back
                unit = q_in[j][s, :, lanes].astype(F32) * qinv[j][t, :, lanes]
                product = turned * unit
                q_term = q_term + fold_rows(product)
                q_turned[j][s, :, lanes] = turned
                q_unit[j][s, :, lanes] = unit

    term_dp[core, dp, 0:1] = jnp.sum(q_term, axis=0, keepdims=True)
    term_dp[core, dp, 1:2] = jnp.sum(k_term, axis=0, keepdims=True) / k_gain

    gathers = core == 1
    outer = 2 * pair + 1

    def dp_copy(step, sender):
        peer = lax.rem(dp + step, n_dp)
        mine_spot = (core, dp)
        return remote(
            term_dp.at[mine_spot],
            term_dp.at[mine_spot],
            td_s.at[step],
            td_r.at[sender, step],
            (peer, outer),
        )

    def ctx_copy(step, side):
        peer = 2 * lax.rem(pair + step, n // 2) + side
        return remote(
            term_ctx.at[pair], term_ctx.at[pair], tc_s.at[step, side], tc_r.at[step], (dp, peer)
        )

    for step in range(1, n_dp):
        dp_copy(step, core).start()

    @pl.when(jnp.logical_not(gathers))
    def _():
        dp_copy(0, 0).start()

    @pl.when(has_prev)
    def _():
        home_prev[share - 1].start()

    @pl.when(has_next)
    def _():
        home_next[share - 1].start()

    for j in range(share):
        for s in (1, 0):
            for h in range(per_group):
                lanes = slice(h * BLOCK, (h + 1) * BLOCK)
                turned, unit = q_turned[j][s, :, lanes], q_unit[j][s, :, lanes]
                weighted = turned * q_gain
                mean = lane_sums(weighted * unit, ones) * (1.0 / BLOCK)
                result = (qinv[j][slot_of[s], :, lanes] * (weighted - unit * mean)).astype(BF16)
                if s == 0:
                    qgrad_ref[mine, :, j * wide + h * BLOCK : j * wide + (h + 1) * BLOCK] = result
                else:
                    q_out[j][:, lanes] = result
            if s == 1:
                q_home[j].start()
    for j in range(share):
        parts = [
            jnp.dot(
                probs_low[j][t][middle[t]],
                stacked(do_in[j][slot_of[t]]),
                preferred_element_type=F32,
            )
            for t in range(2)
        ]
        join(j, 1, parts)

    @pl.when(gathers)
    def _():
        for step in range(n_dp):
            dp_copy(step, 0).wait_recv()
        for step in range(1, n_dp):
            dp_copy(step, 1).wait_recv()
        term_ctx[pair, 0:2] = jnp.sum(jnp.sum(term_dp[:, :, 0:2], axis=0), axis=0)
        for step in range(1, n // 2):
            ctx_copy(step, 0).start()
            ctx_copy(step, 1).start()
        ctx_copy(0, 0).start()

    for j in range(share):

        @pl.when(has_next)
        def _():
            home_prev[j].wait_recv()

        @pl.when(has_prev)
        def _():
            home_next[j].wait_recv()

        lanes = slice(j * BLOCK, (j + 1) * BLOCK)
        for s in (1, 0):
            t = slot_of[s]
            cosine, sine = cosn[s], sinn[s]
            total = dkv[j][t] + arrived[j][t].astype(F32)
            grad = total[:, :BLOCK]
            x = k_raw[s, :, lanes].astype(F32)
            inv = lax.rsqrt(lane_sums(x * x, ones) * (1.0 / BLOCK) + norm_eps)
            unit = x * inv
            turned = grad * cosine - roll_half(grad) * sine
            mean = lane_sums(turned * unit * k_gain, ones) * (1.0 / BLOCK)
            result = (inv * (turned * k_gain - unit * mean)).astype(BF16)
            if s == 0:
                kgrad_ref[mine, :, lanes] = result
                vgrad_ref[mine, :, lanes] = total[:, BLOCK:].astype(BF16)
            else:
                k_out[:, lanes] = result
                v_out[:, lanes] = total[:, BLOCK:].astype(BF16)
    k_home.start()
    v_home.start()

    ids_swap.wait_send()
    k_swap.wait_send()
    v_swap.wait_send()
    for j in range(share):
        q_swap[j].wait_send()
        do_swap[j].wait_send()
        q_home[j].wait_recv()
        q_home[j].wait_send()

        @pl.when(has_next)
        def _():
            to_next[j].wait_send()
            home_next[j].wait_send()

        @pl.when(has_prev)
        def _():
            to_prev[j].wait_send()
            home_prev[j].wait_send()

    @pl.when(has_next)
    def _():
        ahead_next.wait_send()
        for other in range(2):
            near_copy(0, other, core).wait_send()

    @pl.when(has_prev)
    def _():
        ahead_prev.wait_send()
        for other in range(2):
            near_copy(1, other, core).wait_send()

    for step in range(1, n_dp):
        dp_copy(step, core).wait_send()

    @pl.when(jnp.logical_not(gathers))
    def _():
        dp_copy(0, 0).wait_send()

    k_home.wait_recv()
    v_home.wait_recv()
    k_home.wait_send()
    v_home.wait_send()
    for step in range(1, n // 2):
        ctx_copy(step, core).wait_recv()

    @pl.when(jnp.logical_not(gathers))
    def _():
        ctx_copy(0, 0).wait_recv()

    totals = jnp.sum(term_ctx[:, 0:2], axis=0)
    token_count = n_dp * n * BLOCK
    qgain_ref[...] = totals[0:1] * (1.0 / math.sqrt(token_count * groups * per_group))
    kgain_ref[...] = totals[1:2] * (1.0 / math.sqrt(token_count * groups))

    @pl.when(gathers)
    def _():
        for step in range(1, n // 2):
            ctx_copy(step, 0).wait_send()
            ctx_copy(step, 1).wait_send()
        ctx_copy(0, 0).wait_send()


def hand_over(*refs):
    sources, targets, sems = refs[:5], refs[5:10], refs[10]
    copies = []
    for source, target in zip(sources, targets):
        if len(source.shape) == 2:
            copies.append((source, target))
        else:
            width = source.shape[2]
            for half in range(2):
                lanes = slice(half * width, (half + 1) * width)
                copies.append((source.at[half], target.at[0, :, lanes]))
    copies = [
        pltpu.make_async_copy(source, target, sems.at[i])
        for i, (source, target) in enumerate(copies)
    ]
    for copy in copies:
        copy.start()
    for copy in copies:
        copy.wait()


def shards(
    q_proj,
    k_proj,
    v_proj,
    out_grad,
    q_gain,
    k_gain,
    pos_ids,
    stretch_lengths,
    stretch_windows,
    clip_ids,
    dispatch_plan,
):
    n = lax.axis_size("ctx")
    n_dp = lax.axis_size("dp")
    groups = k_proj.shape[2] // BLOCK
    heads = q_proj.shape[2] // BLOCK
    per_group = heads // groups
    share = groups // 2
    wide = per_group * BLOCK
    hbm = pl.BlockSpec(memory_space=pl.ANY)
    vmem = pl.BlockSpec(memory_space=pltpu.VMEM)
    dma = pltpu.SemaphoreType.DMA
    count = stretch_lengths.shape[1]
    nat = 3 * BLOCK + HALF
    central = (SPAN - BLOCK, 2 * BLOCK)
    out = pl.pallas_call(
        functools.partial(kernel, n, n_dp, groups, per_group),
        out_shape=(
            pltpu.VMEM((2, BLOCK, share * wide), BF16),
            pltpu.VMEM((2, BLOCK, share * BLOCK), BF16),
            pltpu.VMEM((2, BLOCK, share * BLOCK), BF16),
            pltpu.VMEM((1, BLOCK), F32),
            pltpu.VMEM((1, BLOCK), F32),
        ),
        in_specs=[hbm] * 11,
        out_specs=(vmem,) * 5,
        scratch_shapes=[
            pltpu.SMEM(dispatch_plan.shape, jnp.int32),
            pltpu.VMEM((1, BLOCK), F32),
            pltpu.VMEM((1, BLOCK), F32),
            pltpu.VMEM((2, 3, 1, BLOCK), jnp.int32),
            pltpu.VMEM((2, 2, 3, 1, BLOCK), jnp.int32),
            pltpu.VMEM((1, count), jnp.int32),
            pltpu.VMEM((1, count), jnp.int32),
            pltpu.VMEM((1, count), jnp.int32),
            pltpu.VMEM((2, BLOCK, share * BLOCK), BF16),
            pltpu.VMEM((2, BLOCK, share * BLOCK), BF16),
            pltpu.VMEM((2, BLOCK, BLOCK), F32),
            pltpu.VMEM((2, BLOCK, BLOCK), F32),
            pltpu.VMEM((BLOCK + HALF, BLOCK), F32),
            pltpu.VMEM((BLOCK + HALF, BLOCK), F32),
            pltpu.VMEM((2, SPAN, BLOCK), F32),
            pltpu.VMEM((share, nat, BLOCK), F32),
            pltpu.VMEM((BLOCK, share * BLOCK), BF16),
            pltpu.VMEM((BLOCK, share * BLOCK), BF16),
            pltpu.VMEM((n // 2, 8, BLOCK), F32),
            pltpu.VMEM((2, n_dp, 8, BLOCK), F32),
        ]
        + [pltpu.VMEM((2, BLOCK, wide), BF16)] * (2 * share)
        + [pltpu.VMEM((nat, 2 * BLOCK), BF16)] * share
        + [pltpu.VMEM((nat, BLOCK), BF16)] * share
        + [pltpu.VMEM((2, wide, BLOCK), BF16)] * share
        + [pltpu.VMEM((2, BLOCK, wide), F32)] * share
        + [pltpu.VMEM((rows, wide), F32) for rows in central] * (2 * share)
        + [pltpu.VMEM((SPAN, wide), BF16)] * (4 * share)
        + [pltpu.VMEM((2, BLOCK, 2 * BLOCK), F32)] * share
        + [pltpu.VMEM((2, wide, 2 * BLOCK), F32)] * share
        + [pltpu.VMEM((BLOCK, 2 * BLOCK), BF16)] * share
        + [pltpu.VMEM((HALF, 2 * BLOCK), BF16)] * share
        + [pltpu.VMEM((2, BLOCK, 2 * BLOCK), BF16)] * share
        + [pltpu.VMEM((BLOCK, wide), BF16)] * share
        + [pltpu.VMEM((2, BLOCK, wide), F32)] * (2 * share)
        + [
            dma((9 + 2 * share,)),
            dma((7 + 7 * share,)),
            dma((7 + 7 * share,)),
            dma((2, 2)),
            dma((2, 2)),
            dma((n // 2, 2)),
            dma((n // 2,)),
            dma((n_dp,)),
            dma((2, n_dp)),
        ],
        compiler_params=pltpu.CompilerParams(
            collective_id=0, has_side_effects=True, vmem_limit_bytes=VMEM_LIMIT
        ),
        cost_estimate=pl.CostEstimate(
            flops=10 * heads * BLOCK * SPAN * BLOCK,
            bytes_accessed=6 * BLOCK * heads * BLOCK,
            transcendentals=heads * BLOCK * SPAN,
        ),
    )(
        *[
            pltpu.with_memory_space_constraint(array, pltpu.HBM)
            for array in (
                dispatch_plan,
                k_proj,
                v_proj,
                q_gain.reshape(1, BLOCK),
                k_gain.reshape(1, BLOCK),
                pos_ids.transpose(1, 0, 2),
                stretch_lengths,
                stretch_windows,
                clip_ids,
                q_proj,
                out_grad,
            )
        ]
    )
    out = pl.pallas_call(
        hand_over,
        out_shape=(
            pltpu.HBM(q_proj.shape, BF16),
            pltpu.HBM(k_proj.shape, BF16),
            pltpu.HBM(v_proj.shape, BF16),
            pltpu.HBM((1, BLOCK), F32),
            pltpu.HBM((1, BLOCK), F32),
        ),
        in_specs=[hbm] * 5,
        out_specs=(pl.BlockSpec(memory_space=pltpu.HBM),) * 5,
        scratch_shapes=[dma((8,))],
    )(*[pltpu.with_memory_space_constraint(array, pltpu.VMEM) for array in out])
    return (out[0], out[1], out[2], out[3].reshape(BLOCK), out[4].reshape(BLOCK))


def solution(mesh):
    row = P("dp", "ctx", None)
    table = P("dp", None)
    return jax.shard_map(
        shards,
        mesh=mesh,
        in_specs=(row, row, row, row, P(), P(), P("dp", None, "ctx"), table, table, table, table),
        out_specs=(row, row, row, P(), P()),
        check_vma=False,
    )
```

```python
import functools
import math

import jax
import jax.numpy as jnp
from jax import lax
from jax.experimental import pallas as pl
from jax.experimental.pallas import tpu as pltpu
from jax.sharding import PartitionSpec as P

MESH = pl.DeviceIdType.MESH
F32 = jnp.float32
BF16 = jnp.bfloat16
BLOCK = 128
HALF = BLOCK // 2
SPAN = 2 * BLOCK + HALF
norm_eps = 1e-06
VMEM_LIMIT = 40 * 1024 * 1024
rope_base = 10000.0

NT = (((1,), (1,)), ((), ()))
TN = (((0,), (0,)), ((), ()))


def sin_cos(angle):
    turns = jnp.floor(angle * (2.0 / math.pi) + 0.5)
    rest = angle - turns * 1.5703125
    rest = rest - turns * 4.837512969970703125e-4
    rest = rest - turns * 7.549789948768648e-8
    square = rest * rest
    sine = rest + rest * square * (
        -1.6666654611e-1 + square * (8.3321608736e-3 + square * -1.9515295891e-4)
    )
    cosine = (
        1.0
        - 0.5 * square
        + square
        * square
        * (4.166664568298827e-2 + square * (-1.388731625493765e-3 + square * 2.443315711809948e-5))
    )
    quarter = turns.astype(jnp.int32)
    odd = (quarter & 1) == 1
    sine_out = jnp.where(odd, cosine, sine)
    cosine_out = jnp.where(odd, sine, cosine)
    sine_out = jnp.where((quarter & 2) == 2, -sine_out, sine_out)
    cosine_out = jnp.where(((quarter + 1) & 2) == 2, -cosine_out, cosine_out)
    return sine_out, cosine_out


def roll_half(x):
    return pltpu.roll(x, HALF, 1)


def rope_tables(ids):
    rows = lax.broadcasted_iota(jnp.int32, (BLOCK, BLOCK), 0)
    lanes = lax.broadcasted_iota(jnp.int32, (BLOCK, BLOCK), 1)
    columns = [
        jnp.sum(jnp.where(rows == lanes, ids[t].astype(F32), 0.0), axis=1, keepdims=True)
        for t in range(3)
    ]
    pair = lanes % HALF
    chosen = jnp.where(pair < 16, columns[0], jnp.where(pair < 40, columns[1], columns[2]))
    pair_row = lax.broadcasted_iota(jnp.int32, (1, BLOCK), 1) % HALF
    frequency = jnp.exp(pair_row.astype(F32) * (-math.log(rope_base) / HALF))
    sine, cosine = sin_cos(chosen * frequency)
    return cosine, jnp.where(lanes < HALF, -sine, sine)


def key_ranges(lengths, windows, clips, start):
    count = lengths.shape[1]
    rows = lax.broadcasted_iota(jnp.int32, (count, count), 0)
    lanes = lax.broadcasted_iota(jnp.int32, (count, count), 1)

    def column(where_, values):
        return jnp.sum(jnp.where(where_, values.astype(F32), 0.0), axis=1, keepdims=True)

    ends = column(lanes <= rows, lengths)
    starts = column(lanes < rows, lengths)
    before = column(lanes == rows - 1, lengths)
    window = column(lanes == rows, windows)
    clip = column(lanes == rows, clips + 1)
    clip_before = column(lanes == rows - 1, clips + 1)
    low = starts - jnp.where(clip == clip_before, window * before, 0.0)
    spots = (start + lax.broadcasted_iota(jnp.int32, (count, BLOCK), 1)).astype(F32)
    inside = (starts <= spots) & (spots < ends)
    low_row = jnp.sum(jnp.where(inside, low, 0.0), axis=0, keepdims=True)
    high_row = jnp.sum(jnp.where(inside, ends, 0.0), axis=0, keepdims=True)
    return low_row, high_row


def lane_sums(x, ones):
    high = x.astype(BF16)
    low = (x - high.astype(F32)).astype(BF16)
    return jnp.dot(jnp.concatenate([high, low], axis=1), ones, preferred_element_type=F32)


def fold_rows(x):
    return jnp.sum(x.reshape(x.shape[0] // 8, 8, x.shape[1]), axis=0)


def kernel(n, n_dp, groups, per_group, *refs):
    share = groups // 2
    wide = per_group * BLOCK
    refs = iter(refs)

    def take(count):
        return [next(refs) for _ in range(count)]

    (
        plan_hbm,
        k_hbm,
        v_hbm,
        qg_hbm,
        kg_hbm,
        ids_hbm,
        len_hbm,
        win_hbm,
        clip_hbm,
        q_hbm,
        do_hbm,
    ) = take(11)
    qgrad_ref, kgrad_ref, vgrad_ref, qgain_ref, kgain_ref = take(5)
    plan_ref, qg_ref, kg_ref, ids, near_ids, len_ref, win_ref, clip_ref = take(8)
    k_raw, v_raw, cosn, sinn, near_cos, near_sin, bias_ref, dk_all = take(8)
    k_out, v_out, term_ctx, term_dp = take(4)
    q_in = take(share)
    do_in = take(share)
    kv = take(share)
    rolled = take(share)
    qrot = take(share)
    qinv = take(share)
    central = [take(2) for _ in range(share)]
    central_grad = [take(2) for _ in range(share)]
    probs_low = [take(2) for _ in range(share)]
    score_grad = [take(2) for _ in range(share)]
    dkv = take(share)
    dq = take(share)
    back_prev = take(share)
    back_next = take(share)
    arrived = take(share)
    q_out = take(share)
    q_turned = take(share)
    q_unit = take(share)
    load_sem, sent, got, near_s, near_r, tc_s, tc_r, td_s, td_r = take(9)

    me = lax.axis_index("ctx")
    dp = lax.axis_index("dp")
    core = lax.rem(me, 2)
    pair = me // 2
    partner = me + 1 - 2 * core
    has_prev = me >= 2
    has_next = me < n - 2
    inv_sqrt = BLOCK ** (-0.5)

    def columns(which, width, j=0):
        return pl.ds(pl.multiple_of(which * (share * width) + j * width, BLOCK), width)

    mine, theirs = core, 1 - core
    both_k = pl.ds(pl.multiple_of(mine * (share * BLOCK), BLOCK), share * BLOCK)
    their_k = pl.ds(pl.multiple_of(theirs * (share * BLOCK), BLOCK), share * BLOCK)
    moves = [
        (plan_hbm, plan_ref),
        (ids_hbm, ids.at[0]),
        (qg_hbm, qg_ref),
        (kg_hbm, kg_ref),
        (k_hbm.at[0, :, both_k], k_raw.at[0]),
        (v_hbm.at[0, :, both_k], v_raw.at[0]),
        (len_hbm, len_ref),
        (win_hbm, win_ref),
        (clip_hbm, clip_ref),
    ]
    for j in range(share):
        moves.append((q_hbm.at[0, :, columns(mine, wide, j)], q_in[j].at[0]))
        moves.append((do_hbm.at[0, :, columns(mine, wide, j)], do_in[j].at[0]))
    loads = [
        pltpu.make_async_copy(source, target, load_sem.at[i])
        for i, (source, target) in enumerate(moves)
    ]

    barrier = pltpu.get_barrier_semaphore()
    pl.semaphore_signal(barrier, inc=1, device_id=(dp, partner), device_id_type=MESH)

    for step in range(1, n // 2):
        for side in range(2):
            peer = (dp, 2 * lax.rem(pair + step, n // 2) + side)
            pl.semaphore_signal(barrier, inc=1, device_id=peer, device_id_type=MESH)
    for step in range(1, n_dp):
        for side in range(2):
            peer = (lax.rem(dp + step, n_dp), 2 * pair + side)
            pl.semaphore_signal(barrier, inc=1, device_id=peer, device_id_type=MESH)

    @pl.when(jnp.logical_not(has_prev))
    def _():
        near_ids[0] = jnp.zeros_like(near_ids[0])
        for j in range(share):
            kv[j][:BLOCK] = jnp.zeros((BLOCK, 2 * BLOCK), BF16)
            arrived[j][0, :HALF] = jnp.zeros((HALF, 2 * BLOCK), BF16)

    @pl.when(jnp.logical_not(has_next))
    def _():
        near_ids[1] = jnp.zeros_like(near_ids[1])
        for j in range(share):
            kv[j][3 * BLOCK :] = jnp.zeros((HALF, 2 * BLOCK), BF16)
            arrived[j][1] = jnp.zeros((BLOCK, 2 * BLOCK), BF16)

    for j in range(share):
        arrived[j][0, HALF:] = jnp.zeros((HALF, 2 * BLOCK), BF16)

    def remote(source, target, send, receive, peer):
        return pltpu.make_async_remote_copy(
            src_ref=source,
            dst_ref=target,
            send_sem=send,
            recv_sem=receive,
            device_id=peer,
            device_id_type=MESH,
        )

    count = [0]

    def numbered(source, target, peer):
        i = count[0]
        count[0] += 1
        return remote(source, target, sent.at[i], got.at[i], (dp, peer))

    k_swap = numbered(k_hbm.at[0, :, their_k], k_raw.at[1], partner)
    v_swap = numbered(v_hbm.at[0, :, their_k], v_raw.at[1], partner)
    ids_swap = numbered(ids_hbm, ids.at[1], partner)
    q_swap = [
        numbered(q_hbm.at[0, :, columns(theirs, wide, j)], q_in[j].at[1], partner)
        for j in range(share)
    ]
    do_swap = [
        numbered(do_hbm.at[0, :, columns(theirs, wide, j)], do_in[j].at[1], partner)
        for j in range(share)
    ]
    last_block, last_half = slice(2 * BLOCK, 3 * BLOCK), slice(3 * BLOCK, SPAN + BLOCK)
    first_block, first_half = slice(0, BLOCK), slice(BLOCK, BLOCK + HALF)
    pieces = [slice(0, BLOCK) if j == 0 else slice(0, 2 * BLOCK) for j in range(share)]
    values = slice(BLOCK, 2 * BLOCK)
    to_next = [
        numbered(kv[j].at[last_block, pieces[j]], kv[j].at[first_block, pieces[j]], me + 2)
        for j in range(share)
    ]
    to_prev = [
        numbered(kv[j].at[first_half, pieces[j]], kv[j].at[last_half, pieces[j]], me - 2)
        for j in range(share)
    ]
    ahead_next = numbered(kv[0].at[last_block, values], kv[0].at[first_block, values], me + 2)
    ahead_prev = numbered(kv[0].at[first_half, values], kv[0].at[last_half, values], me - 2)
    home_prev = [numbered(back_prev[j], arrived[j].at[1], me - 2) for j in range(share)]
    home_next = [numbered(back_next[j], arrived[j].at[0, :HALF], me + 2) for j in range(share)]
    q_home = [
        numbered(q_out[j], qgrad_ref.at[mine, :, j * wide : (j + 1) * wide], partner)
        for j in range(share)
    ]
    k_home = numbered(k_out, kgrad_ref.at[mine], partner)
    v_home = numbered(v_out, vgrad_ref.at[mine], partner)

    def near_copy(side, other, sender):
        peer = 2 * pair + other + (2 if side == 0 else -2)
        return remote(
            ids_hbm,
            near_ids.at[side, sender],
            near_s.at[side, other],
            near_r.at[side, sender],
            (dp, peer),
        )

    pl.semaphore_wait(barrier, n - 1 + 2 * (n_dp - 1))
    v_swap.start()
    ids_swap.start()
    k_swap.start()
    for load in loads:
        load.start()
    for j in range(share):
        q_swap[j].start()
        do_swap[j].start()

    @pl.when(has_next)
    def _():
        for other in range(2):
            near_copy(0, other, core).start()

    @pl.when(has_prev)
    def _():
        for other in range(2):
            near_copy(1, other, core).start()

    for load in loads[:9]:
        load.wait()
    odd = lax.rem(plan_ref[0, me], 2)
    slot_of = (odd, 1 - odd)
    q_gain, k_gain = qg_ref[...], kg_ref[...]
    ones = jnp.ones((2 * BLOCK, BLOCK), BF16)

    for s in range(2):
        if s == 1:
            v_swap.wait_recv()
            for j in range(share):
                for t in range(2):
                    spot = slice((1 + t) * BLOCK, (2 + t) * BLOCK)
                    kv[j][spot, BLOCK:] = v_raw[slot_of[t], :, j * BLOCK : (j + 1) * BLOCK]
                if j == 0:

                    @pl.when(has_prev)
                    def _():
                        ahead_prev.start()

                    @pl.when(has_next)
                    def _():
                        ahead_next.start()

            ids_swap.wait_recv()
        cosine, sine = rope_tables([ids[s, i] for i in range(3)])
        cosn[s] = cosine
        sinn[s] = sine

    def table(t):
        return cosn[slot_of[t]], sinn[slot_of[t]]

    rolled_k_gain, rolled_q_gain = roll_half(k_gain), roll_half(q_gain)
    k_swap.wait_recv()
    for j in range(share):
        lanes = slice(j * BLOCK, (j + 1) * BLOCK)
        for t in range(2):
            cosine, sine = table(t)
            x = k_raw[slot_of[t], :, lanes].astype(F32)
            inv = lax.rsqrt(lane_sums(x * x, ones) * (1.0 / BLOCK) + norm_eps)
            turned = inv * (x * (cosine * k_gain) + roll_half(x) * (sine * rolled_k_gain))
            spot = slice((1 + t) * BLOCK, (2 + t) * BLOCK)
            kv[j][spot, :BLOCK] = turned.astype(BF16)
            rolled[j][spot] = roll_half(turned).astype(BF16)

        @pl.when(has_prev)
        def _():
            to_prev[j].start()

        @pl.when(has_next)
        def _():
            to_next[j].start()

    for t in range(2):
        start = (2 * pair + t) * BLOCK
        low_row, high_row = key_ranges(len_ref[...], win_ref[...], clip_ref[...], start)
        spots = (start - BLOCK + lax.broadcasted_iota(jnp.int32, (SPAN, BLOCK), 0)).astype(F32)
        bias_ref[t] = jnp.where((spots >= low_row) & (spots < high_row), 0.0, -1e30)

    def heads(value, m):
        return jnp.concatenate(
            [
                value[:, 2 * m * BLOCK : (2 * m + 1) * BLOCK],
                value[:, (2 * m + 1) * BLOCK : (2 * m + 2) * BLOCK],
            ],
            axis=0,
        )

    def stacked(value):
        return jnp.concatenate(
            [value[:, h * BLOCK : (h + 1) * BLOCK] for h in range(per_group)], axis=0
        )

    scale = inv_sqrt * math.log2(math.e)
    middle = (slice(BLOCK, SPAN), slice(0, 2 * BLOCK))
    edge = (slice(0, BLOCK), slice(2 * BLOCK, SPAN))
    offset = (0, BLOCK)

    def shifted(spot, t):
        return slice(spot.start + offset[t], spot.stop + offset[t])

    def scored(j, t, spot, m, cot):
        key = kv[j][shifted(spot, t), :BLOCK]
        value = kv[j][shifted(spot, t), BLOCK:]
        query = qrot[j][t, 2 * m * BLOCK : (2 * m + 2) * BLOCK, :]
        scores = lax.dot_general(key, query, NT, preferred_element_type=F32)
        grad = lax.dot_general(value, cot, NT, preferred_element_type=F32)
        bias = bias_ref[t, spot]
        weights = jnp.exp2(scores * scale + jnp.concatenate([bias, bias], axis=1))
        return weights, grad

    sums = {}
    for j in range(share):
        loads[9 + 2 * j].wait()
        loads[10 + 2 * j].wait()
        q_swap[j].wait_recv()
        do_swap[j].wait_recv()
        for t in range(2):
            cosine, sine = table(t)
            qc, qs = cosine * q_gain, sine * rolled_q_gain
            for h in range(per_group):
                lanes = slice(h * BLOCK, (h + 1) * BLOCK)
                x = q_in[j][slot_of[t], :, lanes].astype(F32)
                inv = lax.rsqrt(lane_sums(x * x, ones) * (1.0 / BLOCK) + norm_eps)
                qinv[j][t, :, lanes] = inv
                qrot[j][t, lanes, :] = (inv * (x * qc + roll_half(x) * qs)).astype(BF16)
            for m in range(per_group // 2):
                lanes = slice(2 * m * BLOCK, (2 * m + 2) * BLOCK)
                cot = heads(do_in[j][slot_of[t]], m)
                weights, grad = scored(j, t, middle[t], m, cot)
                central[j][t][:, lanes] = weights
                central_grad[j][t][:, lanes] = grad
                sums[j, t, m] = (
                    jnp.sum(weights, axis=0, keepdims=True),
                    jnp.sum(weights * grad, axis=0, keepdims=True),
                )

    def join(j, i, parts):
        even, late = parts
        lanes = slice(i * BLOCK, (i + 1) * BLOCK)
        dkv[j][0, :, lanes] = even[:BLOCK] + late[:BLOCK]
        dkv[j][1, :HALF, lanes] = even[BLOCK:] + late[BLOCK : BLOCK + HALF]
        dkv[j][1, HALF:, lanes] = late[BLOCK + HALF :]

    def edge_values(j, t):
        grad = jnp.dot(
            probs_low[j][t][edge[t]], stacked(do_in[j][slot_of[t]]), preferred_element_type=F32
        )
        (back_prev, back_next)[t][j][:, BLOCK:] = grad.astype(BF16)

    q_term = jnp.zeros((8, BLOCK), F32)
    k_term = jnp.zeros((8, BLOCK), F32)
    @pl.when(has_prev)
    def _():
        ahead_next.wait_recv()

    @pl.when(has_next)
    def _():
        ahead_prev.wait_recv()

    for j in range(share):

        @pl.when(has_prev)
        def _():
            to_next[j].wait_recv()

        @pl.when(has_next)
        def _():
            to_prev[j].wait_recv()

        if j > 0:

            @pl.when(has_prev)
            def _():
                home_prev[j - 1].start()

            @pl.when(has_next)
            def _():
                home_next[j - 1].start()

        for t in range(2):
            spot = edge[t]
            for m in range(per_group // 2):
                lanes = slice(2 * m * BLOCK, (2 * m + 2) * BLOCK)
                cot = heads(do_in[j][slot_of[t]], m)
                weights, grad = scored(j, t, spot, m, cot)
                total, delta = sums[j, t, m]
                inverse = 1.0 / (total + jnp.sum(weights, axis=0, keepdims=True))
                delta = (delta + jnp.sum(weights * grad, axis=0, keepdims=True)) * inverse
                sums[j, t, m] = (inverse, delta)
                probs = weights * inverse
                probs_low[j][t][spot, lanes] = probs.astype(BF16)
                score_grad[j][t][spot, lanes] = (probs * (grad - delta)).astype(BF16)
            key_grad = (
                jnp.dot(score_grad[j][t][spot], qrot[j][t], preferred_element_type=F32) * inv_sqrt
            )
            dk_all[j, shifted(spot, t)] = key_grad
            (back_prev, back_next)[t][j][:, :BLOCK] = key_grad.astype(BF16)
            if j < share - 1:
                edge_values(j, t)

        if j == 0:
            @pl.when(has_prev)
            def _():
                for sender in range(2):
                    near_copy(0, sender, sender).wait_recv()

            @pl.when(has_next)
            def _():
                for sender in range(2):
                    near_copy(1, sender, sender).wait_recv()

            before = 1 - lax.rem(plan_ref[0, lax.max(2 * pair - 2, 0)], 2)
            after = lax.rem(plan_ref[0, lax.min(2 * pair + 2, n - 2)], 2)
            cosine, sine = rope_tables([near_ids[0, before, i] for i in range(3)])
            near_cos[:BLOCK] = cosine
            near_sin[:BLOCK] = sine
            cosine, sine = rope_tables([near_ids[1, after, i] for i in range(3)])
            near_cos[BLOCK:] = cosine[:HALF]
            near_sin[BLOCK:] = sine[:HALF]

        own_key = kv[j][:, :BLOCK].astype(F32)
        rolled[j][:BLOCK] = roll_half(own_key[:BLOCK]).astype(BF16)
        rolled[j][3 * BLOCK :] = roll_half(own_key[3 * BLOCK :]).astype(BF16)
        parts = []
        for t in range(2):
            spot = middle[t]
            for m in range(per_group // 2):
                lanes = slice(2 * m * BLOCK, (2 * m + 2) * BLOCK)
                inverse, delta = sums[j, t, m]
                probs = central[j][t][:, lanes] * inverse
                probs_low[j][t][spot, lanes] = probs.astype(BF16)
                score_grad[j][t][spot, lanes] = (
                    probs * (central_grad[j][t][:, lanes] - delta)
                ).astype(BF16)
            parts.append(
                jnp.dot(score_grad[j][t][spot], qrot[j][t], preferred_element_type=F32) * inv_sqrt
            )
            window = slice(offset[t], offset[t] + SPAN)
            keys = jnp.concatenate([kv[j][window, :BLOCK], rolled[j][window]], axis=1)
            dq[j][t] = lax.dot_general(score_grad[j][t][...], keys, TN, preferred_element_type=F32)
        join(j, 0, parts)
        for t in range(2):
            dk_all[j, (1 + t) * BLOCK : (2 + t) * BLOCK] = dkv[j][t, :, :BLOCK]
        key, grad = own_key, dk_all[j]
        cosine, sine = (
            jnp.concatenate([near[:BLOCK], own[odd], own[1 - odd], near[BLOCK:]], axis=0)
            for near, own in ((near_cos, cosn), (near_sin, sinn))
        )
        product = (grad * cosine - roll_half(grad) * sine) * (
            key * cosine - rolled[j][...].astype(F32) * sine
        )
        k_term = k_term + fold_rows(product)

    for j in range(share):
        for s in range(2):
            t = slot_of[s]
            cos_back, sin_back = cosn[s] * inv_sqrt, sinn[s] * inv_sqrt
            for h in range(per_group):
                lanes = slice(h * BLOCK, (h + 1) * BLOCK)
                grad = dq[j][t, lanes, :BLOCK]
                turned = grad * cos_back - dq[j][t, lanes, BLOCK:] * sin_back
                unit = q_in[j][s, :, lanes].astype(F32) * qinv[j][t, :, lanes]
                product = turned * unit
                q_term = q_term + fold_rows(product)
                q_turned[j][s, :, lanes] = turned
                q_unit[j][s, :, lanes] = unit

    term_dp[core, dp, 0:1] = jnp.sum(q_term, axis=0, keepdims=True)
    term_dp[core, dp, 1:2] = jnp.sum(k_term, axis=0, keepdims=True) / k_gain

    gathers = core == 1
    outer = 2 * pair + 1

    def dp_copy(step, sender):
        peer = lax.rem(dp + step, n_dp)
        mine_spot = (core, dp)
        return remote(
            term_dp.at[mine_spot],
            term_dp.at[mine_spot],
            td_s.at[step],
            td_r.at[sender, step],
            (peer, outer),
        )

    def ctx_copy(step, side):
        peer = 2 * lax.rem(pair + step, n // 2) + side
        return remote(
            term_ctx.at[pair], term_ctx.at[pair], tc_s.at[step, side], tc_r.at[step], (dp, peer)
        )

    for step in range(1, n_dp):
        dp_copy(step, core).start()

    @pl.when(jnp.logical_not(gathers))
    def _():
        dp_copy(0, 0).start()

    for t in range(2):
        edge_values(share - 1, t)

    @pl.when(has_prev)
    def _():
        home_prev[share - 1].start()

    @pl.when(has_next)
    def _():
        home_next[share - 1].start()

    for j in range(share):
        for s in (1, 0):
            for h in range(per_group):
                lanes = slice(h * BLOCK, (h + 1) * BLOCK)
                turned, unit = q_turned[j][s, :, lanes], q_unit[j][s, :, lanes]
                weighted = turned * q_gain
                mean = lane_sums(weighted * unit, ones) * (1.0 / BLOCK)
                result = (qinv[j][slot_of[s], :, lanes] * (weighted - unit * mean)).astype(BF16)
                if s == 0:
                    qgrad_ref[mine, :, j * wide + h * BLOCK : j * wide + (h + 1) * BLOCK] = result
                else:
                    q_out[j][:, lanes] = result
            if s == 1:
                q_home[j].start()
    for j in range(share):
        parts = [
            jnp.dot(
                probs_low[j][t][middle[t]],
                stacked(do_in[j][slot_of[t]]),
                preferred_element_type=F32,
            )
            for t in range(2)
        ]
        join(j, 1, parts)

    k_norm = {}
    for j in range(share):
        for s in range(2):
            x = k_raw[s, :, j * BLOCK : (j + 1) * BLOCK].astype(F32)
            inv = lax.rsqrt(lane_sums(x * x, ones) * (1.0 / BLOCK) + norm_eps)
            k_norm[j, s] = (inv, x * inv)

    @pl.when(gathers)
    def _():
        for step in range(n_dp):
            dp_copy(step, 0).wait_recv()
        for step in range(1, n_dp):
            dp_copy(step, 1).wait_recv()
        term_ctx[pair, 0:2] = jnp.sum(jnp.sum(term_dp[:, :, 0:2], axis=0), axis=0)
        for step in range(1, n // 2):
            ctx_copy(step, 0).start()
            ctx_copy(step, 1).start()
        ctx_copy(0, 0).start()

    for j in range(share):

        @pl.when(has_next)
        def _():
            home_prev[j].wait_recv()

        @pl.when(has_prev)
        def _():
            home_next[j].wait_recv()

        lanes = slice(j * BLOCK, (j + 1) * BLOCK)
        for s in (1, 0):
            t = slot_of[s]
            cosine, sine = cosn[s], sinn[s]
            total = dkv[j][t] + arrived[j][t].astype(F32)
            grad = total[:, :BLOCK]
            inv, unit = k_norm[j, s]
            turned = grad * cosine - roll_half(grad) * sine
            mean = lane_sums(turned * unit * k_gain, ones) * (1.0 / BLOCK)
            result = (inv * (turned * k_gain - unit * mean)).astype(BF16)
            if s == 0:
                kgrad_ref[mine, :, lanes] = result
                vgrad_ref[mine, :, lanes] = total[:, BLOCK:].astype(BF16)
            else:
                k_out[:, lanes] = result
                v_out[:, lanes] = total[:, BLOCK:].astype(BF16)
    k_home.start()
    v_home.start()

    ids_swap.wait_send()
    k_swap.wait_send()
    v_swap.wait_send()
    for j in range(share):
        q_swap[j].wait_send()
        do_swap[j].wait_send()
        q_home[j].wait_recv()
        q_home[j].wait_send()

        @pl.when(has_next)
        def _():
            to_next[j].wait_send()
            home_next[j].wait_send()

        @pl.when(has_prev)
        def _():
            to_prev[j].wait_send()
            home_prev[j].wait_send()

    @pl.when(has_next)
    def _():
        ahead_next.wait_send()
        for other in range(2):
            near_copy(0, other, core).wait_send()

    @pl.when(has_prev)
    def _():
        ahead_prev.wait_send()
        for other in range(2):
            near_copy(1, other, core).wait_send()

    for step in range(1, n_dp):
        dp_copy(step, core).wait_send()

    @pl.when(jnp.logical_not(gathers))
    def _():
        dp_copy(0, 0).wait_send()

    k_home.wait_recv()
    v_home.wait_recv()
    k_home.wait_send()
    v_home.wait_send()
    for step in range(1, n // 2):
        ctx_copy(step, core).wait_recv()

    @pl.when(jnp.logical_not(gathers))
    def _():
        ctx_copy(0, 0).wait_recv()

    totals = jnp.sum(term_ctx[:, 0:2], axis=0)
    token_count = n_dp * n * BLOCK
    qgain_ref[...] = totals[0:1] * (1.0 / math.sqrt(token_count * groups * per_group))
    kgain_ref[...] = totals[1:2] * (1.0 / math.sqrt(token_count * groups))

    @pl.when(gathers)
    def _():
        for step in range(1, n // 2):
            ctx_copy(step, 0).wait_send()
            ctx_copy(step, 1).wait_send()
        ctx_copy(0, 0).wait_send()


def hand_over(*refs):
    sources, targets, sems = refs[:5], refs[5:10], refs[10]
    copies = []
    for source, target in zip(sources, targets):
        if len(source.shape) == 2:
            copies.append((source, target))
        else:
            width = source.shape[2]
            for half in range(2):
                lanes = slice(half * width, (half + 1) * width)
                copies.append((source.at[half], target.at[0, :, lanes]))
    copies = [
        pltpu.make_async_copy(source, target, sems.at[i])
        for i, (source, target) in enumerate(copies)
    ]
    for copy in copies:
        copy.start()
    for copy in copies:
        copy.wait()


def shards(
    q_proj,
    k_proj,
    v_proj,
    out_grad,
    q_gain,
    k_gain,
    pos_ids,
    stretch_lengths,
    stretch_windows,
    clip_ids,
    dispatch_plan,
):
    n = lax.axis_size("ctx")
    n_dp = lax.axis_size("dp")
    groups = k_proj.shape[2] // BLOCK
    heads = q_proj.shape[2] // BLOCK
    per_group = heads // groups
    share = groups // 2
    wide = per_group * BLOCK
    hbm = pl.BlockSpec(memory_space=pl.ANY)
    vmem = pl.BlockSpec(memory_space=pltpu.VMEM)
    dma = pltpu.SemaphoreType.DMA
    count = stretch_lengths.shape[1]
    nat = 3 * BLOCK + HALF
    central = (SPAN - BLOCK, 2 * BLOCK)
    out = pl.pallas_call(
        functools.partial(kernel, n, n_dp, groups, per_group),
        out_shape=(
            pltpu.VMEM((2, BLOCK, share * wide), BF16),
            pltpu.VMEM((2, BLOCK, share * BLOCK), BF16),
            pltpu.VMEM((2, BLOCK, share * BLOCK), BF16),
            pltpu.VMEM((1, BLOCK), F32),
            pltpu.VMEM((1, BLOCK), F32),
        ),
        in_specs=[hbm] * 11,
        out_specs=(vmem,) * 5,
        scratch_shapes=[
            pltpu.SMEM(dispatch_plan.shape, jnp.int32),
            pltpu.VMEM((1, BLOCK), F32),
            pltpu.VMEM((1, BLOCK), F32),
            pltpu.VMEM((2, 3, 1, BLOCK), jnp.int32),
            pltpu.VMEM((2, 2, 3, 1, BLOCK), jnp.int32),
            pltpu.VMEM((1, count), jnp.int32),
            pltpu.VMEM((1, count), jnp.int32),
            pltpu.VMEM((1, count), jnp.int32),
            pltpu.VMEM((2, BLOCK, share * BLOCK), BF16),
            pltpu.VMEM((2, BLOCK, share * BLOCK), BF16),
            pltpu.VMEM((2, BLOCK, BLOCK), F32),
            pltpu.VMEM((2, BLOCK, BLOCK), F32),
            pltpu.VMEM((BLOCK + HALF, BLOCK), F32),
            pltpu.VMEM((BLOCK + HALF, BLOCK), F32),
            pltpu.VMEM((2, SPAN, BLOCK), F32),
            pltpu.VMEM((share, nat, BLOCK), F32),
            pltpu.VMEM((BLOCK, share * BLOCK), BF16),
            pltpu.VMEM((BLOCK, share * BLOCK), BF16),
            pltpu.VMEM((n // 2, 8, BLOCK), F32),
            pltpu.VMEM((2, n_dp, 8, BLOCK), F32),
        ]
        + [pltpu.VMEM((2, BLOCK, wide), BF16)] * (2 * share)
        + [pltpu.VMEM((nat, 2 * BLOCK), BF16)] * share
        + [pltpu.VMEM((nat, BLOCK), BF16)] * share
        + [pltpu.VMEM((2, wide, BLOCK), BF16)] * share
        + [pltpu.VMEM((2, BLOCK, wide), F32)] * share
        + [pltpu.VMEM((rows, wide), F32) for rows in central] * (2 * share)
        + [pltpu.VMEM((SPAN, wide), BF16)] * (4 * share)
        + [pltpu.VMEM((2, BLOCK, 2 * BLOCK), F32)] * share
        + [pltpu.VMEM((2, wide, 2 * BLOCK), F32)] * share
        + [pltpu.VMEM((BLOCK, 2 * BLOCK), BF16)] * share
        + [pltpu.VMEM((HALF, 2 * BLOCK), BF16)] * share
        + [pltpu.VMEM((2, BLOCK, 2 * BLOCK), BF16)] * share
        + [pltpu.VMEM((BLOCK, wide), BF16)] * share
        + [pltpu.VMEM((2, BLOCK, wide), F32)] * (2 * share)
        + [
            dma((9 + 2 * share,)),
            dma((7 + 7 * share,)),
            dma((7 + 7 * share,)),
            dma((2, 2)),
            dma((2, 2)),
            dma((n // 2, 2)),
            dma((n // 2,)),
            dma((n_dp,)),
            dma((2, n_dp)),
        ],
        compiler_params=pltpu.CompilerParams(
            collective_id=0, has_side_effects=True, vmem_limit_bytes=VMEM_LIMIT
        ),
        cost_estimate=pl.CostEstimate(
            flops=10 * heads * BLOCK * SPAN * BLOCK,
            bytes_accessed=6 * BLOCK * heads * BLOCK,
            transcendentals=heads * BLOCK * SPAN,
        ),
    )(
        *[
            pltpu.with_memory_space_constraint(array, pltpu.HBM)
            for array in (
                dispatch_plan,
                k_proj,
                v_proj,
                q_gain.reshape(1, BLOCK),
                k_gain.reshape(1, BLOCK),
                pos_ids.transpose(1, 0, 2),
                stretch_lengths,
                stretch_windows,
                clip_ids,
                q_proj,
                out_grad,
            )
        ]
    )
    out = pl.pallas_call(
        hand_over,
        out_shape=(
            pltpu.HBM(q_proj.shape, BF16),
            pltpu.HBM(k_proj.shape, BF16),
            pltpu.HBM(v_proj.shape, BF16),
            pltpu.HBM((1, BLOCK), F32),
            pltpu.HBM((1, BLOCK), F32),
        ),
        in_specs=[hbm] * 5,
        out_specs=(pl.BlockSpec(memory_space=pltpu.HBM),) * 5,
        scratch_shapes=[dma((8,))],
    )(*[pltpu.with_memory_space_constraint(array, pltpu.VMEM) for array in out])
    return (out[0], out[1], out[2], out[3].reshape(BLOCK), out[4].reshape(BLOCK))


def solution(mesh):
    row = P("dp", "ctx", None)
    table = P("dp", None)
    return jax.shard_map(
        shards,
        mesh=mesh,
        in_specs=(row, row, row, row, P(), P(), P("dp", None, "ctx"), table, table, table, table),
        out_specs=(row, row, row, P(), P()),
        check_vma=False,
    )
```

```python
import functools
import math

import jax
import jax.numpy as jnp
from jax import lax
from jax.experimental import pallas as pl
from jax.experimental.pallas import tpu as pltpu
from jax.sharding import PartitionSpec as P

MESH = pl.DeviceIdType.MESH
F32 = jnp.float32
BF16 = jnp.bfloat16
BLOCK = 128
HALF = BLOCK // 2
SPAN = 2 * BLOCK + HALF
norm_eps = 1e-06
VMEM_LIMIT = 40 * 1024 * 1024
rope_base = 10000.0

NT = (((1,), (1,)), ((), ()))
TN = (((0,), (0,)), ((), ()))


def sin_cos(angle):
    turns = jnp.floor(angle * (2.0 / math.pi) + 0.5)
    rest = angle - turns * 1.5703125
    rest = rest - turns * 4.837512969970703125e-4
    rest = rest - turns * 7.549789948768648e-8
    square = rest * rest
    sine = rest + rest * square * (
        -1.6666654611e-1 + square * (8.3321608736e-3 + square * -1.9515295891e-4)
    )
    cosine = (
        1.0
        - 0.5 * square
        + square
        * square
        * (4.166664568298827e-2 + square * (-1.388731625493765e-3 + square * 2.443315711809948e-5))
    )
    quarter = turns.astype(jnp.int32)
    odd = (quarter & 1) == 1
    sine_out = jnp.where(odd, cosine, sine)
    cosine_out = jnp.where(odd, sine, cosine)
    sine_out = jnp.where((quarter & 2) == 2, -sine_out, sine_out)
    cosine_out = jnp.where(((quarter + 1) & 2) == 2, -cosine_out, cosine_out)
    return sine_out, cosine_out


def roll_half(x):
    return pltpu.roll(x, HALF, 1)


def rope_tables(ids):
    rows = lax.broadcasted_iota(jnp.int32, (BLOCK, BLOCK), 0)
    lanes = lax.broadcasted_iota(jnp.int32, (BLOCK, BLOCK), 1)
    columns = [
        jnp.sum(jnp.where(rows == lanes, ids[t].astype(F32), 0.0), axis=1, keepdims=True)
        for t in range(3)
    ]
    pair = lanes % HALF
    chosen = jnp.where(pair < 16, columns[0], jnp.where(pair < 40, columns[1], columns[2]))
    pair_row = lax.broadcasted_iota(jnp.int32, (1, BLOCK), 1) % HALF
    frequency = jnp.exp(pair_row.astype(F32) * (-math.log(rope_base) / HALF))
    sine, cosine = sin_cos(chosen * frequency)
    return cosine, jnp.where(lanes < HALF, -sine, sine)


def key_ranges(lengths, windows, clips, start):
    count = lengths.shape[1]
    rows = lax.broadcasted_iota(jnp.int32, (count, count), 0)
    lanes = lax.broadcasted_iota(jnp.int32, (count, count), 1)

    def column(where_, values):
        return jnp.sum(jnp.where(where_, values.astype(F32), 0.0), axis=1, keepdims=True)

    ends = column(lanes <= rows, lengths)
    starts = column(lanes < rows, lengths)
    before = column(lanes == rows - 1, lengths)
    window = column(lanes == rows, windows)
    clip = column(lanes == rows, clips + 1)
    clip_before = column(lanes == rows - 1, clips + 1)
    low = starts - jnp.where(clip == clip_before, window * before, 0.0)
    spots = (start + lax.broadcasted_iota(jnp.int32, (count, BLOCK), 1)).astype(F32)
    inside = (starts <= spots) & (spots < ends)
    low_row = jnp.sum(jnp.where(inside, low, 0.0), axis=0, keepdims=True)
    high_row = jnp.sum(jnp.where(inside, ends, 0.0), axis=0, keepdims=True)
    return low_row, high_row


def lane_sums(x, ones):
    high = x.astype(BF16)
    low = (x - high.astype(F32)).astype(BF16)
    return jnp.dot(jnp.concatenate([high, low], axis=1), ones, preferred_element_type=F32)


def fold_rows(x):
    return jnp.sum(x.reshape(x.shape[0] // 8, 8, x.shape[1]), axis=0)


def kernel(n, n_dp, groups, per_group, *refs):
    share = groups // 2
    wide = per_group * BLOCK
    refs = iter(refs)

    def take(count):
        return [next(refs) for _ in range(count)]

    (
        plan_hbm,
        k_hbm,
        v_hbm,
        qg_hbm,
        kg_hbm,
        ids_hbm,
        len_hbm,
        win_hbm,
        clip_hbm,
        q_hbm,
        do_hbm,
    ) = take(11)
    qgrad_ref, kgrad_ref, vgrad_ref, qgain_ref, kgain_ref = take(5)
    plan_ref, qg_ref, kg_ref, ids, near_ids, len_ref, win_ref, clip_ref = take(8)
    k_raw, v_raw, cosn, sinn, near_cos, near_sin, bias_ref, dk_all = take(8)
    k_out, v_out, term_ctx, term_dp = take(4)
    q_in = take(share)
    do_in = take(share)
    kv = take(share)
    rolled = take(share)
    qrot = take(share)
    qinv = take(share)
    central = [take(2) for _ in range(share)]
    central_grad = [take(2) for _ in range(share)]
    probs_low = [take(2) for _ in range(share)]
    score_grad = [take(2) for _ in range(share)]
    dkv = take(share)
    dq = take(share)
    back_prev = take(share)
    back_next = take(share)
    arrived = take(share)
    q_out = take(share)
    q_turned = take(share)
    q_unit = take(share)
    load_sem, sent, got, near_s, near_r, tc_s, tc_r, td_s, td_r = take(9)

    me = lax.axis_index("ctx")
    dp = lax.axis_index("dp")
    core = lax.rem(me, 2)
    pair = me // 2
    partner = me + 1 - 2 * core
    has_prev = me >= 2
    has_next = me < n - 2
    inv_sqrt = BLOCK ** (-0.5)

    def columns(which, width, j=0):
        return pl.ds(pl.multiple_of(which * (share * width) + j * width, BLOCK), width)

    mine, theirs = core, 1 - core
    both_k = pl.ds(pl.multiple_of(mine * (share * BLOCK), BLOCK), share * BLOCK)
    their_k = pl.ds(pl.multiple_of(theirs * (share * BLOCK), BLOCK), share * BLOCK)
    moves = [
        (plan_hbm, plan_ref),
        (ids_hbm, ids.at[0]),
        (qg_hbm, qg_ref),
        (kg_hbm, kg_ref),
        (k_hbm.at[0, :, both_k], k_raw.at[0]),
        (v_hbm.at[0, :, both_k], v_raw.at[0]),
        (len_hbm, len_ref),
        (win_hbm, win_ref),
        (clip_hbm, clip_ref),
    ]
    for j in range(share):
        moves.append((q_hbm.at[0, :, columns(mine, wide, j)], q_in[j].at[0]))
        moves.append((do_hbm.at[0, :, columns(mine, wide, j)], do_in[j].at[0]))
    loads = [
        pltpu.make_async_copy(source, target, load_sem.at[i])
        for i, (source, target) in enumerate(moves)
    ]

    barrier = pltpu.get_barrier_semaphore()
    pl.semaphore_signal(barrier, inc=1, device_id=(dp, partner), device_id_type=MESH)

    for step in range(1, n // 2):
        for side in range(2):
            peer = (dp, 2 * lax.rem(pair + step, n // 2) + side)
            pl.semaphore_signal(barrier, inc=1, device_id=peer, device_id_type=MESH)
    for step in range(1, n_dp):
        for side in range(2):
            peer = (lax.rem(dp + step, n_dp), 2 * pair + side)
            pl.semaphore_signal(barrier, inc=1, device_id=peer, device_id_type=MESH)

    @pl.when(jnp.logical_not(has_prev))
    def _():
        near_ids[0] = jnp.zeros_like(near_ids[0])
        for j in range(share):
            kv[j][:BLOCK] = jnp.zeros((BLOCK, 2 * BLOCK), BF16)
            arrived[j][0, :HALF] = jnp.zeros((HALF, 2 * BLOCK), BF16)

    @pl.when(jnp.logical_not(has_next))
    def _():
        near_ids[1] = jnp.zeros_like(near_ids[1])
        for j in range(share):
            kv[j][3 * BLOCK :] = jnp.zeros((HALF, 2 * BLOCK), BF16)
            arrived[j][1] = jnp.zeros((BLOCK, 2 * BLOCK), BF16)

    for j in range(share):
        arrived[j][0, HALF:] = jnp.zeros((HALF, 2 * BLOCK), BF16)

    def remote(source, target, send, receive, peer):
        return pltpu.make_async_remote_copy(
            src_ref=source,
            dst_ref=target,
            send_sem=send,
            recv_sem=receive,
            device_id=peer,
            device_id_type=MESH,
        )

    count = [0]

    def numbered(source, target, peer):
        i = count[0]
        count[0] += 1
        return remote(source, target, sent.at[i], got.at[i], (dp, peer))

    k_swap = numbered(k_hbm.at[0, :, their_k], k_raw.at[1], partner)
    v_swap = numbered(v_hbm.at[0, :, their_k], v_raw.at[1], partner)
    ids_swap = numbered(ids_hbm, ids.at[1], partner)
    q_swap = [
        numbered(q_hbm.at[0, :, columns(theirs, wide, j)], q_in[j].at[1], partner)
        for j in range(share)
    ]
    do_swap = [
        numbered(do_hbm.at[0, :, columns(theirs, wide, j)], do_in[j].at[1], partner)
        for j in range(share)
    ]
    last_block, last_half = slice(2 * BLOCK, 3 * BLOCK), slice(3 * BLOCK, SPAN + BLOCK)
    first_block, first_half = slice(0, BLOCK), slice(BLOCK, BLOCK + HALF)
    pieces = [slice(0, BLOCK) if j == 0 else slice(0, 2 * BLOCK) for j in range(share)]
    values = slice(BLOCK, 2 * BLOCK)
    to_next = [
        numbered(kv[j].at[last_block, pieces[j]], kv[j].at[first_block, pieces[j]], me + 2)
        for j in range(share)
    ]
    to_prev = [
        numbered(kv[j].at[first_half, pieces[j]], kv[j].at[last_half, pieces[j]], me - 2)
        for j in range(share)
    ]
    ahead_next = numbered(kv[0].at[last_block, values], kv[0].at[first_block, values], me + 2)
    ahead_prev = numbered(kv[0].at[first_half, values], kv[0].at[last_half, values], me - 2)
    home_prev = [numbered(back_prev[j], arrived[j].at[1], me - 2) for j in range(share)]
    home_next = [numbered(back_next[j], arrived[j].at[0, :HALF], me + 2) for j in range(share)]
    q_home = [
        numbered(q_out[j], qgrad_ref.at[mine, :, j * wide : (j + 1) * wide], partner)
        for j in range(share)
    ]
    k_home = numbered(k_out, kgrad_ref.at[mine], partner)
    v_home = numbered(v_out, vgrad_ref.at[mine], partner)

    def near_copy(side, other, sender):
        peer = 2 * pair + other + (2 if side == 0 else -2)
        return remote(
            ids_hbm,
            near_ids.at[side, sender],
            near_s.at[side, other],
            near_r.at[side, sender],
            (dp, peer),
        )

    pl.semaphore_wait(barrier, n - 1 + 2 * (n_dp - 1))
    v_swap.start()
    ids_swap.start()
    k_swap.start()
    for load in loads:
        load.start()
    for j in range(share):
        q_swap[j].start()
        do_swap[j].start()

    @pl.when(has_next)
    def _():
        for other in range(2):
            near_copy(0, other, core).start()

    @pl.when(has_prev)
    def _():
        for other in range(2):
            near_copy(1, other, core).start()

    for load in loads[:9]:
        load.wait()
    odd = lax.rem(plan_ref[0, me], 2)
    slot_of = (odd, 1 - odd)
    q_gain, k_gain = qg_ref[...], kg_ref[...]
    ones = jnp.ones((2 * BLOCK, BLOCK), BF16)

    for s in range(2):
        if s == 1:
            v_swap.wait_recv()
            for j in range(share):
                for t in range(2):
                    spot = slice((1 + t) * BLOCK, (2 + t) * BLOCK)
                    kv[j][spot, BLOCK:] = v_raw[slot_of[t], :, j * BLOCK : (j + 1) * BLOCK]
                if j == 0:

                    @pl.when(has_prev)
                    def _():
                        ahead_prev.start()

                    @pl.when(has_next)
                    def _():
                        ahead_next.start()

            ids_swap.wait_recv()
        cosine, sine = rope_tables([ids[s, i] for i in range(3)])
        cosn[s] = cosine
        sinn[s] = sine

    def table(t):
        return cosn[slot_of[t]], sinn[slot_of[t]]

    rolled_k_gain, rolled_q_gain = roll_half(k_gain), roll_half(q_gain)
    k_swap.wait_recv()
    for j in range(share):
        lanes = slice(j * BLOCK, (j + 1) * BLOCK)
        for t in range(2):
            cosine, sine = table(t)
            x = k_raw[slot_of[t], :, lanes].astype(F32)
            inv = lax.rsqrt(lane_sums(x * x, ones) * (1.0 / BLOCK) + norm_eps)
            turned = inv * (x * (cosine * k_gain) + roll_half(x) * (sine * rolled_k_gain))
            spot = slice((1 + t) * BLOCK, (2 + t) * BLOCK)
            kv[j][spot, :BLOCK] = turned.astype(BF16)
            rolled[j][spot] = roll_half(turned).astype(BF16)

        @pl.when(has_prev)
        def _():
            to_prev[j].start()

        @pl.when(has_next)
        def _():
            to_next[j].start()

    for t in range(2):
        start = (2 * pair + t) * BLOCK
        low_row, high_row = key_ranges(len_ref[...], win_ref[...], clip_ref[...], start)
        spots = (start - BLOCK + lax.broadcasted_iota(jnp.int32, (SPAN, BLOCK), 0)).astype(F32)
        bias_ref[t] = jnp.where((spots >= low_row) & (spots < high_row), 0.0, -1e30)

    def heads(value, m):
        return jnp.concatenate(
            [
                value[:, 2 * m * BLOCK : (2 * m + 1) * BLOCK],
                value[:, (2 * m + 1) * BLOCK : (2 * m + 2) * BLOCK],
            ],
            axis=0,
        )

    def stacked(value):
        return jnp.concatenate(
            [value[:, h * BLOCK : (h + 1) * BLOCK] for h in range(per_group)], axis=0
        )

    scale = inv_sqrt * math.log2(math.e)
    middle = (slice(BLOCK, SPAN), slice(0, 2 * BLOCK))
    edge = (slice(0, BLOCK), slice(2 * BLOCK, SPAN))
    offset = (0, BLOCK)

    def shifted(spot, t):
        return slice(spot.start + offset[t], spot.stop + offset[t])

    def scored(j, t, spot, m, cot):
        key = kv[j][shifted(spot, t), :BLOCK]
        value = kv[j][shifted(spot, t), BLOCK:]
        query = qrot[j][t, 2 * m * BLOCK : (2 * m + 2) * BLOCK, :]
        scores = lax.dot_general(key, query, NT, preferred_element_type=F32)
        grad = lax.dot_general(value, cot, NT, preferred_element_type=F32)
        bias = bias_ref[t, spot]
        weights = jnp.exp2(scores * scale + jnp.concatenate([bias, bias], axis=1))
        return weights, grad

    sums = {}
    for j in range(share):
        loads[9 + 2 * j].wait()
        loads[10 + 2 * j].wait()
        q_swap[j].wait_recv()
        do_swap[j].wait_recv()
        for t in range(2):
            cosine, sine = table(t)
            qc, qs = cosine * q_gain, sine * rolled_q_gain
            for h in range(per_group):
                lanes = slice(h * BLOCK, (h + 1) * BLOCK)
                x = q_in[j][slot_of[t], :, lanes].astype(F32)
                inv = lax.rsqrt(lane_sums(x * x, ones) * (1.0 / BLOCK) + norm_eps)
                qinv[j][t, :, lanes] = inv
                qrot[j][t, lanes, :] = (inv * (x * qc + roll_half(x) * qs)).astype(BF16)
            for m in range(per_group // 2):
                lanes = slice(2 * m * BLOCK, (2 * m + 2) * BLOCK)
                cot = heads(do_in[j][slot_of[t]], m)
                weights, grad = scored(j, t, middle[t], m, cot)
                central[j][t][:, lanes] = weights
                central_grad[j][t][:, lanes] = grad
                sums[j, t, m] = (
                    jnp.sum(weights, axis=0, keepdims=True),
                    jnp.sum(weights * grad, axis=0, keepdims=True),
                )

    def join(j, i, parts):
        even, late = parts
        lanes = slice(i * BLOCK, (i + 1) * BLOCK)
        dkv[j][0, :, lanes] = even[:BLOCK] + late[:BLOCK]
        dkv[j][1, :HALF, lanes] = even[BLOCK:] + late[BLOCK : BLOCK + HALF]
        dkv[j][1, HALF:, lanes] = late[BLOCK + HALF :]

    def edge_values(j, t):
        grad = jnp.dot(
            probs_low[j][t][edge[t]], stacked(do_in[j][slot_of[t]]), preferred_element_type=F32
        )
        (back_prev, back_next)[t][j][:, BLOCK:] = grad.astype(BF16)

    q_term = jnp.zeros((8, BLOCK), F32)
    k_term = jnp.zeros((8, BLOCK), F32)
    @pl.when(has_prev)
    def _():
        ahead_next.wait_recv()

    @pl.when(has_next)
    def _():
        ahead_prev.wait_recv()

    for j in range(share):

        @pl.when(has_prev)
        def _():
            to_next[j].wait_recv()

        @pl.when(has_next)
        def _():
            to_prev[j].wait_recv()

        if j > 0:

            @pl.when(has_prev)
            def _():
                home_prev[j - 1].start()

            @pl.when(has_next)
            def _():
                home_next[j - 1].start()

        for t in range(2):
            spot = edge[t]
            for m in range(per_group // 2):
                lanes = slice(2 * m * BLOCK, (2 * m + 2) * BLOCK)
                cot = heads(do_in[j][slot_of[t]], m)
                weights, grad = scored(j, t, spot, m, cot)
                total, delta = sums[j, t, m]
                inverse = 1.0 / (total + jnp.sum(weights, axis=0, keepdims=True))
                delta = (delta + jnp.sum(weights * grad, axis=0, keepdims=True)) * inverse
                sums[j, t, m] = (inverse, delta)
                probs = weights * inverse
                probs_low[j][t][spot, lanes] = probs.astype(BF16)
                score_grad[j][t][spot, lanes] = (probs * (grad - delta)).astype(BF16)
            key_grad = (
                jnp.dot(score_grad[j][t][spot], qrot[j][t], preferred_element_type=F32) * inv_sqrt
            )
            dk_all[j, shifted(spot, t)] = key_grad
            (back_prev, back_next)[t][j][:, :BLOCK] = key_grad.astype(BF16)
            if j < share - 1:
                edge_values(j, t)

        if j == 0:
            @pl.when(has_prev)
            def _():
                for sender in range(2):
                    near_copy(0, sender, sender).wait_recv()

            @pl.when(has_next)
            def _():
                for sender in range(2):
                    near_copy(1, sender, sender).wait_recv()

            before = 1 - lax.rem(plan_ref[0, lax.max(2 * pair - 2, 0)], 2)
            after = lax.rem(plan_ref[0, lax.min(2 * pair + 2, n - 2)], 2)
            cosine, sine = rope_tables([near_ids[0, before, i] for i in range(3)])
            near_cos[:BLOCK] = cosine
            near_sin[:BLOCK] = sine
            cosine, sine = rope_tables([near_ids[1, after, i] for i in range(3)])
            near_cos[BLOCK:] = cosine[:HALF]
            near_sin[BLOCK:] = sine[:HALF]

        own_key = kv[j][:, :BLOCK].astype(F32)
        rolled[j][:BLOCK] = roll_half(own_key[:BLOCK]).astype(BF16)
        rolled[j][3 * BLOCK :] = roll_half(own_key[3 * BLOCK :]).astype(BF16)
        parts = []
        for t in range(2):
            spot = middle[t]
            for m in range(per_group // 2):
                lanes = slice(2 * m * BLOCK, (2 * m + 2) * BLOCK)
                inverse, delta = sums[j, t, m]
                probs = central[j][t][:, lanes] * inverse
                probs_low[j][t][spot, lanes] = probs.astype(BF16)
                score_grad[j][t][spot, lanes] = (
                    probs * (central_grad[j][t][:, lanes] - delta)
                ).astype(BF16)
            parts.append(
                jnp.dot(score_grad[j][t][spot], qrot[j][t], preferred_element_type=F32) * inv_sqrt
            )
            window = slice(offset[t], offset[t] + SPAN)
            keys = jnp.concatenate([kv[j][window, :BLOCK], rolled[j][window]], axis=1)
            dq[j][t] = lax.dot_general(score_grad[j][t][...], keys, TN, preferred_element_type=F32)
        join(j, 0, parts)
        for t in range(2):
            dk_all[j, (1 + t) * BLOCK : (2 + t) * BLOCK] = dkv[j][t, :, :BLOCK]
        key, grad = own_key, dk_all[j]
        cosine, sine = (
            jnp.concatenate([near[:BLOCK], own[odd], own[1 - odd], near[BLOCK:]], axis=0)
            for near, own in ((near_cos, cosn), (near_sin, sinn))
        )
        product = (grad * cosine - roll_half(grad) * sine) * (
            key * cosine - rolled[j][...].astype(F32) * sine
        )
        k_term = k_term + fold_rows(product)

    for j in range(share):
        for s in range(2):
            t = slot_of[s]
            cos_back, sin_back = cosn[s] * inv_sqrt, sinn[s] * inv_sqrt
            for h in range(per_group):
                lanes = slice(h * BLOCK, (h + 1) * BLOCK)
                grad = dq[j][t, lanes, :BLOCK]
                turned = grad * cos_back - dq[j][t, lanes, BLOCK:] * sin_back
                unit = q_in[j][s, :, lanes].astype(F32) * qinv[j][t, :, lanes]
                product = turned * unit
                q_term = q_term + fold_rows(product)
                q_turned[j][s, :, lanes] = turned
                q_unit[j][s, :, lanes] = unit

    term_dp[core, dp, 0:1] = jnp.sum(q_term, axis=0, keepdims=True)
    term_dp[core, dp, 1:2] = jnp.sum(k_term, axis=0, keepdims=True) / k_gain

    gathers = core == 1
    outer = 2 * pair + 1

    def dp_copy(step, sender):
        peer = lax.rem(dp + step, n_dp)
        mine_spot = (core, dp)
        return remote(
            term_dp.at[mine_spot],
            term_dp.at[mine_spot],
            td_s.at[step],
            td_r.at[sender, step],
            (peer, outer),
        )

    def ctx_copy(step, side):
        peer = 2 * lax.rem(pair + step, n // 2) + side
        return remote(
            term_ctx.at[pair], term_ctx.at[pair], tc_s.at[step, side], tc_r.at[step], (dp, peer)
        )

    for step in range(1, n_dp):
        dp_copy(step, core).start()

    @pl.when(jnp.logical_not(gathers))
    def _():
        dp_copy(0, 0).start()

    for t in range(2):
        edge_values(share - 1, t)

    @pl.when(has_prev)
    def _():
        home_prev[share - 1].start()

    @pl.when(has_next)
    def _():
        home_next[share - 1].start()

    for j in range(share):
        for s in (1, 0):
            for h in range(per_group):
                lanes = slice(h * BLOCK, (h + 1) * BLOCK)
                turned, unit = q_turned[j][s, :, lanes], q_unit[j][s, :, lanes]
                weighted = turned * q_gain
                mean = lane_sums(weighted * unit, ones) * (1.0 / BLOCK)
                result = (qinv[j][slot_of[s], :, lanes] * (weighted - unit * mean)).astype(BF16)
                if s == 0:
                    qgrad_ref[mine, :, j * wide + h * BLOCK : j * wide + (h + 1) * BLOCK] = result
                else:
                    q_out[j][:, lanes] = result
            if s == 1:
                q_home[j].start()
    for j in range(share):
        parts = [
            jnp.dot(
                probs_low[j][t][middle[t]],
                stacked(do_in[j][slot_of[t]]),
                preferred_element_type=F32,
            )
            for t in range(2)
        ]
        join(j, 1, parts)

    k_norm = {}
    for j in range(share):
        for s in range(2):
            x = k_raw[s, :, j * BLOCK : (j + 1) * BLOCK].astype(F32)
            inv = lax.rsqrt(lane_sums(x * x, ones) * (1.0 / BLOCK) + norm_eps)
            k_norm[j, s] = (inv, x * inv)

    @pl.when(gathers)
    def _():
        for step in range(n_dp):
            dp_copy(step, 0).wait_recv()
        for step in range(1, n_dp):
            dp_copy(step, 1).wait_recv()
        term_ctx[pair, 0:2] = jnp.sum(jnp.sum(term_dp[:, :, 0:2], axis=0), axis=0)
        for side in range(2):
            for step in range(1, n // 2):
                ctx_copy(step, side).start()
        ctx_copy(0, 0).start()

    for j in range(share):

        @pl.when(has_next)
        def _():
            home_prev[j].wait_recv()

        @pl.when(has_prev)
        def _():
            home_next[j].wait_recv()

        lanes = slice(j * BLOCK, (j + 1) * BLOCK)
        for s in (1, 0):
            t = slot_of[s]
            cosine, sine = cosn[s], sinn[s]
            total = dkv[j][t] + arrived[j][t].astype(F32)
            grad = total[:, :BLOCK]
            inv, unit = k_norm[j, s]
            turned = grad * cosine - roll_half(grad) * sine
            mean = lane_sums(turned * unit * k_gain, ones) * (1.0 / BLOCK)
            result = (inv * (turned * k_gain - unit * mean)).astype(BF16)
            if s == 0:
                kgrad_ref[mine, :, lanes] = result
                vgrad_ref[mine, :, lanes] = total[:, BLOCK:].astype(BF16)
            else:
                k_out[:, lanes] = result
                v_out[:, lanes] = total[:, BLOCK:].astype(BF16)
    k_home.start()
    v_home.start()

    ids_swap.wait_send()
    k_swap.wait_send()
    v_swap.wait_send()
    for j in range(share):
        q_swap[j].wait_send()
        do_swap[j].wait_send()
        q_home[j].wait_recv()
        q_home[j].wait_send()

        @pl.when(has_next)
        def _():
            to_next[j].wait_send()
            home_next[j].wait_send()

        @pl.when(has_prev)
        def _():
            to_prev[j].wait_send()
            home_prev[j].wait_send()

    @pl.when(has_next)
    def _():
        ahead_next.wait_send()
        for other in range(2):
            near_copy(0, other, core).wait_send()

    @pl.when(has_prev)
    def _():
        ahead_prev.wait_send()
        for other in range(2):
            near_copy(1, other, core).wait_send()

    for step in range(1, n_dp):
        dp_copy(step, core).wait_send()

    @pl.when(jnp.logical_not(gathers))
    def _():
        dp_copy(0, 0).wait_send()

    k_home.wait_recv()
    v_home.wait_recv()
    k_home.wait_send()
    v_home.wait_send()
    for step in range(1, n // 2):
        ctx_copy(step, core).wait_recv()

    @pl.when(jnp.logical_not(gathers))
    def _():
        ctx_copy(0, 0).wait_recv()

    totals = jnp.sum(term_ctx[:, 0:2], axis=0)
    token_count = n_dp * n * BLOCK
    qgain_ref[...] = totals[0:1] * (1.0 / math.sqrt(token_count * groups * per_group))
    kgain_ref[...] = totals[1:2] * (1.0 / math.sqrt(token_count * groups))

    @pl.when(gathers)
    def _():
        for step in range(1, n // 2):
            ctx_copy(step, 0).wait_send()
            ctx_copy(step, 1).wait_send()
        ctx_copy(0, 0).wait_send()


def hand_over(*refs):
    sources, targets, sems = refs[:5], refs[5:10], refs[10]
    copies = []
    for source, target in zip(sources, targets):
        if len(source.shape) == 2:
            copies.append((source, target))
        else:
            width = source.shape[2]
            for half in range(2):
                lanes = slice(half * width, (half + 1) * width)
                copies.append((source.at[half], target.at[0, :, lanes]))
    copies = [
        pltpu.make_async_copy(source, target, sems.at[i])
        for i, (source, target) in enumerate(copies)
    ]
    for copy in copies:
        copy.start()
    for copy in copies:
        copy.wait()


def shards(
    q_proj,
    k_proj,
    v_proj,
    out_grad,
    q_gain,
    k_gain,
    pos_ids,
    stretch_lengths,
    stretch_windows,
    clip_ids,
    dispatch_plan,
):
    n = lax.axis_size("ctx")
    n_dp = lax.axis_size("dp")
    groups = k_proj.shape[2] // BLOCK
    heads = q_proj.shape[2] // BLOCK
    per_group = heads // groups
    share = groups // 2
    wide = per_group * BLOCK
    hbm = pl.BlockSpec(memory_space=pl.ANY)
    vmem = pl.BlockSpec(memory_space=pltpu.VMEM)
    dma = pltpu.SemaphoreType.DMA
    count = stretch_lengths.shape[1]
    nat = 3 * BLOCK + HALF
    central = (SPAN - BLOCK, 2 * BLOCK)
    out = pl.pallas_call(
        functools.partial(kernel, n, n_dp, groups, per_group),
        out_shape=(
            pltpu.VMEM((2, BLOCK, share * wide), BF16),
            pltpu.VMEM((2, BLOCK, share * BLOCK), BF16),
            pltpu.VMEM((2, BLOCK, share * BLOCK), BF16),
            pltpu.VMEM((1, BLOCK), F32),
            pltpu.VMEM((1, BLOCK), F32),
        ),
        in_specs=[hbm] * 11,
        out_specs=(vmem,) * 5,
        scratch_shapes=[
            pltpu.SMEM(dispatch_plan.shape, jnp.int32),
            pltpu.VMEM((1, BLOCK), F32),
            pltpu.VMEM((1, BLOCK), F32),
            pltpu.VMEM((2, 3, 1, BLOCK), jnp.int32),
            pltpu.VMEM((2, 2, 3, 1, BLOCK), jnp.int32),
            pltpu.VMEM((1, count), jnp.int32),
            pltpu.VMEM((1, count), jnp.int32),
            pltpu.VMEM((1, count), jnp.int32),
            pltpu.VMEM((2, BLOCK, share * BLOCK), BF16),
            pltpu.VMEM((2, BLOCK, share * BLOCK), BF16),
            pltpu.VMEM((2, BLOCK, BLOCK), F32),
            pltpu.VMEM((2, BLOCK, BLOCK), F32),
            pltpu.VMEM((BLOCK + HALF, BLOCK), F32),
            pltpu.VMEM((BLOCK + HALF, BLOCK), F32),
            pltpu.VMEM((2, SPAN, BLOCK), F32),
            pltpu.VMEM((share, nat, BLOCK), F32),
            pltpu.VMEM((BLOCK, share * BLOCK), BF16),
            pltpu.VMEM((BLOCK, share * BLOCK), BF16),
            pltpu.VMEM((n // 2, 8, BLOCK), F32),
            pltpu.VMEM((2, n_dp, 8, BLOCK), F32),
        ]
        + [pltpu.VMEM((2, BLOCK, wide), BF16)] * (2 * share)
        + [pltpu.VMEM((nat, 2 * BLOCK), BF16)] * share
        + [pltpu.VMEM((nat, BLOCK), BF16)] * share
        + [pltpu.VMEM((2, wide, BLOCK), BF16)] * share
        + [pltpu.VMEM((2, BLOCK, wide), F32)] * share
        + [pltpu.VMEM((rows, wide), F32) for rows in central] * (2 * share)
        + [pltpu.VMEM((SPAN, wide), BF16)] * (4 * share)
        + [pltpu.VMEM((2, BLOCK, 2 * BLOCK), F32)] * share
        + [pltpu.VMEM((2, wide, 2 * BLOCK), F32)] * share
        + [pltpu.VMEM((BLOCK, 2 * BLOCK), BF16)] * share
        + [pltpu.VMEM((HALF, 2 * BLOCK), BF16)] * share
        + [pltpu.VMEM((2, BLOCK, 2 * BLOCK), BF16)] * share
        + [pltpu.VMEM((BLOCK, wide), BF16)] * share
        + [pltpu.VMEM((2, BLOCK, wide), F32)] * (2 * share)
        + [
            dma((9 + 2 * share,)),
            dma((7 + 7 * share,)),
            dma((7 + 7 * share,)),
            dma((2, 2)),
            dma((2, 2)),
            dma((n // 2, 2)),
            dma((n // 2,)),
            dma((n_dp,)),
            dma((2, n_dp)),
        ],
        compiler_params=pltpu.CompilerParams(
            collective_id=0, has_side_effects=True, vmem_limit_bytes=VMEM_LIMIT
        ),
        cost_estimate=pl.CostEstimate(
            flops=10 * heads * BLOCK * SPAN * BLOCK,
            bytes_accessed=6 * BLOCK * heads * BLOCK,
            transcendentals=heads * BLOCK * SPAN,
        ),
    )(
        *[
            pltpu.with_memory_space_constraint(array, pltpu.HBM)
            for array in (
                dispatch_plan,
                k_proj,
                v_proj,
                q_gain.reshape(1, BLOCK),
                k_gain.reshape(1, BLOCK),
                pos_ids.transpose(1, 0, 2),
                stretch_lengths,
                stretch_windows,
                clip_ids,
                q_proj,
                out_grad,
            )
        ]
    )
    out = pl.pallas_call(
        hand_over,
        out_shape=(
            pltpu.HBM(q_proj.shape, BF16),
            pltpu.HBM(k_proj.shape, BF16),
            pltpu.HBM(v_proj.shape, BF16),
            pltpu.HBM((1, BLOCK), F32),
            pltpu.HBM((1, BLOCK), F32),
        ),
        in_specs=[hbm] * 5,
        out_specs=(pl.BlockSpec(memory_space=pltpu.HBM),) * 5,
        scratch_shapes=[dma((8,))],
    )(*[pltpu.with_memory_space_constraint(array, pltpu.VMEM) for array in out])
    return (out[0], out[1], out[2], out[3].reshape(BLOCK), out[4].reshape(BLOCK))


def solution(mesh):
    row = P("dp", "ctx", None)
    table = P("dp", None)
    return jax.shard_map(
        shards,
        mesh=mesh,
        in_specs=(row, row, row, row, P(), P(), P("dp", None, "ctx"), table, table, table, table),
        out_specs=(row, row, row, P(), P()),
        check_vma=False,
    )
```
